32 devices in a mesh: sim: 8 (over z, x), grp: 4 (over y, core).
Axes of the slice: x: 2, y: 2, z: 4, core: 2. Of those that a mesh axis runs over, the one named last changes fastest.
Arguments:
- velocity: float32 [8, 4, 3, 256, 512], P('sim', 'grp'), may hold values from -6 to 6
- slot_of: int32 [8, 4, 256], P('sim', 'grp'), may hold values from 0 to 255, each once within a row
- w_encode: bfloat16 [1024, 256], replicated, may hold values from -0.1875 to 0.1875
- w_conv: bfloat16 [27, 256, 256], replicated, may hold values from -0.078125 to 0.078125
- w_head: bfloat16 [256, 128], replicated, may hold values from -0.375 to 0.375
Outputs:
- velocity_next: float32 [8, 4, 3, 256, 512], P('sim', 'grp')
- grad_encode: float32 [1024, 256], P(None, 'grp')
- grad_conv: float32 [27, 256, 256], P(None, None, 'grp')
- grad_head: float32 [256, 128], P('grp')
The draws below stay inside these ranges and needn't reach their ends.
Inputs may be any that keep to these rules, and one draw needn't show every extreme that they name: `slot_of`: each block's row of 256 entries names every slot once.
All inputs are finite; a program needn't handle non-finite values.
Results may differ from the reference program's by a relative error of at most 0.0085.
Values may be sent and summed in bfloat16 or wider, within the bound.
No kernel may reach another device: no remote copies, remote signals or barrier semaphores. Data moves between devices by JAX's collectives and lax.ppermute only.
A program may use at most 128 MiB of HBM per device.

```python
import jax
import jax.numpy as jnp
import numpy as np
from jax import lax

NP = 8
PTS = 512
CH = 256
FEAT = 1024
OUT = 128
TAPS = 27
EX = 2
EY = 4
EZ = 32
STEPS = 2
E_DEV = 256
NXE = 16
NYE = 16
CZ = 8
ELEMS = 8192
N_SIM = 8
N_GRP = 4


def shard_levels(rng, dims, pieces, smallest, high):
    def one(position, shards_of):
        heights = jax.random.uniform(jax.random.fold_in(jax.random.fold_in(rng, 6), position), (shards_of,), jnp.float32, smallest / len(pieces), high / len(pieces))
        return jnp.repeat(jnp.exp(heights), dims[position] // shards_of).reshape((-1,) + (1,) * (len(dims) - position - 1))

    factor_of = one(*pieces[0])
    for cut in pieces[1:]:
        factor_of = factor_of * one(*cut)
    return factor_of


def normal_values(key, shape, scale, limit, split=(), kind=jnp.bfloat16):
    array = scale * jax.random.normal(key, shape, jnp.float32)
    if split:
        array = array * shard_levels(key, shape, split, -0.22, 0.18)
    return jnp.clip(array, -limit, limit).astype(kind)


def setup_inputs(seed: int = 0) -> dict:
    seeds = jax.random.split(jax.random.key(seed), 6)
    velocity = normal_values(seeds[0], (N_SIM, N_GRP, 3, E_DEV, PTS), 1.0, 6.0, ((0, 8), (1, 4)), jnp.float32)
    slot_of = jax.vmap(lambda own: jax.random.permutation(own, E_DEV))(jax.random.split(seeds[1], N_SIM * N_GRP)).reshape((N_SIM, N_GRP, E_DEV)).astype(jnp.int32)
    w_encode = normal_values(seeds[2], (FEAT, CH), FEAT ** -0.5, 0.1875)
    w_conv = normal_values(seeds[3], (TAPS, CH, CH), (27 * CH) ** -0.5, 0.078125)
    w_head = normal_values(seeds[4], (CH, OUT), CH ** -0.5, 0.375)
    return {"velocity": velocity, "slot_of": slot_of, "w_encode": w_encode, "w_conv": w_conv, "w_head": w_head}


VISCOSITY = 0.2
TIME_STEP = 0.005
PENALTY = 100.0
LOSS_WEIGHT = 64.0

def derivative_matrix(count):
    places = np.arange(count)
    points = -np.cos(np.pi * places / (count - 1))
    weights = np.where(places % 2 == 0, 1.0, -1.0)
    weights[0] = weights[0] * 0.5
    weights[count - 1] = weights[count - 1] * 0.5
    identity = np.eye(count)
    spread = points[:, None] - points[None, :] + identity
    deriv = weights[None, :] / weights[:, None] / spread
    deriv = deriv * (1.0 - identity)
    return deriv - identity * deriv.sum(axis=1)[:, None]

def element_tables(count):
    deriv = derivative_matrix(count)
    single = np.eye(count)
    square = np.eye(count * count)
    along_x = np.kron(deriv, square)
    along_y = np.kron(single, np.kron(deriv, single))
    along_z = np.kron(square, deriv)
    laplace = along_x @ along_x + along_y @ along_y + along_z @ along_z
    stencil = np.concatenate([along_x.T, along_y.T, along_z.T, laplace.T], axis=1)
    grid = np.arange(count ** 3).reshape(count, count, count)
    final = count - 1
    chosen = np.concatenate([grid[0].ravel(), grid[final].ravel(), grid[:, 0].ravel(), grid[:, final].ravel(), grid[:, :, 0].ravel(), grid[:, :, final].ravel()])
    select = np.zeros((count ** 3, chosen.size))
    select[chosen, np.arange(chosen.size)] = 1.0
    bottom = np.zeros((count ** 3, count * count))
    for first in range(count):
        for middle in range(count):
            for inner in range(count):
                bottom[grid[first, middle, inner], first * count + inner] = VISCOSITY * deriv[0, middle]
    return (jnp.asarray(stencil, jnp.float32), jnp.asarray(select, jnp.float32), jnp.asarray(bottom, jnp.float32))

def silu_grad(value):
    sigma = jax.nn.sigmoid(value)
    return sigma * (1.0 + value * (1.0 - sigma))

def advance(field, faces, beside, stencil, select):
    points = field.shape[-1]
    derived = jnp.einsum('cxyzp,pq->cxyzq', field, stencil, precision=lax.Precision.HIGHEST)
    advect = field[0][None] * derived[..., 0:points]
    advect = advect + field[1][None] * derived[..., points:2 * points]
    advect = advect + field[2][None] * derived[..., 2 * points:3 * points]
    laplace = derived[..., 3 * points:]
    penalty = jnp.einsum('cxyzq,pq->cxyzp', beside - faces, select, precision=lax.Precision.HIGHEST)
    return field + TIME_STEP * (VISCOSITY * (laplace + PENALTY * penalty) - advect)

def face_part(faces, which):
    width = faces.shape[-1] // 6
    return faces[..., which * width:(which + 1) * width]

def reorder(blocks, slots):
    return jax.vmap(jax.vmap(lambda values, order: values[:, order]))(blocks, slots)

def window(padded, shift_x, shift_y, shift_z, sizes):
    part = padded[:, 1 + shift_x:1 + shift_x + sizes[0], 1 + shift_y:1 + shift_y + sizes[1], 1 + shift_z:1 + shift_z + sizes[2]]
    return part.reshape(-1, padded.shape[-1])

def reference(velocity, slot_of, w_encode, w_conv, w_head):
    stencil, select, bottom = element_tables(NP)
    ordered = reorder(velocity, slot_of)
    field = ordered.reshape(N_SIM, N_GRP, 3, EX, EY, EZ, PTS).transpose(2, 0, 3, 1, 4, 5, 6).reshape(3, NXE, NYE, EZ, PTS)
    for step in range(STEPS):
        faces = jnp.einsum('cxyzp,pq->cxyzq', field, select, precision=lax.Precision.HIGHEST)
        before_x = jnp.roll(face_part(faces, 1), 1, axis=1)
        after_x = jnp.roll(face_part(faces, 0), -1, axis=1)
        zero_layer = jnp.zeros_like(face_part(faces, 2)[:, :, :1])
        below = jnp.concatenate([zero_layer, face_part(faces, 3)[:, :, :-1]], axis=2)
        above = jnp.concatenate([face_part(faces, 2)[:, :, 1:], zero_layer], axis=2)
        before_z = jnp.roll(face_part(faces, 5), 1, axis=3)
        after_z = jnp.roll(face_part(faces, 4), -1, axis=3)
        beside = jnp.concatenate([before_x, after_x, below, above, before_z, after_z], axis=-1)
        field = advance(field, faces, beside, stencil, select)
    back = field.reshape(3, N_SIM, EX, N_GRP, EY, EZ, PTS).transpose(1, 3, 0, 2, 4, 5, 6).reshape(N_SIM, N_GRP, 3, E_DEV, PTS)
    inverse = jnp.argsort(slot_of, axis=-1).astype(jnp.int32)
    velocity_next = reorder(back, inverse)
    snapshot = jnp.concatenate([field[0], field[2]], axis=-1).astype(jnp.bfloat16)
    wall_low = jnp.einsum('xyzp,pq->xyzq', field[0], bottom, precision=lax.Precision.HIGHEST)
    wall_side = jnp.einsum('xyzp,pq->xyzq', field[2], bottom, precision=lax.Precision.HIGHEST)
    target = jnp.concatenate([wall_low, wall_side], axis=-1).astype(jnp.bfloat16)

    def cropped(values):
        shaped = values.reshape(N_SIM, EX, NYE, N_GRP, CZ, values.shape[-1])
        return shaped.transpose(0, 3, 1, 2, 4, 5).reshape(N_SIM * N_GRP, EX, NYE, CZ, values.shape[-1])
    crop_x = cropped(snapshot)
    crop_t = cropped(target).reshape(-1, OUT)
    sizes = (EX, NYE, CZ)
    rows = crop_x.reshape(-1, FEAT)
    z1 = jnp.dot(rows, w_encode, preferred_element_type=jnp.float32)
    h1 = jax.nn.silu(z1).astype(jnp.bfloat16)
    crops = crop_x.shape[0]
    pad_one = jnp.pad(h1.reshape(crops, EX, NYE, CZ, CH), ((0, 0), (1, 1), (1, 1), (1, 1), (0, 0)))
    offsets = [(sx, sy, sz) for sx in (-1, 0, 1) for sy in (-1, 0, 1) for sz in (-1, 0, 1)]
    z2 = jnp.zeros((rows.shape[0], CH), jnp.float32)
    for index, (sx, sy, sz) in enumerate(offsets):
        z2 = z2 + jnp.dot(window(pad_one, sx, sy, sz, sizes), w_conv[index], preferred_element_type=jnp.float32)
    h2 = jax.nn.silu(z2).astype(jnp.bfloat16)
    output = jnp.dot(h2, w_head, preferred_element_type=jnp.float32)
    resid = (LOSS_WEIGHT * (output - crop_t.astype(jnp.float32)) / ELEMS).astype(jnp.bfloat16)
    grad_head = jnp.dot(h2.T, resid, preferred_element_type=jnp.float32)
    dh2 = jnp.dot(resid, w_head.T, preferred_element_type=jnp.float32)
    dz2 = (dh2 * silu_grad(z2)).astype(jnp.bfloat16)
    pad_two = jnp.pad(dz2.reshape(crops, EX, NYE, CZ, CH), ((0, 0), (1, 1), (1, 1), (1, 1), (0, 0)))
    grad_list = []
    dh1 = jnp.zeros((rows.shape[0], CH), jnp.float32)
    for index, (sx, sy, sz) in enumerate(offsets):
        grad_list.append(jnp.dot(window(pad_one, sx, sy, sz, sizes).T, dz2, preferred_element_type=jnp.float32))
        dh1 = dh1 + jnp.dot(window(pad_two, -sx, -sy, -sz, sizes), w_conv[index].T, preferred_element_type=jnp.float32)
    grad_conv = jnp.stack(grad_list)
    dz1 = (dh1 * silu_grad(z1)).astype(jnp.bfloat16)
    grad_encode = jnp.dot(rows.T, dz1, preferred_element_type=jnp.float32)
    return (velocity_next, grad_encode, grad_conv, grad_head)
```

```python
import functools

import jax
import jax.numpy as jnp
import ml_dtypes
import numpy as np
from jax import lax
from jax.experimental import pallas as pl
from jax.experimental.pallas import tpu as pltpu
from jax.sharding import PartitionSpec as P

NP = 8
EX = 2
EY = 4
STEPS = 2

VISCOSITY = 0.2
TIME_STEP = 0.005
PENALTY = 100.0
LOSS_WEIGHT = 64.0
FACE_RATE = TIME_STEP * VISCOSITY * PENALTY

F32 = jnp.float32
BF16 = jnp.bfloat16
VMEM_LIMIT = 40 * 1024 * 1024


def derivative_matrix(count):
    places = np.arange(count)
    points = -np.cos(np.pi * places / (count - 1))
    weights = np.where(places % 2 == 0, 1.0, -1.0)
    weights[0] = weights[0] * 0.5
    weights[count - 1] = weights[count - 1] * 0.5
    identity = np.eye(count)
    spread = points[:, None] - points[None, :] + identity
    deriv = weights[None, :] / weights[:, None] / spread
    deriv = deriv * (1.0 - identity)
    return deriv - identity * deriv.sum(axis=1)[:, None]


def short(table):
    return np.asarray(table, np.float32).astype(ml_dtypes.bfloat16)


def in_three(table):
    table = np.asarray(table, np.float32)
    high = table.astype(ml_dtypes.bfloat16)
    low = (table - high.astype(np.float32)).astype(ml_dtypes.bfloat16)
    return np.concatenate([high, high, low], axis=0)


@functools.lru_cache(maxsize=None)
def element_tables():
    count = NP
    deriv = derivative_matrix(count)
    single = np.eye(count)
    square = np.eye(count * count)
    along_x = np.kron(deriv, square)
    along_y = np.kron(single, np.kron(deriv, single))
    along_z = np.kron(square, deriv)
    laplace = along_x @ along_x + along_y @ along_y + along_z @ along_z
    half = count**3 // 2
    grid = np.arange(count**3).reshape(count, count, count)
    final = count - 1
    faces = [
        grid[0].ravel(),
        grid[final].ravel(),
        grid[:, 0].ravel(),
        grid[:, final].ravel(),
        grid[:, :, 0].ravel(),
        grid[:, :, final].ravel(),
    ]

    def pick(which):
        table = np.zeros((count**3, count * count))
        table[which, np.arange(count * count)] = 1.0
        return table

    picks = [pick(which) for which in faces]
    none = np.zeros_like(picks[0])
    taken = np.concatenate([picks[i] for i in (1, 0, 3, 2, 5, 4)], axis=1)
    placed = np.concatenate(picks, axis=1).T
    shares = np.concatenate(picks, axis=1).sum(axis=1)[None, :]
    bottom = np.zeros((count**3, count * count))
    for first in range(count):
        for middle in range(count):
            for inner in range(count):
                bottom[grid[first, middle, inner], first * count + inner] = (
                    VISCOSITY * deriv[0, middle]
                )
    return {
        "lap": in_three(TIME_STEP * VISCOSITY * laplace.T),
        "kx": in_three(-TIME_STEP * along_x.T),
        "ky": in_three(-TIME_STEP * along_y.T[:half, :half]),
        "kz": in_three(-TIME_STEP * along_z.T[:half, :half]),
        "taken": short(taken),
        "placed": short(placed),
        "keep": np.asarray(1.0 - FACE_RATE * shares, np.float32),
        "low_first": short(np.concatenate([picks[2], none], axis=1)),
        "low_second": short(np.concatenate([none, picks[2]], axis=1)),
        "top_first": short(np.concatenate([picks[3], none], axis=1)),
        "top_second": short(np.concatenate([none, picks[3]], axis=1)),
        "wall_first": in_three(np.concatenate([bottom, none], axis=1)),
        "wall_second": in_three(np.concatenate([none, bottom], axis=1)),
    }


def dot(left, right):
    return jnp.dot(left, right, preferred_element_type=F32)


def dot_nt(left, right):
    return lax.dot_general(left, right, (((1,), (1,)), ((), ())), preferred_element_type=F32)


def split_two(value):
    high = value.astype(BF16)
    return high, (value - high.astype(F32)).astype(BF16)


def moved(order, value):
    high = value.astype(BF16)
    rest = value - high.astype(F32)
    middle, low = split_two(rest)
    return dot(order, high) + dot(order, middle) + dot(order, low)


def slot_matrix(slots):
    count = slots.shape[1]
    rows = lax.broadcasted_iota(jnp.int32, (count, count), 0)
    return jnp.where(rows == slots, 1.0, 0.0).astype(F32)


def layer_rows(value, layer, ez):
    step = EY * ez
    start = layer * ez
    return value[start : start + ez], value[step + start : step + start + ez]


def write_edges(fields, tabs, outs, ez):
    lf, ls, tf, ts = tabs
    to_left, to_right, to_below, to_above = outs
    side = NP * NP
    half = EY * ez // 2
    last = NP * side - side
    for c, field in enumerate(fields):
        near = field[0 : 2 * half, 0:side]
        far = field[2 * half : 4 * half, last : last + side]
        to_left[c] = jnp.concatenate([near[:half], near[half:]], axis=1).astype(BF16)
        to_right[c] = jnp.concatenate([far[:half], far[half:]], axis=1).astype(BF16)
        one, two = layer_rows(field, 0, ez)
        to_below[c] = (dot(one.astype(BF16), lf[...]) + dot(two.astype(BF16), ls[...])).astype(BF16)
        one, two = layer_rows(field, EY - 1, ez)
        to_above[c] = (dot(one.astype(BF16), tf[...]) + dot(two.astype(BF16), ts[...])).astype(BF16)


def add_edges(part, c, from_left, from_right, from_below, from_above, tabs, ez):
    lf, ls, tf, ts = tabs
    side = NP * NP
    half = EY * ez // 2
    width = NP * side
    value = part[c]
    left = FACE_RATE * from_left[c].astype(F32)
    right = FACE_RATE * from_right[c].astype(F32)
    below = from_below[c]
    above = from_above[c]
    rest = jnp.zeros((half, width - side), F32)
    x_add = jnp.concatenate(
        [
            jnp.concatenate([left[:, :side], rest], axis=1),
            jnp.concatenate([left[:, side:], rest], axis=1),
            jnp.concatenate([rest, right[:, :side]], axis=1),
            jnp.concatenate([rest, right[:, side:]], axis=1),
        ],
        axis=0,
    )
    none = jnp.zeros(((EY - 2) * ez, width), F32)
    y_add = jnp.concatenate(
        [
            dot_nt(below, lf[...]),
            none,
            dot_nt(above, tf[...]),
            dot_nt(below, ls[...]),
            none,
            dot_nt(above, ts[...]),
        ],
        axis=0,
    )
    return value + x_add + FACE_RATE * y_add


def prepare_kernel(vel, slots, lf, ls, tf, ts, field, to_left, to_right, to_below, to_above):
    ez = vel.shape[1] // (EX * EY)
    order = slot_matrix(slots[...]).T.astype(BF16)
    fields = [moved(order, vel[c]) for c in range(3)]
    for c in range(3):
        field[c] = fields[c]
    write_edges(fields, (lf, ls, tf, ts), (to_left, to_right, to_below, to_above), ez)


def inside_kernel(field, lap, kx, ky, kz, taken, placed, keep, part):
    rows = field.shape[1]
    width = field.shape[2]
    ez = rows // (EX * EY)
    half = width // 2
    whole = field[...].reshape(3 * rows, width)
    high, low = split_two(whole)
    lanes = lax.broadcasted_iota(jnp.int32, (1, 2 * NP * NP), 1)
    first = lanes < NP * NP

    faces = dot(high, taken[...])
    in_x = faces[:, 0 : 2 * NP * NP].reshape(3, EX, EY * ez, 2 * NP * NP)
    beside_x = jnp.concatenate(
        [
            jnp.where(first, 0.0, in_x[:, 1:2]),
            jnp.where(first, in_x[:, 0:1], 0.0),
        ],
        axis=1,
    ).reshape(3 * rows, 2 * NP * NP)
    in_y = faces[:, 2 * NP * NP : 4 * NP * NP].reshape(3 * EX, EY, ez, 2 * NP * NP)
    wall = jnp.zeros((3 * EX, 1, ez, 2 * NP * NP), F32)
    beside_y = jnp.where(
        first,
        jnp.concatenate([wall, in_y[:, :-1]], axis=1),
        jnp.concatenate([in_y[:, 1:], wall], axis=1),
    ).reshape(3 * rows, 2 * NP * NP)
    in_z = faces[:, 4 * NP * NP :].reshape(3 * EX * EY, ez, 2 * NP * NP)
    beside_z = jnp.where(
        first, pltpu.roll(in_z, 1, 1), pltpu.roll(in_z, ez - 1, 1)
    ).reshape(3 * rows, 2 * NP * NP)
    beside = jnp.concatenate([beside_x, beside_y, beside_z], axis=1).astype(BF16)

    three = jnp.concatenate([high, low, high], axis=1)
    for n in range(2):
        cols = slice(n * half, (n + 1) * half)
        own = jnp.concatenate([high[:, cols], low[:, cols], high[:, cols]], axis=1)
        value = whole[:, cols] * keep[:, cols] + dot(three, lap[:, cols])
        value = value + FACE_RATE * dot(beside, placed[:, cols])
        for d, slope in enumerate((dot(three, kx[:, cols]), dot(own, ky[...]), dot(own, kz[...]))):
            speed = field[d][:, cols]
            value = value + (slope.reshape(3, rows, half) * speed[None]).reshape(3 * rows, half)
        part[:, :, cols] = value.reshape(3, rows, half)


def join_kernel(
    part, from_left, from_right, from_below, from_above, lf, ls, tf, ts,
    field, to_left, to_right, to_below, to_above,
):
    ez = part.shape[1] // (EX * EY)
    tabs = (lf, ls, tf, ts)
    fields = [
        add_edges(part, c, from_left, from_right, from_below, from_above, tabs, ez)
        for c in range(3)
    ]
    for c in range(3):
        field[c] = fields[c]
    write_edges(fields, tabs, (to_left, to_right, to_below, to_above), ez)


def encode_kernel(
    part, from_left, from_right, from_below, from_above, lf, ls, tf, ts, wall_one, wall_two,
    w_encode, field, snapshot, target, z1, h1,
):
    ez = part.shape[1] // (EX * EY)
    tabs = (lf, ls, tf, ts)
    fields = [
        add_edges(part, c, from_left, from_right, from_below, from_above, tabs, ez)
        for c in range(3)
    ]
    for c in range(3):
        field[c] = fields[c]
    high0, low0 = split_two(fields[0])
    high2, low2 = split_two(fields[2])
    snap = jnp.concatenate([high0, high2], axis=1)
    snapshot[...] = snap
    target[...] = (
        dot(jnp.concatenate([high0, low0, high0], axis=1), wall_one[...])
        + dot(jnp.concatenate([high2, low2, high2], axis=1), wall_two[...])
    ).astype(BF16)
    hidden = dot(snap, w_encode[...])
    z1[...] = hidden
    h1[...] = (hidden * jax.nn.sigmoid(hidden)).astype(BF16)


def restore_kernel(field, slots, out):
    order = slot_matrix(slots[...]).astype(BF16)
    for c in range(3):
        out[c] = moved(order, field[c])


def silu_grad(value):
    sigma = jax.nn.sigmoid(value)
    return sigma * (1.0 + value * (1.0 - sigma))


def with_layers(own, behind, ahead, ez, groups):
    channels = own.shape[-1]
    place = lax.axis_index("grp")
    grid = own[...].astype(F32).reshape(EX, EY, ez, channels)
    before = behind[...].reshape(EX, EY, ez, channels)[:, EY - 1 :].astype(F32)
    after = ahead[...].reshape(EX, EY, ez, channels)[:, :1].astype(F32)
    before = jnp.where(place > 0, before, 0.0)
    after = jnp.where(place < groups - 1, after, 0.0)
    return jnp.concatenate([before, grid, after], axis=1)


def along_span(grid, ez, groups):
    shape = grid.shape
    rows = int(np.prod(shape[:-1]))
    crop = ez // groups
    flat = grid.reshape(rows, shape[-1])
    place = lax.rem(lax.broadcasted_iota(jnp.int32, (rows, 1), 0), crop)
    before = jnp.where(place == 0, 0.0, pltpu.roll(flat, 1, 0))
    after = jnp.where(place == crop - 1, 0.0, pltpu.roll(flat, rows - 1, 0))
    return before.reshape(shape), after.reshape(shape)


def forward_kernel(groups, total, h1, behind, ahead, w_conv, w_head, target, dz2, h2, resid, padded, z2):
    rows, channels = h1.shape
    ez = rows // (EX * EY)
    grid = with_layers(h1, behind, ahead, ez, groups)
    before, after = along_span(grid, ez, groups)
    padded[...] = jnp.concatenate([before, grid, after], axis=-1).astype(BF16)
    half = rows // 2
    for dy in range(3):
        taken = padded[:, dy : dy + EY].reshape(EX, half, 3 * channels)
        first = 3 * dy
        both = dot(taken.reshape(rows, 3 * channels), w_conv[9 + first : 12 + first].reshape(-1, channels))
        ahead_x = dot(taken[1], w_conv[18 + first : 21 + first].reshape(-1, channels))
        behind_x = dot(taken[0], w_conv[first : 3 + first].reshape(-1, channels))
        step = both + jnp.concatenate([ahead_x, behind_x], axis=0)
        if dy == 0:
            z2[...] = step
        else:
            z2[...] += step
    hidden = z2[...]
    act = (hidden * jax.nn.sigmoid(hidden)).astype(BF16)
    output = dot(act, w_head[...])
    miss = (LOSS_WEIGHT * (output - target[...].astype(F32)) / total).astype(BF16)
    h2[...] = act
    resid[...] = miss
    dz2[...] = (dot_nt(miss, w_head[...]) * silu_grad(hidden)).astype(BF16)


def back_kernel(groups, dz2, behind, ahead, w_conv, z1, snapshot, h2, resid, out, dh1):
    rows, channels = dz2.shape
    ez = rows // (EX * EY)
    half = rows // 2
    grid = with_layers(dz2, behind, ahead, ez, groups)
    before, after = along_span(grid, ez, groups)
    shifted = [part.astype(BF16) for part in (after, grid, before)]
    features = snapshot.shape[1]
    out[:, features:] = dot(h2[...].astype(F32).T.astype(BF16), resid[...]).astype(BF16)
    for dy in range(3):
        for dz in range(3):
            tap = 3 * dy + dz
            taken = shifted[dz][:, 2 - dy : 2 - dy + EY].reshape(EX, half, channels)
            both = dot_nt(taken.reshape(rows, channels), w_conv[9 + tap])
            ahead_x = dot_nt(taken[0], w_conv[18 + tap])
            behind_x = dot_nt(taken[1], w_conv[tap])
            step = both + jnp.concatenate([behind_x, ahead_x], axis=0)
            if tap == 0:
                dh1[...] = step
            else:
                dh1[...] += step
    dz1 = dh1[...] * silu_grad(z1[...])
    out[:, :features] = dot(dz1.T.astype(BF16), snapshot[...]).astype(BF16)


def taps_kernel(groups, h_own, h_one, h_two, h_three, d_own, d_one, d_two, d_three, out, h_all, r_all):
    rows, channels = h_own.shape
    ez = rows // (EX * EY)
    quarter = channels // groups
    crop = ez // groups
    place = lax.axis_index("grp")
    layer = EY * ez
    lane = lax.broadcasted_iota(jnp.int32, (channels, channels), 1)
    channel = lax.broadcasted_iota(jnp.int32, (channels, channels), 0)
    chosen = jnp.where(
        (channel == place * quarter + lax.rem(lane, quarter)) & (lane < 3 * quarter), 1.0, 0.0
    ).astype(BF16)
    pairs = ((h_own, d_own), (h_one, d_one), (h_two, d_two), (h_three, d_three))
    for k, (h, d) in enumerate(pairs):
        at = lax.rem(place - k + groups, groups)
        mine = dot(d[...], chosen)
        for x in range(EX):
            h_all[x, at] = h[x * layer : (x + 1) * layer]
            r_all[x, at] = mine[x * layer : (x + 1) * layer]
    deep = groups * layer
    flat = r_all[...].reshape(EX * deep, channels)
    spot = lax.rem(lax.broadcasted_iota(jnp.int32, (EX * deep, 1), 0), crop)
    lane = lax.broadcasted_iota(jnp.int32, (1, channels), 1)
    after = jnp.where(spot == crop - 1, 0.0, pltpu.roll(flat, EX * deep - 1, 0))
    before = jnp.where(spot == 0, 0.0, pltpu.roll(flat, 1, 0))
    mixed = jnp.where(lane < quarter, after, jnp.where(lane < 2 * quarter, flat, before))
    turned = mixed.T
    spot = lax.rem(lax.broadcasted_iota(jnp.int32, (1, EX * deep), 1), deep)
    up = jnp.where(spot >= deep - ez, 0.0, pltpu.roll(turned, EX * deep - ez, 1))
    down = jnp.where(spot < ez, 0.0, pltpu.roll(turned, ez, 1))
    whole = h_all[...].reshape(EX * deep, channels)
    for dy, side in enumerate((up, turned, down)):
        side = side.astype(BF16)
        for dx in range(3):
            if dx == 0:
                got = dot(side[:, deep:], whole[:deep])
            elif dx == 1:
                got = dot(side, whole)
            else:
                got = dot(side[:, :deep], whole[deep:])
            start = (9 * dx + 3 * dy) * quarter
            out[start : start + 3 * quarter] = got[: 3 * quarter].astype(BF16)


def call(kernel, outs, scratch=(), flops=0):
    return pl.pallas_call(
        kernel,
        out_shape=outs,
        scratch_shapes=list(scratch),
        compiler_params=pltpu.CompilerParams(vmem_limit_bytes=VMEM_LIMIT),
        cost_estimate=pl.CostEstimate(flops=flops, bytes_accessed=4_000_000, transcendentals=0),
    )


def shaped(shape, kind):
    return jax.ShapeDtypeStruct(shape, kind)


def ring(value, axis, steps):
    count = lax.axis_size(axis)
    return lax.ppermute(value, axis, [(i, (i + steps) % count) for i in range(count)])


def line(value, axis, steps):
    count = lax.axis_size(axis)
    return lax.ppermute(value, axis, [(i, i + steps) for i in range(count) if 0 <= i + steps < count])


def exchanged(edges):
    to_left, to_right, to_below, to_above = edges
    from_left = ring(to_right, "sim", 1)
    from_right = ring(to_left, "sim", -1)
    from_below = line(to_above, "grp", 1)
    from_above = line(to_below, "grp", -1)
    return from_left, from_right, from_below, from_above


def body(velocity, slot_of, w_encode, w_conv, w_head):
    tables = {name: jnp.asarray(table) for name, table in element_tables().items()}
    block = velocity[0, 0]
    slots = slot_of[0]
    rows, width = block.shape[1:]
    ez = rows // (EX * EY)
    channels = w_encode.shape[1]
    features = w_encode.shape[0]
    outputs = w_head.shape[1]
    sims = lax.axis_size("sim")
    groups = lax.axis_size("grp")
    total = rows * sims * groups
    quarter = channels // groups

    whole = shaped((3, rows, width), F32)
    x_edge = shaped((3, EY * ez // 2, 2 * NP * NP), BF16)
    y_edge = shaped((3, ez, 2 * NP * NP), BF16)
    edge_shapes = (x_edge, x_edge, y_edge, y_edge)
    picks = [tables[name] for name in ("low_first", "low_second", "top_first", "top_second")]
    inside = [tables[name] for name in ("lap", "kx", "ky", "kz", "taken", "placed", "keep")]

    field, *edges = call(prepare_kernel, (whole,) + edge_shapes, flops=10**9)(block, slots, *picks)
    halos = exchanged(edges)
    part = call(inside_kernel, whole, flops=8 * 10**9)(field, *inside)
    field, *edges = call(join_kernel, (whole,) + edge_shapes, flops=10**9)(part, *halos, *picks)
    halos = exchanged(edges)
    part = call(inside_kernel, whole, flops=8 * 10**9)(field, *inside)
    field, snapshot, target, z1, h1 = call(
        encode_kernel,
        (
            whole,
            shaped((rows, features), BF16),
            shaped((rows, outputs), BF16),
            shaped((rows, channels), F32),
            shaped((rows, channels), BF16),
        ),
        flops=10**9,
    )(part, *halos, *picks, tables["wall_first"], tables["wall_second"], w_encode)

    h_one = ring(h1, "grp", 1)
    h_three = ring(h1, "grp", -1)
    h_two = ring(h1, "grp", 2)
    rows_bf = shaped((rows, channels), BF16)
    dz2, h2, resid = call(
        functools.partial(forward_kernel, groups, total),
        (rows_bf, rows_bf, shaped((rows, outputs), BF16)),
        (
            pltpu.VMEM((EX, EY + 2, ez, 3 * channels), BF16),
            pltpu.VMEM((rows, channels), F32),
        ),
        flops=10**9,
    )(h1, h_one, h_three, w_conv, w_head, target)

    d_one = ring(dz2, "grp", 1)
    d_three = ring(dz2, "grp", -1)
    d_two = ring(dz2, "grp", 2)
    dense = call(
        functools.partial(back_kernel, groups),
        shaped((channels, features + outputs), BF16),
        (pltpu.VMEM((rows, channels), F32),),
        flops=2 * 10**9,
    )(dz2, d_one, d_three, w_conv, z1, snapshot, h2, resid)
    taps = call(
        functools.partial(taps_kernel, groups),
        shaped((27 * quarter, channels), BF16),
        (
            pltpu.VMEM((EX, groups, EY * ez, channels), BF16),
            pltpu.VMEM((EX, groups, EY * ez, channels), F32),
        ),
        flops=2 * 10**9,
    )(h1, h_one, h_two, h_three, dz2, d_one, d_two, d_three)

    velocity_next = call(restore_kernel, whole, flops=10**9)(field, slots)

    tap_rows = 27 * quarter // sims
    taps = lax.all_to_all(taps.reshape(sims, tap_rows, channels), "sim", 0, 0, tiled=True)
    taps = jnp.sum(taps.astype(F32), axis=0).astype(BF16)
    own_rows = quarter // sims
    dense = dense.reshape(groups, sims, own_rows, features + outputs).transpose(1, 0, 2, 3)
    dense = dense.reshape(sims * groups, own_rows, features + outputs)
    dense = lax.all_to_all(dense, ("sim", "grp"), 0, 0, tiled=True)
    dense = jnp.sum(dense.astype(F32), axis=0).astype(BF16)
    extra = -(features + outputs) % channels
    dense = jnp.pad(dense, ((0, 0), (0, extra)))
    mine = jnp.concatenate([taps, dense.reshape(-1, channels)], axis=0)
    everything = lax.all_gather(mine, "sim")
    taps = everything[:, :tap_rows].reshape(27, quarter, channels).astype(F32)
    dense = everything[:, tap_rows:].reshape(quarter, -1)[:, : features + outputs].astype(F32)
    return (
        velocity_next[None, None],
        dense[:, :features].T,
        taps.transpose(0, 2, 1),
        dense[:, features:],
    )


def solution(mesh):
    placed = (P("sim", "grp", None, None, None), P("sim", "grp", None), P(), P(), P())
    return jax.shard_map(
        body,
        mesh=mesh,
        in_specs=placed,
        out_specs=(
            P("sim", "grp", None, None, None),
            P(None, "grp"),
            P(None, None, "grp"),
            P("grp", None),
        ),
        check_vma=False,
    )
```

```python
import functools

import jax
import jax.numpy as jnp
import ml_dtypes
import numpy as np
from jax import lax
from jax.experimental import pallas as pl
from jax.experimental.pallas import tpu as pltpu
from jax.sharding import PartitionSpec as P

NP = 8
EX = 2
EY = 4
STEPS = 2

VISCOSITY = 0.2
TIME_STEP = 0.005
PENALTY = 100.0
LOSS_WEIGHT = 64.0
FACE_RATE = TIME_STEP * VISCOSITY * PENALTY

F32 = jnp.float32
BF16 = jnp.bfloat16
VMEM_LIMIT = 16 * 1024 * 1024


def derivative_matrix(count):
    places = np.arange(count)
    points = -np.cos(np.pi * places / (count - 1))
    weights = np.where(places % 2 == 0, 1.0, -1.0)
    weights[0] = weights[0] * 0.5
    weights[count - 1] = weights[count - 1] * 0.5
    identity = np.eye(count)
    spread = points[:, None] - points[None, :] + identity
    deriv = weights[None, :] / weights[:, None] / spread
    deriv = deriv * (1.0 - identity)
    return deriv - identity * deriv.sum(axis=1)[:, None]


def short(table):
    return np.asarray(table, np.float32).astype(ml_dtypes.bfloat16)


def in_three(table):
    table = np.asarray(table, np.float32)
    high = table.astype(ml_dtypes.bfloat16)
    low = (table - high.astype(np.float32)).astype(ml_dtypes.bfloat16)
    return np.concatenate([high, high, low], axis=0)


@functools.lru_cache(maxsize=None)
def element_tables():
    count = NP
    deriv = derivative_matrix(count)
    single = np.eye(count)
    square = np.eye(count * count)
    along_x = np.kron(deriv, square)
    along_y = np.kron(single, np.kron(deriv, single))
    along_z = np.kron(square, deriv)
    laplace = along_x @ along_x + along_y @ along_y + along_z @ along_z
    half = count**3 // 2
    grid = np.arange(count**3).reshape(count, count, count)
    final = count - 1
    faces = [
        grid[0].ravel(),
        grid[final].ravel(),
        grid[:, 0].ravel(),
        grid[:, final].ravel(),
        grid[:, :, 0].ravel(),
        grid[:, :, final].ravel(),
    ]

    def pick(which):
        table = np.zeros((count**3, count * count))
        table[which, np.arange(count * count)] = 1.0
        return table

    picks = [pick(which) for which in faces]
    none = np.zeros_like(picks[0])
    taken = np.concatenate([picks[i] for i in (1, 0, 3, 2, 5, 4)], axis=1)
    placed = np.concatenate(picks, axis=1).T
    bottom = np.zeros((count**3, count * count))
    for first in range(count):
        for middle in range(count):
            for inner in range(count):
                bottom[grid[first, middle, inner], first * count + inner] = (
                    VISCOSITY * deriv[0, middle]
                )
    first = in_three(TIME_STEP * VISCOSITY * laplace.T)
    second = in_three(-TIME_STEP * along_x.T)
    third = np.concatenate(
        [
            in_three(-TIME_STEP * along_y.T[:half, :half]),
            in_three(-TIME_STEP * along_z.T[:half, :half]),
        ],
        axis=1,
    )
    filled = np.zeros((count**3, count**3 - taken.shape[1]))
    fourth = short(placed)
    fifth = short(np.concatenate([taken, filled], axis=1))
    stencil = np.concatenate([first, second, third, fourth, fifth], axis=0)
    wall = in_three(np.concatenate([bottom, none, none, bottom], axis=1))
    return stencil, wall


def dot(left, right):
    return jnp.dot(left, right, preferred_element_type=F32)


def dot_nt(left, right):
    return lax.dot_general(left, right, (((1,), (1,)), ((), ())), preferred_element_type=F32)


def split_two(value):
    high = value.astype(BF16)
    return high, (value - high.astype(F32)).astype(BF16)


def moved(order, value):
    high = value.astype(BF16)
    rest = value - high.astype(F32)
    middle, low = split_two(rest)
    return dot(order, high) + dot(order, middle) + dot(order, low)


def slot_matrix(slots):
    count = slots.shape[1]
    rows = lax.broadcasted_iota(jnp.int32, (count, count), 0)
    return jnp.where(rows == slots, 1.0, 0.0).astype(F32)


def layer_rows(value, layer, ez):
    step = EY * ez
    start = layer * ez
    return value[start : start + ez], value[step + start : step + start + ez]


def edge_tables():
    side = NP * NP
    point = lax.broadcasted_iota(jnp.int32, (NP * side, 2 * side), 0)
    lane = lax.broadcasted_iota(jnp.int32, (NP * side, 2 * side), 1)
    middle = lax.rem(lax.div(point, NP), NP)
    place = lax.div(point, side) * NP + lax.rem(point, NP)

    def table(level, shift):
        return jnp.where((middle == level) & (lane == place + shift), 1.0, 0.0).astype(BF16)

    return table(0, 0), table(0, side), table(NP - 1, 0), table(NP - 1, side)


def is_even(axis):
    return lax.rem(lax.axis_index(axis), 2) == 0


def write_edges(fields, tabs, outs, ez):
    lf, ls, tf, ts = tabs
    pair_x, cross_x, pair_y, cross_y = outs
    side = NP * NP
    half = EY * ez // 2
    last = NP * side - side
    even_x = is_even("sim")
    even_y = is_even("grp")
    for c, field in enumerate(fields):
        near = field[0 : 2 * half, 0:side]
        far = field[2 * half : 4 * half, last : last + side]
        to_left = jnp.concatenate([near[:half], near[half:]], axis=1)
        to_right = jnp.concatenate([far[:half], far[half:]], axis=1)
        pair_x[c] = jnp.where(even_x, to_right, to_left).astype(BF16)
        cross_x[c] = jnp.where(even_x, to_left, to_right).astype(BF16)
        one, two = layer_rows(field, 0, ez)
        to_below = dot(one.astype(BF16), lf) + dot(two.astype(BF16), ls)
        one, two = layer_rows(field, EY - 1, ez)
        to_above = dot(one.astype(BF16), tf) + dot(two.astype(BF16), ts)
        pair_y[c] = jnp.where(even_y, to_above, to_below).astype(BF16)
        cross_y[c] = jnp.where(even_y, to_below, to_above).astype(BF16)


def add_edges(part, c, pair_x, cross_x, pair_y, cross_y, tabs, ez):
    lf, ls, tf, ts = tabs
    side = NP * NP
    half = EY * ez // 2
    width = NP * side
    value = part[c]
    even_x = is_even("sim")
    even_y = is_even("grp")
    pair = FACE_RATE * pair_x[c].astype(F32)
    cross = FACE_RATE * cross_x[c].astype(F32)
    left = jnp.where(even_x, cross, pair)
    right = jnp.where(even_x, pair, cross)
    pair = pair_y[c].astype(F32)
    cross = cross_y[c].astype(F32)
    below = jnp.where(even_y, cross, pair).astype(BF16)
    above = jnp.where(even_y, pair, cross).astype(BF16)
    rest = jnp.zeros((half, width - side), F32)
    x_add = jnp.concatenate(
        [
            jnp.concatenate([left[:, :side], rest], axis=1),
            jnp.concatenate([left[:, side:], rest], axis=1),
            jnp.concatenate([rest, right[:, :side]], axis=1),
            jnp.concatenate([rest, right[:, side:]], axis=1),
        ],
        axis=0,
    )
    none = jnp.zeros(((EY - 2) * ez, width), F32)
    y_add = jnp.concatenate(
        [
            dot_nt(below, lf),
            none,
            dot_nt(above, tf),
            dot_nt(below, ls),
            none,
            dot_nt(above, ts),
        ],
        axis=0,
    )
    return value + x_add + FACE_RATE * y_add


def prepare_kernel(vel, slots, field, *edges):
    ez = vel.shape[1] // (EX * EY)
    order = slot_matrix(slots[...]).T.astype(BF16)
    fields = [moved(order, vel[c]) for c in range(3)]
    for c in range(3):
        field[c] = fields[c]
    write_edges(fields, edge_tables(), edges, ez)


def face_count(width):
    point = lax.broadcasted_iota(jnp.int32, (1, width), 1)
    count = jnp.zeros((1, width), F32)
    for stride in (NP * NP, NP, 1):
        index = lax.rem(lax.div(point, stride), NP)
        count = count + jnp.where((index == 0) | (index == NP - 1), 1.0, 0.0)
    return count


def inside_kernel(field, stencil, part):
    rows = field.shape[1]
    width = field.shape[2]
    ez = rows // (EX * EY)
    half = width // 2
    chosen = 6 * NP * NP
    lap = stencil.at[0 : 3 * width]
    kx = stencil.at[3 * width : 6 * width]
    kyz = stencil.at[6 * width : 6 * width + 3 * half]
    start = 6 * width + 3 * half
    placed = stencil.at[start : start + chosen]
    taken = stencil.at[start + chosen : start + chosen + width]
    keep = 1.0 - FACE_RATE * face_count(width)
    whole = field[...].reshape(3 * rows, width)
    high, low = split_two(whole)
    lanes = lax.broadcasted_iota(jnp.int32, (1, 2 * NP * NP), 1)
    first = lanes < NP * NP

    faces = dot(high, taken[:, :chosen])
    in_x = faces[:, 0 : 2 * NP * NP].reshape(3, EX, EY * ez, 2 * NP * NP)
    beside_x = jnp.concatenate(
        [
            jnp.where(first, 0.0, in_x[:, 1:2]),
            jnp.where(first, in_x[:, 0:1], 0.0),
        ],
        axis=1,
    ).reshape(3 * rows, 2 * NP * NP)
    in_y = faces[:, 2 * NP * NP : 4 * NP * NP].reshape(3 * EX, EY, ez, 2 * NP * NP)
    wall = jnp.zeros((3 * EX, 1, ez, 2 * NP * NP), F32)
    beside_y = jnp.where(
        first,
        jnp.concatenate([wall, in_y[:, :-1]], axis=1),
        jnp.concatenate([in_y[:, 1:], wall], axis=1),
    ).reshape(3 * rows, 2 * NP * NP)
    in_z = faces[:, 4 * NP * NP :].reshape(3 * EX * EY, ez, 2 * NP * NP)
    beside_z = jnp.where(
        first, pltpu.roll(in_z, 1, 1), pltpu.roll(in_z, ez - 1, 1)
    ).reshape(3 * rows, 2 * NP * NP)
    beside = jnp.concatenate([beside_x, beside_y, beside_z], axis=1).astype(BF16)

    three = jnp.concatenate([high, low, high], axis=1)
    for n in range(2):
        cols = slice(n * half, (n + 1) * half)
        own = jnp.concatenate([high[:, cols], low[:, cols], high[:, cols]], axis=1)
        value = whole[:, cols] * keep[:, cols] + dot(three, lap[:, cols])
        value = value + FACE_RATE * dot(beside, placed[:, cols])
        for d, slope in enumerate(
            (dot(three, kx[:, cols]), dot(own, kyz[:, :half]), dot(own, kyz[:, half:]))
        ):
            speed = field[d][:, cols]
            value = value + (slope.reshape(3, rows, half) * speed[None]).reshape(3 * rows, half)
        part[:, :, cols] = value.reshape(3, rows, half)


def join_kernel(part, pair_x, cross_x, pair_y, cross_y, field, *edges):
    ez = part.shape[1] // (EX * EY)
    tabs = edge_tables()
    fields = [add_edges(part, c, pair_x, cross_x, pair_y, cross_y, tabs, ez) for c in range(3)]
    for c in range(3):
        field[c] = fields[c]
    write_edges(fields, tabs, edges, ez)


def encode_kernel(
    part, pair_x, cross_x, pair_y, cross_y, wall, w_encode,
    field, snapshot, target, z1, h1,
):
    ez = part.shape[1] // (EX * EY)
    tabs = edge_tables()
    fields = [add_edges(part, c, pair_x, cross_x, pair_y, cross_y, tabs, ez) for c in range(3)]
    for c in range(3):
        field[c] = fields[c]
    high0, low0 = split_two(fields[0])
    high2, low2 = split_two(fields[2])
    snap = jnp.concatenate([high0, high2], axis=1)
    snapshot[...] = snap
    target[...] = (
        dot(jnp.concatenate([high0, low0, high0], axis=1), wall[:, : 2 * NP * NP])
        + dot(jnp.concatenate([high2, low2, high2], axis=1), wall[:, 2 * NP * NP :])
    ).astype(BF16)
    hidden = dot(snap, w_encode[...])
    z1[...] = hidden
    h1[...] = (hidden * jax.nn.sigmoid(hidden)).astype(BF16)


def restore_kernel(field, slots, out):
    order = slot_matrix(slots[...]).astype(BF16)
    for c in range(3):
        out[c] = moved(order, field[c])


def silu_grad(value):
    sigma = jax.nn.sigmoid(value)
    return sigma * (1.0 + value * (1.0 - sigma))


def with_layers(own, pair, cross, ez, groups):
    channels = own.shape[-1]
    place = lax.axis_index("grp")
    grid = own[...].astype(F32).reshape(EX, EY, ez, channels)
    even = is_even("grp")
    pair = pair[...].reshape(EX, EY, ez, channels).astype(F32)
    cross = cross[...].reshape(EX, EY, ez, channels).astype(F32)
    before = jnp.where(even, cross[:, EY - 1 :], pair[:, EY - 1 :])
    after = jnp.where(even, pair[:, :1], cross[:, :1])
    before = jnp.where(place > 0, before, 0.0)
    after = jnp.where(place < groups - 1, after, 0.0)
    return jnp.concatenate([before, grid, after], axis=1)


def along_span(grid, ez, groups):
    shape = grid.shape
    rows = int(np.prod(shape[:-1]))
    crop = ez // groups
    flat = grid.reshape(rows, shape[-1])
    place = lax.rem(lax.broadcasted_iota(jnp.int32, (rows, 1), 0), crop)
    before = jnp.where(place == 0, 0.0, pltpu.roll(flat, 1, 0))
    after = jnp.where(place == crop - 1, 0.0, pltpu.roll(flat, rows - 1, 0))
    return before.reshape(shape), after.reshape(shape)


def forward_kernel(groups, total, h1, pair, cross, w_conv, w_head, target, dz2, h2, resid, padded, z2):
    rows, channels = h1.shape
    ez = rows // (EX * EY)
    grid = with_layers(h1, pair, cross, ez, groups)
    before, after = along_span(grid, ez, groups)
    padded[...] = jnp.concatenate([before, grid, after], axis=-1).astype(BF16)
    half = rows // 2
    for dy in range(3):
        taken = padded[:, dy : dy + EY].reshape(EX, half, 3 * channels)
        first = 3 * dy
        both = dot(taken.reshape(rows, 3 * channels), w_conv[9 + first : 12 + first].reshape(-1, channels))
        ahead_x = dot(taken[1], w_conv[18 + first : 21 + first].reshape(-1, channels))
        behind_x = dot(taken[0], w_conv[first : 3 + first].reshape(-1, channels))
        step = both + jnp.concatenate([ahead_x, behind_x], axis=0)
        if dy == 0:
            z2[...] = step
        else:
            z2[...] += step
    hidden = z2[...]
    act = (hidden * jax.nn.sigmoid(hidden)).astype(BF16)
    output = dot(act, w_head[...])
    miss = (LOSS_WEIGHT * (output - target[...].astype(F32)) / total).astype(BF16)
    h2[...] = act
    resid[...] = miss
    dz2[...] = (dot_nt(miss, w_head[...]) * silu_grad(hidden)).astype(BF16)


def back_kernel(
    groups, dz2, pair, cross, w_conv, z1, snapshot, h2, resid,
    to_one, to_two, to_three, kept, dh1, out,
):
    rows, channels = dz2.shape
    ez = rows // (EX * EY)
    half = rows // 2
    grid = with_layers(dz2, pair, cross, ez, groups)
    before, after = along_span(grid, ez, groups)
    shifted = [part.astype(BF16) for part in (after, grid, before)]
    features = snapshot.shape[1]
    out[:, features:] = dot(h2[...].astype(F32).T.astype(BF16), resid[...])
    for dy in range(3):
        for dz in range(3):
            tap = 3 * dy + dz
            taken = shifted[dz][:, 2 - dy : 2 - dy + EY].reshape(EX, half, channels)
            both = dot_nt(taken.reshape(rows, channels), w_conv[9 + tap])
            ahead_x = dot_nt(taken[0], w_conv[18 + tap])
            behind_x = dot_nt(taken[1], w_conv[tap])
            step = both + jnp.concatenate([behind_x, ahead_x], axis=0)
            if tap == 0:
                dh1[...] = step
            else:
                dh1[...] += step
    dz1 = dh1[...] * silu_grad(z1[...])
    out[:, :features] = dot(dz1.T.astype(BF16), snapshot[...])
    quarter = channels // groups
    place = lax.axis_index("grp")
    for k, piece in enumerate((kept, to_one, to_two, to_three)):
        at = pl.multiple_of(jnp.bitwise_xor(place, k) * quarter, quarter)
        piece[...] = out[pl.ds(at, quarter)].astype(piece.dtype)


def taps_kernel(
    groups, sims, h_own, h_one, h_two, h_three, d_own, d_one, d_two, d_three, after_this, *refs
):
    out, h_all, r_all = refs[-3:]
    rows, channels = h_own.shape
    ez = rows // (EX * EY)
    quarter = channels // groups
    crop = ez // groups
    place = lax.axis_index("grp")
    layer = EY * ez
    lane = lax.broadcasted_iota(jnp.int32, (channels, channels), 1)
    channel = lax.broadcasted_iota(jnp.int32, (channels, channels), 0)
    chosen = jnp.where(
        (channel == place * quarter + lax.rem(lane, quarter)) & (lane < 3 * quarter), 1.0, 0.0
    ).astype(BF16)
    pairs = ((h_own, d_own), (h_one, d_one), (h_two, d_two), (h_three, d_three))
    for k, (h, d) in enumerate(pairs):
        at = jnp.bitwise_xor(place, k)
        mine = dot(d[...], chosen)
        for x in range(EX):
            h_all[x, at] = h[x * layer : (x + 1) * layer]
            r_all[x, at] = mine[x * layer : (x + 1) * layer]
    deep = groups * layer
    flat = r_all[...].reshape(EX * deep, channels)
    spot = lax.rem(lax.broadcasted_iota(jnp.int32, (EX * deep, 1), 0), crop)
    lane = lax.broadcasted_iota(jnp.int32, (1, channels), 1)
    after = jnp.where(spot == crop - 1, 0.0, pltpu.roll(flat, EX * deep - 1, 0))
    before = jnp.where(spot == 0, 0.0, pltpu.roll(flat, 1, 0))
    mixed = jnp.where(lane < quarter, after, jnp.where(lane < 2 * quarter, flat, before))
    turned = mixed.T
    spot = lax.rem(lax.broadcasted_iota(jnp.int32, (1, EX * deep), 1), deep)
    up = jnp.where(spot >= deep - ez, 0.0, pltpu.roll(turned, EX * deep - ez, 1))
    down = jnp.where(spot < ez, 0.0, pltpu.roll(turned, ez, 1))
    whole = h_all[...].reshape(EX * deep, channels)
    for dy, side in enumerate((up, turned, down)):
        side = side.astype(BF16)
        for dx in range(3):
            if dx == 0:
                got = dot(side[:, deep:], whole[:deep])
            elif dx == 1:
                got = dot(side, whole)
            else:
                got = dot(side[:, :deep], whole[deep:])
            start = (9 * dx + 3 * dy) * quarter
            out[start : start + 3 * quarter] = got[: 3 * quarter]
    me = lax.rem(lax.axis_index("sim"), sims)
    piece_rows = 27 * quarter // sims
    for k, piece in enumerate(refs[:-3]):
        at = pl.multiple_of(jnp.bitwise_xor(me, k) * piece_rows, 8)
        piece[...] = out[pl.ds(at, piece_rows)].astype(piece.dtype)


def dense_kernel(sims, kept, one, two, three, out_kept, out_sent):
    total = kept[...] + one[...].astype(F32) + two[...].astype(F32) + three[...].astype(F32)
    own_rows = kept.shape[0] // sims
    odd = lax.rem(lax.axis_index("sim"), 2)
    grid = total.reshape(sims // 2, 2, own_rows, kept.shape[1])
    even_part = grid[:, 0]
    odd_part = grid[:, 1]
    mine = jnp.where(odd == 1, odd_part, even_part)
    out_kept[...] = mine
    out_sent[...] = jnp.where(odd == 1, even_part, odd_part).reshape(out_sent.shape).astype(BF16)


def packed(taps, dense):
    channels = taps.shape[1]
    parts = [taps]
    for start in range(0, dense.shape[1], channels):
        piece = dense[:, start : start + channels]
        short_by = channels - piece.shape[1]
        if short_by:
            piece = jnp.concatenate([piece, jnp.zeros((piece.shape[0], short_by), F32)], axis=1)
        parts.append(piece)
    return jnp.concatenate(parts, axis=0)


def pair_sum(mask, taps, taps_in, dense, dense_in):
    at = lax.div(jnp.bitwise_xor(lax.axis_index("sim"), mask), 2)
    own_rows = dense.shape[1]
    got = dense_in[...].astype(F32).reshape(dense.shape)
    also = dense[at]
    for i in range(dense.shape[0]):
        also = also + jnp.where(at == i, got[i], 0.0)
    return packed(taps[...] + taps_in[...].astype(F32), also)


def pair_kernel(mask, taps, taps_in, dense, dense_in, out):
    out[...] = pair_sum(mask, taps, taps_in, dense, dense_in).astype(BF16)


def share_kernel(taps, taps_in, dense, dense_in, *refs):
    total = pair_sum(0, taps, taps_in, dense, dense_in)
    for other in refs[:-1]:
        total = total + other[...].astype(F32)
    refs[-1][...] = total.astype(BF16)


def spread_kernel(features, own, *refs):
    count = len(refs) - 3 + 1
    shares = (own,) + refs[:-3]
    taps, encode, head = refs[-3:]
    channels = own.shape[1]
    tap_rows = taps.shape[0] // count
    own_rows = encode.shape[0] // count
    me = lax.axis_index("sim")
    for k, share in enumerate(shares):
        source = jnp.bitwise_xor(me, k)
        value = share[...].astype(F32)
        taps[pl.ds(pl.multiple_of(source * tap_rows, 8), tap_rows)] = value[:tap_rows]
        rows = pl.ds(pl.multiple_of(source * own_rows, 8), own_rows)
        start = tap_rows
        for first in range(0, features, channels):
            encode[rows, first : first + channels] = value[start : start + own_rows]
            start += own_rows
        head[rows] = value[start : start + own_rows, : head.shape[1]]


def call(kernel, outs, scratch=(), ordered_after=0, inputs=0):
    specs = {}
    if ordered_after:
        specs["in_specs"] = [pl.BlockSpec(memory_space=pltpu.VMEM)] * inputs + [
            pl.BlockSpec(memory_space=pl.ANY)
        ] * ordered_after
    return pl.pallas_call(
        kernel,
        out_shape=outs,
        scratch_shapes=list(scratch),
        compiler_params=pltpu.CompilerParams(vmem_limit_bytes=VMEM_LIMIT),
        cost_estimate=pl.CostEstimate(flops=1000, bytes_accessed=1000, transcendentals=0),
        **specs,
    )


def shaped(shape, kind):
    return jax.ShapeDtypeStruct(shape, kind)


def swapped(value, axis, mask):
    count = lax.axis_size(axis)
    return lax.ppermute(value, axis, [(i, i ^ mask) for i in range(count)])


def crossed(value, axis, periodic):
    count = lax.axis_size(axis)
    route = [(i, i + 1 if i % 2 else i - 1) for i in range(count)]
    if periodic:
        route = [(i, j % count) for i, j in route]
    return lax.ppermute(value, axis, [(i, j) for i, j in route if 0 <= j < count])


def exchanged(edges):
    pair_x, cross_x, pair_y, cross_y = edges
    cross_x = crossed(cross_x, "sim", True)
    pair_x = swapped(pair_x, "sim", 1)
    cross_y = crossed(cross_y, "grp", False)
    pair_y = swapped(pair_y, "grp", 1)
    return pair_x, cross_x, pair_y, cross_y


def gathered(share, sims):
    got = {0: share}
    for k in sorted(range(2, sims, 2), reverse=True):
        got[k] = swapped(share, "sim", k)
    for k in range(0, sims, 2):
        got[k + 1] = swapped(got[k], "sim", 1)
    return [got[k] for k in range(sims)]


def body(velocity, slot_of, w_encode, w_conv, w_head):
    stencil, wall = (jnp.asarray(table) for table in element_tables())
    block = velocity[0, 0]
    slots = slot_of[0]
    rows, width = block.shape[1:]
    ez = rows // (EX * EY)
    channels = w_encode.shape[1]
    features = w_encode.shape[0]
    outputs = w_head.shape[1]
    sims = lax.axis_size("sim")
    groups = lax.axis_size("grp")
    total = rows * sims * groups
    quarter = channels // groups

    whole = shaped((3, rows, width), F32)
    x_edge = shaped((3, EY * ez // 2, 2 * NP * NP), BF16)
    y_edge = shaped((3, ez, 2 * NP * NP), BF16)
    edge_shapes = (x_edge, x_edge, y_edge, y_edge)

    field, *edges = call(prepare_kernel, (whole,) + edge_shapes)(block, slots)
    halos = exchanged(edges)
    part = call(inside_kernel, whole)(field, stencil)
    field, *edges = call(join_kernel, (whole,) + edge_shapes)(part, *halos)
    halos = exchanged(edges)
    part = call(inside_kernel, whole)(field, stencil)
    field, snapshot, target, z1, h1 = call(
        encode_kernel,
        (
            whole,
            shaped((rows, features), BF16),
            shaped((rows, outputs), BF16),
            shaped((rows, channels), F32),
            shaped((rows, channels), BF16),
        ),
    )(part, *halos, wall, w_encode)

    h_one = swapped(h1, "grp", 1)
    h_three = swapped(h1, "grp", 3)
    h_two = swapped(h1, "grp", 2)
    rows_bf = shaped((rows, channels), BF16)
    dz2, h2, resid = call(
        functools.partial(forward_kernel, groups, total),
        (rows_bf, rows_bf, shaped((rows, outputs), BF16)),
        (
            pltpu.VMEM((EX, EY + 2, ez, 3 * channels), BF16),
            pltpu.VMEM((rows, channels), F32),
        ),
    )(h1, h_one, h_three, w_conv, w_head, target)

    d_one = swapped(dz2, "grp", 1)
    d_three = swapped(dz2, "grp", 3)
    d_two = swapped(dz2, "grp", 2)
    wide = features + outputs
    piece = shaped((quarter, wide), BF16)
    e_one, e_two, e_three, e_own = call(
        functools.partial(back_kernel, groups),
        (piece, piece, piece, shaped((quarter, wide), F32)),
        (pltpu.VMEM((rows, channels), F32), pltpu.VMEM((channels, wide), F32)),
    )(dz2, d_one, d_three, w_conv, z1, snapshot, h2, resid)
    tap_rows = 27 * quarter // sims
    own_rows = quarter // sims
    direct = sims == 8
    if direct:
        pieces = [shaped((tap_rows, channels), BF16 if k % 2 else F32) for k in range(sims)]
    else:
        pieces = [shaped((27 * quarter, channels), BF16)]
    taps = call(
        functools.partial(taps_kernel, groups, sims if direct else 1),
        tuple(pieces),
        (
            pltpu.VMEM((27 * quarter, channels), F32),
            pltpu.VMEM((EX, groups, EY * ez, channels), BF16),
            pltpu.VMEM((EX, groups, EY * ez, channels), F32),
        ),
        ordered_after=1,
        inputs=8,
    )(h1, h_one, h_two, h_three, dz2, d_one, d_two, d_three, e_own)
    e_three = swapped(e_three, "grp", 3)
    e_two = swapped(e_two, "grp", 2)
    e_one = swapped(e_one, "grp", 1)

    velocity_next = call(restore_kernel, whole)(field, slots)

    if direct:
        e_kept, e_sent = call(
            functools.partial(dense_kernel, sims),
            (
                shaped((sims // 2, own_rows, wide), F32),
                shaped((sims // 2 * own_rows, wide), BF16),
            ),
        )(e_own, e_one, e_two, e_three)
        taps_in = {k: swapped(taps[k + 1], "sim", 1) for k in (6, 4, 2, 0)}
        e_in = swapped(e_sent, "sim", 1)
        blocks = -(-wide // channels)
        share = shaped((tap_rows + blocks * own_rows, channels), BF16)
        others = []
        for k in (6, 4, 2):
            both = call(functools.partial(pair_kernel, k), share)(taps[k], taps_in[k], e_kept, e_in)
            others.append(swapped(both, "sim", k))
        share = call(share_kernel, share)(taps[0], taps_in[0], e_kept, e_in, *others)
        taps, encode, head = call(
            functools.partial(spread_kernel, features),
            (
                shaped((27 * quarter, channels), F32),
                shaped((quarter, features), F32),
                shaped((quarter, outputs), F32),
            ),
        )(*gathered(share, sims))
    else:
        taps = taps[0].reshape(sims, tap_rows, channels)
        taps = lax.all_to_all(taps, "sim", 0, 0, tiled=True)
        taps = jnp.sum(taps.astype(F32), axis=0).astype(BF16)
        taps = lax.all_gather(taps, "sim").astype(F32)
        dense = e_own + e_one.astype(F32) + e_two.astype(F32) + e_three.astype(F32)
        dense = dense.astype(BF16).reshape(sims, own_rows, wide)
        dense = lax.all_to_all(dense, "sim", 0, 0, tiled=True)
        dense = jnp.sum(dense.astype(F32), axis=0).astype(BF16)
        dense = lax.all_gather(dense, "sim").reshape(quarter, wide).astype(F32)
        encode = dense[:, :features]
        head = dense[:, features:]
    taps = taps.reshape(27, quarter, channels)
    return velocity_next[None, None], encode.T, taps.transpose(0, 2, 1), head


def solution(mesh):
    placed = (P("sim", "grp", None, None, None), P("sim", "grp", None), P(), P(), P())
    return jax.shard_map(
        body,
        mesh=mesh,
        in_specs=placed,
        out_specs=(
            P("sim", "grp", None, None, None),
            P(None, "grp"),
            P(None, None, "grp"),
            P("grp", None),
        ),
        check_vma=False,
    )
```

```python
import functools

import jax
import jax.numpy as jnp
import ml_dtypes
import numpy as np
from jax import lax
from jax.experimental import pallas as pl
from jax.experimental.pallas import tpu as pltpu
from jax.sharding import PartitionSpec as P

NP = 8
EX = 2
EY = 4
STEPS = 2

VISCOSITY = 0.2
TIME_STEP = 0.005
PENALTY = 100.0
LOSS_WEIGHT = 64.0
FACE_RATE = TIME_STEP * VISCOSITY * PENALTY

F32 = jnp.float32
BF16 = jnp.bfloat16
VMEM_LIMIT = 16 * 1024 * 1024


def derivative_matrix(count):
    places = np.arange(count)
    points = -np.cos(np.pi * places / (count - 1))
    weights = np.where(places % 2 == 0, 1.0, -1.0)
    weights[0] = weights[0] * 0.5
    weights[count - 1] = weights[count - 1] * 0.5
    identity = np.eye(count)
    spread = points[:, None] - points[None, :] + identity
    deriv = weights[None, :] / weights[:, None] / spread
    deriv = deriv * (1.0 - identity)
    return deriv - identity * deriv.sum(axis=1)[:, None]


def short(table):
    return np.asarray(table, np.float32).astype(ml_dtypes.bfloat16)


def in_three(table):
    table = np.asarray(table, np.float32)
    high = table.astype(ml_dtypes.bfloat16)
    low = (table - high.astype(np.float32)).astype(ml_dtypes.bfloat16)
    return np.concatenate([high, high, low], axis=0)


@functools.lru_cache(maxsize=None)
def element_tables():
    count = NP
    deriv = derivative_matrix(count)
    single = np.eye(count)
    square = np.eye(count * count)
    along_x = np.kron(deriv, square)
    along_y = np.kron(single, np.kron(deriv, single))
    along_z = np.kron(square, deriv)
    laplace = along_x @ along_x + along_y @ along_y + along_z @ along_z
    half = count**3 // 2
    grid = np.arange(count**3).reshape(count, count, count)
    final = count - 1
    faces = [
        grid[0].ravel(),
        grid[final].ravel(),
        grid[:, 0].ravel(),
        grid[:, final].ravel(),
        grid[:, :, 0].ravel(),
        grid[:, :, final].ravel(),
    ]

    def pick(which):
        table = np.zeros((count**3, count * count))
        table[which, np.arange(count * count)] = 1.0
        return table

    picks = [pick(which) for which in faces]
    none = np.zeros_like(picks[0])
    taken = np.concatenate([picks[i] for i in (1, 0, 3, 2, 5, 4)], axis=1)
    placed = np.concatenate(picks, axis=1).T
    bottom = np.zeros((count**3, count * count))
    for first in range(count):
        for middle in range(count):
            for inner in range(count):
                bottom[grid[first, middle, inner], first * count + inner] = (
                    VISCOSITY * deriv[0, middle]
                )
    first = in_three(TIME_STEP * VISCOSITY * laplace.T)
    second = in_three(-TIME_STEP * along_x.T)
    third = np.concatenate(
        [
            in_three(-TIME_STEP * along_y.T[:half, :half]),
            in_three(-TIME_STEP * along_z.T[:half, :half]),
        ],
        axis=1,
    )
    filled = np.zeros((count**3, count**3 - taken.shape[1]))
    fourth = short(placed)
    fifth = short(np.concatenate([taken, filled], axis=1))
    stencil = np.concatenate([first, second, third, fourth, fifth], axis=0)
    wall = in_three(np.concatenate([bottom, none, none, bottom], axis=1))
    return stencil, wall


def dot(left, right):
    return jnp.dot(left, right, preferred_element_type=F32)


def dot_nt(left, right):
    return lax.dot_general(left, right, (((1,), (1,)), ((), ())), preferred_element_type=F32)


def split_two(value):
    high = value.astype(BF16)
    return high, (value - high.astype(F32)).astype(BF16)


def moved(order, value):
    high = value.astype(BF16)
    rest = value - high.astype(F32)
    middle, low = split_two(rest)
    return dot(order, high) + dot(order, middle) + dot(order, low)


def slot_matrix(slots):
    count = slots.shape[1]
    rows = lax.broadcasted_iota(jnp.int32, (count, count), 0)
    return jnp.where(rows == slots, 1.0, 0.0).astype(F32)


def layer_rows(value, layer, ez):
    step = EY * ez
    start = layer * ez
    return value[start : start + ez], value[step + start : step + start + ez]


def edge_tables():
    side = NP * NP
    point = lax.broadcasted_iota(jnp.int32, (NP * side, 2 * side), 0)
    lane = lax.broadcasted_iota(jnp.int32, (NP * side, 2 * side), 1)
    middle = lax.rem(lax.div(point, NP), NP)
    place = lax.div(point, side) * NP + lax.rem(point, NP)

    def table(level, shift):
        return jnp.where((middle == level) & (lane == place + shift), 1.0, 0.0).astype(BF16)

    return table(0, 0), table(0, side), table(NP - 1, 0), table(NP - 1, side)


def is_even(axis):
    return lax.rem(lax.axis_index(axis), 2) == 0


def write_edges(fields, tabs, outs, ez):
    lf, ls, tf, ts = tabs
    pair_x, cross_x, pair_y, cross_y = outs
    side = NP * NP
    half = EY * ez // 2
    last = NP * side - side
    even_x = is_even("sim")
    even_y = is_even("grp")
    for c, field in enumerate(fields):
        near = field[0 : 2 * half, 0:side]
        far = field[2 * half : 4 * half, last : last + side]
        to_left = jnp.concatenate([near[:half], near[half:]], axis=1)
        to_right = jnp.concatenate([far[:half], far[half:]], axis=1)
        pair_x[c] = jnp.where(even_x, to_right, to_left).astype(BF16)
        cross_x[c] = jnp.where(even_x, to_left, to_right).astype(BF16)
        one, two = layer_rows(field, 0, ez)
        to_below = dot(one.astype(BF16), lf) + dot(two.astype(BF16), ls)
        one, two = layer_rows(field, EY - 1, ez)
        to_above = dot(one.astype(BF16), tf) + dot(two.astype(BF16), ts)
        pair_y[c] = jnp.where(even_y, to_above, to_below).astype(BF16)
        cross_y[c] = jnp.where(even_y, to_below, to_above).astype(BF16)


def add_edges(part, c, pair_x, cross_x, pair_y, cross_y, tabs, ez):
    lf, ls, tf, ts = tabs
    side = NP * NP
    half = EY * ez // 2
    width = NP * side
    value = part[c]
    even_x = is_even("sim")
    even_y = is_even("grp")
    pair = FACE_RATE * pair_x[c].astype(F32)
    cross = FACE_RATE * cross_x[c].astype(F32)
    left = jnp.where(even_x, cross, pair)
    right = jnp.where(even_x, pair, cross)
    pair = pair_y[c].astype(F32)
    cross = cross_y[c].astype(F32)
    below = jnp.where(even_y, cross, pair).astype(BF16)
    above = jnp.where(even_y, pair, cross).astype(BF16)
    rest = jnp.zeros((half, width - side), F32)
    x_add = jnp.concatenate(
        [
            jnp.concatenate([left[:, :side], rest], axis=1),
            jnp.concatenate([left[:, side:], rest], axis=1),
            jnp.concatenate([rest, right[:, :side]], axis=1),
            jnp.concatenate([rest, right[:, side:]], axis=1),
        ],
        axis=0,
    )
    none = jnp.zeros(((EY - 2) * ez, width), F32)
    y_add = jnp.concatenate(
        [
            dot_nt(below, lf),
            none,
            dot_nt(above, tf),
            dot_nt(below, ls),
            none,
            dot_nt(above, ts),
        ],
        axis=0,
    )
    return value + x_add + FACE_RATE * y_add


def prepare_kernel(vel, slots, field, *edges):
    ez = vel.shape[1] // (EX * EY)
    order = slot_matrix(slots[...]).T.astype(BF16)
    fields = [moved(order, vel[c]) for c in range(3)]
    for c in range(3):
        field[c] = fields[c]
    write_edges(fields, edge_tables(), edges, ez)


def face_count(width):
    point = lax.broadcasted_iota(jnp.int32, (1, width), 1)
    count = jnp.zeros((1, width), F32)
    for stride in (NP * NP, NP, 1):
        index = lax.rem(lax.div(point, stride), NP)
        count = count + jnp.where((index == 0) | (index == NP - 1), 1.0, 0.0)
    return count


def inside_kernel(field, stencil, part):
    rows = field.shape[1]
    width = field.shape[2]
    ez = rows // (EX * EY)
    half = width // 2
    chosen = 6 * NP * NP
    lap = stencil.at[0 : 3 * width]
    kx = stencil.at[3 * width : 6 * width]
    kyz = stencil.at[6 * width : 6 * width + 3 * half]
    start = 6 * width + 3 * half
    placed = stencil.at[start : start + chosen]
    taken = stencil.at[start + chosen : start + chosen + width]
    keep = 1.0 - FACE_RATE * face_count(width)
    whole = field[...].reshape(3 * rows, width)
    high, low = split_two(whole)
    lanes = lax.broadcasted_iota(jnp.int32, (1, 2 * NP * NP), 1)
    first = lanes < NP * NP

    faces = dot(high, taken[:, :chosen])
    in_x = faces[:, 0 : 2 * NP * NP].reshape(3, EX, EY * ez, 2 * NP * NP)
    beside_x = jnp.concatenate(
        [
            jnp.where(first, 0.0, in_x[:, 1:2]),
            jnp.where(first, in_x[:, 0:1], 0.0),
        ],
        axis=1,
    ).reshape(3 * rows, 2 * NP * NP)
    in_y = faces[:, 2 * NP * NP : 4 * NP * NP].reshape(3 * EX, EY, ez, 2 * NP * NP)
    wall = jnp.zeros((3 * EX, 1, ez, 2 * NP * NP), F32)
    beside_y = jnp.where(
        first,
        jnp.concatenate([wall, in_y[:, :-1]], axis=1),
        jnp.concatenate([in_y[:, 1:], wall], axis=1),
    ).reshape(3 * rows, 2 * NP * NP)
    in_z = faces[:, 4 * NP * NP :].reshape(3 * EX * EY, ez, 2 * NP * NP)
    beside_z = jnp.where(
        first, pltpu.roll(in_z, 1, 1), pltpu.roll(in_z, ez - 1, 1)
    ).reshape(3 * rows, 2 * NP * NP)
    beside = jnp.concatenate([beside_x, beside_y, beside_z], axis=1).astype(BF16)

    three = jnp.concatenate([high, low, high], axis=1)
    for n in range(2):
        cols = slice(n * half, (n + 1) * half)
        own = jnp.concatenate([high[:, cols], low[:, cols], high[:, cols]], axis=1)
        value = whole[:, cols] * keep[:, cols] + dot(three, lap[:, cols])
        value = value + FACE_RATE * dot(beside, placed[:, cols])
        for d, slope in enumerate(
            (dot(three, kx[:, cols]), dot(own, kyz[:, :half]), dot(own, kyz[:, half:]))
        ):
            speed = field[d][:, cols]
            value = value + (slope.reshape(3, rows, half) * speed[None]).reshape(3 * rows, half)
        part[:, :, cols] = value.reshape(3, rows, half)


def join_kernel(part, pair_x, cross_x, pair_y, cross_y, field, *edges):
    ez = part.shape[1] // (EX * EY)
    tabs = edge_tables()
    fields = [add_edges(part, c, pair_x, cross_x, pair_y, cross_y, tabs, ez) for c in range(3)]
    for c in range(3):
        field[c] = fields[c]
    write_edges(fields, tabs, edges, ez)


def encode_kernel(
    part, pair_x, cross_x, pair_y, cross_y, wall, w_encode,
    field, snapshot, target, z1, h1,
):
    ez = part.shape[1] // (EX * EY)
    tabs = edge_tables()
    fields = [add_edges(part, c, pair_x, cross_x, pair_y, cross_y, tabs, ez) for c in range(3)]
    for c in range(3):
        field[c] = fields[c]
    high0, low0 = split_two(fields[0])
    high2, low2 = split_two(fields[2])
    snap = jnp.concatenate([high0, high2], axis=1)
    snapshot[...] = snap
    target[...] = (
        dot(jnp.concatenate([high0, low0, high0], axis=1), wall[:, : 2 * NP * NP])
        + dot(jnp.concatenate([high2, low2, high2], axis=1), wall[:, 2 * NP * NP :])
    ).astype(BF16)
    hidden = dot(snap, w_encode[...])
    z1[...] = hidden
    h1[...] = (hidden * jax.nn.sigmoid(hidden)).astype(BF16)


def restore_kernel(field, slots, after_this, out):
    order = slot_matrix(slots[...]).astype(BF16)
    for c in range(3):
        out[c] = moved(order, field[c])


def silu_grad(value):
    sigma = jax.nn.sigmoid(value)
    return sigma * (1.0 + value * (1.0 - sigma))


def with_layers(own, pair, cross, ez, groups):
    channels = own.shape[-1]
    place = lax.axis_index("grp")
    grid = own[...].astype(F32).reshape(EX, EY, ez, channels)
    even = is_even("grp")
    pair = pair[...].reshape(EX, EY, ez, channels).astype(F32)
    cross = cross[...].reshape(EX, EY, ez, channels).astype(F32)
    before = jnp.where(even, cross[:, EY - 1 :], pair[:, EY - 1 :])
    after = jnp.where(even, pair[:, :1], cross[:, :1])
    before = jnp.where(place > 0, before, 0.0)
    after = jnp.where(place < groups - 1, after, 0.0)
    return jnp.concatenate([before, grid, after], axis=1)


def along_span(grid, ez, groups):
    shape = grid.shape
    rows = int(np.prod(shape[:-1]))
    crop = ez // groups
    flat = grid.reshape(rows, shape[-1])
    place = lax.rem(lax.broadcasted_iota(jnp.int32, (rows, 1), 0), crop)
    before = jnp.where(place == 0, 0.0, pltpu.roll(flat, 1, 0))
    after = jnp.where(place == crop - 1, 0.0, pltpu.roll(flat, rows - 1, 0))
    return before.reshape(shape), after.reshape(shape)


def forward_kernel(groups, total, h1, pair, cross, w_conv, w_head, target, dz2, h2, resid, padded, z2):
    rows, channels = h1.shape
    ez = rows // (EX * EY)
    grid = with_layers(h1, pair, cross, ez, groups)
    before, after = along_span(grid, ez, groups)
    padded[...] = jnp.concatenate([before, grid, after], axis=-1).astype(BF16)
    half = rows // 2
    for dy in range(3):
        taken = padded[:, dy : dy + EY].reshape(EX, half, 3 * channels)
        first = 3 * dy
        both = dot(taken.reshape(rows, 3 * channels), w_conv[9 + first : 12 + first].reshape(-1, channels))
        ahead_x = dot(taken[1], w_conv[18 + first : 21 + first].reshape(-1, channels))
        behind_x = dot(taken[0], w_conv[first : 3 + first].reshape(-1, channels))
        step = both + jnp.concatenate([ahead_x, behind_x], axis=0)
        if dy == 0:
            z2[...] = step
        else:
            z2[...] += step
    hidden = z2[...]
    act = (hidden * jax.nn.sigmoid(hidden)).astype(BF16)
    output = dot(act, w_head[...])
    miss = (LOSS_WEIGHT * (output - target[...].astype(F32)) / total).astype(BF16)
    h2[...] = act
    resid[...] = miss
    dz2[...] = (dot_nt(miss, w_head[...]) * silu_grad(hidden)).astype(BF16)


def back_kernel(
    groups, dz2, pair, cross, w_conv, z1, snapshot, h2, resid,
    kept, sent, dh1, out,
):
    rows, channels = dz2.shape
    ez = rows // (EX * EY)
    half = rows // 2
    grid = with_layers(dz2, pair, cross, ez, groups)
    before, after = along_span(grid, ez, groups)
    shifted = [part.astype(BF16) for part in (after, grid, before)]
    features = snapshot.shape[1]
    out[:, features:] = dot(h2[...].astype(F32).T.astype(BF16), resid[...])
    for dy in range(3):
        for dz in range(3):
            tap = 3 * dy + dz
            taken = shifted[dz][:, 2 - dy : 2 - dy + EY].reshape(EX, half, channels)
            both = dot_nt(taken.reshape(rows, channels), w_conv[9 + tap])
            ahead_x = dot_nt(taken[0], w_conv[18 + tap])
            behind_x = dot_nt(taken[1], w_conv[tap])
            step = both + jnp.concatenate([behind_x, ahead_x], axis=0)
            if tap == 0:
                dh1[...] = step
            else:
                dh1[...] += step
    dz1 = dh1[...] * silu_grad(z1[...])
    out[:, :features] = dot(dz1.T.astype(BF16), snapshot[...])
    quarter = channels // groups
    place = lax.axis_index("grp")
    for k in range(groups):
        piece = sent if k % 2 else kept
        at = pl.multiple_of(jnp.bitwise_xor(place, k) * quarter, quarter)
        piece[k // 2] = out[pl.ds(at, quarter)].astype(piece.dtype)


def core_kernel(kept, got, out_kept, out_sent):
    out_kept[...] = kept[0] + got[0].astype(F32)
    out_sent[...] = (kept[1] + got[1].astype(F32)).astype(BF16)


def taps_kernel(
    groups, sims, h_own, h_one, h_two, h_three, d_own, d_one, d_two, d_three, after_this, *refs
):
    out, h_all, r_all = refs[-3:]
    rows, channels = h_own.shape
    ez = rows // (EX * EY)
    quarter = channels // groups
    crop = ez // groups
    place = lax.axis_index("grp")
    layer = EY * ez
    lane = lax.broadcasted_iota(jnp.int32, (channels, channels), 1)
    channel = lax.broadcasted_iota(jnp.int32, (channels, channels), 0)
    chosen = jnp.where(
        (channel == place * quarter + lax.rem(lane, quarter)) & (lane < 3 * quarter), 1.0, 0.0
    ).astype(BF16)
    pairs = ((h_own, d_own), (h_one, d_one), (h_two, d_two), (h_three, d_three))
    for k, (h, d) in enumerate(pairs):
        at = jnp.bitwise_xor(place, k)
        mine = dot(d[...], chosen)
        for x in range(EX):
            h_all[x, at] = h[x * layer : (x + 1) * layer]
            r_all[x, at] = mine[x * layer : (x + 1) * layer]
    deep = groups * layer
    flat = r_all[...].reshape(EX * deep, channels)
    spot = lax.rem(lax.broadcasted_iota(jnp.int32, (EX * deep, 1), 0), crop)
    lane = lax.broadcasted_iota(jnp.int32, (1, channels), 1)
    after = jnp.where(spot == crop - 1, 0.0, pltpu.roll(flat, EX * deep - 1, 0))
    before = jnp.where(spot == 0, 0.0, pltpu.roll(flat, 1, 0))
    mixed = jnp.where(lane < quarter, after, jnp.where(lane < 2 * quarter, flat, before))
    turned = mixed.T
    spot = lax.rem(lax.broadcasted_iota(jnp.int32, (1, EX * deep), 1), deep)
    up = jnp.where(spot >= deep - ez, 0.0, pltpu.roll(turned, EX * deep - ez, 1))
    down = jnp.where(spot < ez, 0.0, pltpu.roll(turned, ez, 1))
    whole = h_all[...].reshape(EX * deep, channels)
    for dy, side in enumerate((up, turned, down)):
        side = side.astype(BF16)
        for dx in range(3):
            if dx == 0:
                got = dot(side[:, deep:], whole[:deep])
            elif dx == 1:
                got = dot(side, whole)
            else:
                got = dot(side[:, :deep], whole[deep:])
            start = (9 * dx + 3 * dy) * quarter
            out[start : start + 3 * quarter] = got[: 3 * quarter]
    me = lax.rem(lax.axis_index("sim"), sims)
    piece_rows = 27 * quarter // sims
    for k, piece in enumerate(refs[:-3]):
        at = pl.multiple_of(jnp.bitwise_xor(me, k) * piece_rows, 8)
        piece[...] = out[pl.ds(at, piece_rows)].astype(piece.dtype)


def dense_kernel(kept, got, out_kept, out_sent):
    total = kept[...] + got[...].astype(F32)
    grid = total.reshape(2, 2, kept.shape[0] // 4, kept.shape[1])
    odd = lax.rem(lax.div(lax.axis_index("sim"), 2), 2) == 1
    out_kept[...] = jnp.where(odd, grid[:, 1], grid[:, 0])
    out_sent[...] = jnp.where(odd, grid[:, 0], grid[:, 1]).astype(BF16)


def half_kernel(scale, kept, got, out_kept, out_sent):
    total = kept[...] + got[...].astype(F32)
    upper = lax.rem(lax.div(lax.axis_index("sim"), scale), 2) == 1
    out_kept[...] = jnp.where(upper, total[1], total[0])
    out_sent[...] = jnp.where(upper, total[0], total[1]).astype(BF16)


def packed(taps, dense):
    channels = taps.shape[1]
    parts = [taps]
    for start in range(0, dense.shape[1], channels):
        piece = dense[:, start : start + channels]
        short_by = channels - piece.shape[1]
        if short_by:
            piece = jnp.concatenate([piece, jnp.zeros((piece.shape[0], short_by), F32)], axis=1)
        parts.append(piece)
    return jnp.concatenate(parts, axis=0)


def sum_kernel(parts, kept, *refs):
    total = kept[...]
    for other in refs[: parts - 1]:
        total = total + other[...].astype(F32)
    refs[-1][...] = total.astype(BF16)


def share_kernel(taps, one, two, three, dense, dense_in, out):
    total = taps[...]
    for other in (one, two, three):
        total = total + other[...].astype(F32)
    out[...] = packed(total, dense[...] + dense_in[...].astype(F32)).astype(BF16)


def spread_kernel(features, own, *refs):
    count = len(refs) - 3 + 1
    shares = (own,) + refs[:-3]
    taps, encode, head = refs[-3:]
    channels = own.shape[1]
    tap_rows = taps.shape[0] // count
    own_rows = encode.shape[0] // count
    me = lax.axis_index("sim")
    for k, share in enumerate(shares):
        source = jnp.bitwise_xor(me, k)
        value = share[...].astype(F32)
        taps[pl.ds(pl.multiple_of(source * tap_rows, 8), tap_rows)] = value[:tap_rows]
        rows = pl.ds(pl.multiple_of(source * own_rows, 8), own_rows)
        start = tap_rows
        for first in range(0, features, channels):
            encode[rows, first : first + channels] = value[start : start + own_rows]
            start += own_rows
        head[rows] = value[start : start + own_rows, : head.shape[1]]


def call(kernel, outs, scratch=(), in_hbm=(), inputs=0, flops=1000):
    specs = {}
    if in_hbm:
        specs["in_specs"] = [
            pl.BlockSpec(memory_space=pl.ANY if i in in_hbm else pltpu.VMEM) for i in range(inputs)
        ]
    return pl.pallas_call(
        kernel,
        out_shape=outs,
        scratch_shapes=list(scratch),
        compiler_params=pltpu.CompilerParams(vmem_limit_bytes=VMEM_LIMIT),
        cost_estimate=pl.CostEstimate(flops=flops, bytes_accessed=1000, transcendentals=0),
        **specs,
    )


def shaped(shape, kind):
    return jax.ShapeDtypeStruct(shape, kind)


def swapped(value, axis, mask):
    count = lax.axis_size(axis)
    return lax.ppermute(value, axis, [(i, i ^ mask) for i in range(count)])


def crossed(value, axis, periodic):
    count = lax.axis_size(axis)
    route = [(i, i + 1 if i % 2 else i - 1) for i in range(count)]
    if periodic:
        route = [(i, j % count) for i, j in route]
    return lax.ppermute(value, axis, [(i, j) for i, j in route if 0 <= j < count])


def exchanged(edges):
    pair_x, cross_x, pair_y, cross_y = edges
    cross_x = crossed(cross_x, "sim", True)
    pair_x = swapped(pair_x, "sim", 1)
    cross_y = crossed(cross_y, "grp", False)
    pair_y = swapped(pair_y, "grp", 1)
    return pair_x, cross_x, pair_y, cross_y


def gathered(share, sims):
    got = {0: share}
    for k in sorted(range(2, sims, 2), reverse=True):
        got[k] = swapped(share, "sim", k)
    for k in range(0, sims, 2):
        got[k + 1] = swapped(got[k], "sim", 1)
    return [got[k] for k in range(sims)]


def body(velocity, slot_of, w_encode, w_conv, w_head):
    stencil, wall = (jnp.asarray(table) for table in element_tables())
    block = velocity[0, 0]
    slots = slot_of[0]
    rows, width = block.shape[1:]
    ez = rows // (EX * EY)
    channels = w_encode.shape[1]
    features = w_encode.shape[0]
    outputs = w_head.shape[1]
    sims = lax.axis_size("sim")
    groups = lax.axis_size("grp")
    total = rows * sims * groups
    quarter = channels // groups

    whole = shaped((3, rows, width), F32)
    x_edge = shaped((3, EY * ez // 2, 2 * NP * NP), BF16)
    y_edge = shaped((3, ez, 2 * NP * NP), BF16)
    edge_shapes = (x_edge, x_edge, y_edge, y_edge)

    field, *edges = call(prepare_kernel, (whole,) + edge_shapes, flops=4 * 10**9)(block, slots)
    halos = exchanged(edges)
    part = call(inside_kernel, whole)(field, stencil)
    field, *edges = call(join_kernel, (whole,) + edge_shapes)(part, *halos)
    halos = exchanged(edges)
    part = call(inside_kernel, whole)(field, stencil)
    field, snapshot, target, z1, h1 = call(
        encode_kernel,
        (
            whole,
            shaped((rows, features), BF16),
            shaped((rows, outputs), BF16),
            shaped((rows, channels), F32),
            shaped((rows, channels), BF16),
        ),
    )(part, *halos, wall, w_encode)

    h_three = swapped(h1, "grp", 3)
    h_one = swapped(h1, "grp", 1)
    h_two = swapped(h_three, "grp", 1)
    rows_bf = shaped((rows, channels), BF16)
    dz2, h2, resid = call(
        functools.partial(forward_kernel, groups, total),
        (rows_bf, rows_bf, shaped((rows, outputs), BF16)),
        (
            pltpu.VMEM((EX, EY + 2, ez, 3 * channels), BF16),
            pltpu.VMEM((rows, channels), F32),
        ),
    )(h1, h_one, h_three, w_conv, w_head, target)

    d_three = swapped(dz2, "grp", 3)
    d_one = swapped(dz2, "grp", 1)
    d_two = swapped(d_three, "grp", 1)
    wide = features + outputs
    pair = (groups // 2, quarter, wide)
    e_kept, e_sent = call(
        functools.partial(back_kernel, groups),
        (shaped(pair, F32), shaped(pair, BF16)),
        (pltpu.VMEM((rows, channels), F32), pltpu.VMEM((channels, wide), F32)),
    )(dz2, d_one, d_three, w_conv, z1, snapshot, h2, resid)
    e_got = swapped(e_sent, "grp", 1)
    e_kept, e_sent = call(core_kernel, (shaped(pair[1:], F32), shaped(pair[1:], BF16)))(e_kept, e_got)
    e_got = swapped(e_sent, "grp", 2)
    tap_rows = 27 * quarter // sims
    own_rows = quarter // sims
    direct = sims == 8
    if direct:
        pieces = [shaped((tap_rows, channels), BF16 if k % 2 else F32) for k in range(sims)]
    else:
        pieces = [shaped((27 * quarter, channels), BF16)]
    taps = call(
        functools.partial(taps_kernel, groups, sims if direct else 1),
        tuple(pieces),
        (
            pltpu.VMEM((27 * quarter, channels), F32),
            pltpu.VMEM((EX, groups, EY * ez, channels), BF16),
            pltpu.VMEM((EX, groups, EY * ez, channels), F32),
        ),
        in_hbm=(8,),
        inputs=9,
    )(h1, h_one, h_two, h_three, dz2, d_one, d_two, d_three, e_kept)
    if direct:
        taps_in = {k: swapped(taps[k + 1], "sim", 1) for k in (6, 4, 2, 0)}
        tap_piece = shaped((tap_rows, channels), BF16)
        part = (2, 2 * own_rows, wide)
        e_kept, e_sent = call(dense_kernel, (shaped(part, F32), shaped(part, BF16)))(e_kept, e_got)
        e_got = swapped(e_sent, "sim", 2)
        add_two = call(functools.partial(sum_kernel, 2), tap_piece)
        add_three = call(functools.partial(sum_kernel, 3), tap_piece)
        six = swapped(add_two(taps[6], taps_in[6], e_sent), "sim", 2)
        two = swapped(add_two(taps[2], taps_in[2]), "sim", 2)
        part = shaped((2 * own_rows, wide), F32), shaped((2 * own_rows, wide), BF16)
        e_kept, e_sent = call(functools.partial(half_kernel, 4), part)(e_kept, e_got)
        e_got = swapped(e_sent, "sim", 4)
        four = swapped(add_three(taps[4], taps_in[4], six, e_sent), "sim", 4)
        part = shaped((own_rows, wide), F32), shaped((own_rows, wide), BF16)
        e_kept, e_sent = call(functools.partial(half_kernel, 1), part)(
            e_kept.reshape(2, own_rows, wide), e_got.reshape(2, own_rows, wide)
        )
        e_got = swapped(e_sent, "sim", 1)
        blocks = -(-wide // channels)
        share = call(share_kernel, shaped((tap_rows + blocks * own_rows, channels), BF16))(
            taps[0], taps_in[0], two, four, e_kept, e_got
        )
        velocity_next = call(restore_kernel, whole, in_hbm=(2,), inputs=3)(field, slots, share)
        taps, encode, head = call(
            functools.partial(spread_kernel, features),
            (
                shaped((27 * quarter, channels), F32),
                shaped((quarter, features), F32),
                shaped((quarter, outputs), F32),
            ),
        )(*gathered(share, sims))
    else:
        taps = taps[0].reshape(sims, tap_rows, channels)
        taps = lax.all_to_all(taps, "sim", 0, 0, tiled=True)
        taps = jnp.sum(taps.astype(F32), axis=0).astype(BF16)
        taps = lax.all_gather(taps, "sim").astype(F32)
        velocity_next = call(restore_kernel, whole, in_hbm=(2,), inputs=3)(field, slots, e_kept)
        dense = e_kept + e_got.astype(F32)
        dense = dense.astype(BF16).reshape(sims, own_rows, wide)
        dense = lax.all_to_all(dense, "sim", 0, 0, tiled=True)
        dense = jnp.sum(dense.astype(F32), axis=0).astype(BF16)
        dense = lax.all_gather(dense, "sim").reshape(quarter, wide).astype(F32)
        encode = dense[:, :features]
        head = dense[:, features:]
    taps = taps.reshape(27, quarter, channels)
    return velocity_next[None, None], encode.T, taps.transpose(0, 2, 1), head


def solution(mesh):
    placed = (P("sim", "grp", None, None, None), P("sim", "grp", None), P(), P(), P())
    return jax.shard_map(
        body,
        mesh=mesh,
        in_specs=placed,
        out_specs=(
            P("sim", "grp", None, None, None),
            P(None, "grp"),
            P(None, None, "grp"),
            P("grp", None),
        ),
        check_vma=False,
    )
```

```python
import functools

import jax
import jax.numpy as jnp
import ml_dtypes
import numpy as np
from jax import lax
from jax.experimental import pallas as pl
from jax.experimental.pallas import tpu as pltpu
from jax.sharding import PartitionSpec as P

NP = 8
EX = 2
EY = 4
STEPS = 2

VISCOSITY = 0.2
TIME_STEP = 0.005
PENALTY = 100.0
LOSS_WEIGHT = 64.0
FACE_RATE = TIME_STEP * VISCOSITY * PENALTY

F32 = jnp.float32
BF16 = jnp.bfloat16
VMEM_LIMIT = 16 * 1024 * 1024


def derivative_matrix(count):
    places = np.arange(count)
    points = -np.cos(np.pi * places / (count - 1))
    weights = np.where(places % 2 == 0, 1.0, -1.0)
    weights[0] = weights[0] * 0.5
    weights[count - 1] = weights[count - 1] * 0.5
    identity = np.eye(count)
    spread = points[:, None] - points[None, :] + identity
    deriv = weights[None, :] / weights[:, None] / spread
    deriv = deriv * (1.0 - identity)
    return deriv - identity * deriv.sum(axis=1)[:, None]


def short(table):
    return np.asarray(table, np.float32).astype(ml_dtypes.bfloat16)


def in_three(table):
    table = np.asarray(table, np.float32)
    high = table.astype(ml_dtypes.bfloat16)
    low = (table - high.astype(np.float32)).astype(ml_dtypes.bfloat16)
    return np.concatenate([high, high, low], axis=0)


@functools.lru_cache(maxsize=None)
def element_tables():
    count = NP
    deriv = derivative_matrix(count)
    single = np.eye(count)
    square = np.eye(count * count)
    grid = np.arange(count**3).reshape(count, count, count)
    final = count - 1
    faces = [
        grid[0].ravel(),
        grid[final].ravel(),
        grid[:, 0].ravel(),
        grid[:, final].ravel(),
        grid[:, :, 0].ravel(),
        grid[:, :, final].ravel(),
    ]

    def pick(which):
        table = np.zeros((count**3, count * count))
        table[which, np.arange(count * count)] = 1.0
        return table

    picks = [pick(which) for which in faces]
    none = np.zeros_like(picks[0])
    taken = np.concatenate([picks[i] for i in (3, 2, 5, 4)], axis=1)
    placed = np.concatenate(picks[2:], axis=1).T
    bottom = np.zeros((count**3, count * count))
    for first in range(count):
        for middle in range(count):
            for inner in range(count):
                bottom[grid[first, middle, inner], first * count + inner] = (
                    VISCOSITY * deriv[0, middle]
                )
    mirrored = np.concatenate([deriv, deriv @ deriv], axis=0)[:, ::-1].reshape(2, count, count)
    straight = np.stack([deriv, deriv @ deriv])
    half = count // 2
    scale = np.array([-TIME_STEP, TIME_STEP * VISCOSITY])[:, None, None]

    def along_first(sign):
        mixed = (0.5 * scale * (straight + sign * mirrored))[:, :half, :half]
        return in_three(np.concatenate([np.kron(part.T, square) for part in mixed], axis=1))

    small_y = np.kron(deriv, single)
    small_z = np.kron(single, deriv)
    curved = TIME_STEP * VISCOSITY * (small_y @ small_y + small_z @ small_z).T
    small_y = -TIME_STEP * small_y.T
    small_z = -TIME_STEP * small_z.T
    blank = np.zeros_like(curved)

    def across(blocks):
        table = in_three(np.concatenate(blocks, axis=1))
        return np.concatenate([table, np.zeros((count * count, table.shape[1]), table.dtype)], axis=0)

    both = np.concatenate(
        [
            across([small_y, curved, small_z, blank]),
            across([curved, small_y, blank, small_z]),
        ],
        axis=1,
    )
    filled = np.zeros((count**3, count**3 - taken.shape[1]))
    stencil = np.concatenate(
        [
            along_first(1.0),
            along_first(-1.0),
            both,
            short(placed),
            short(np.concatenate([taken, filled], axis=1)),
        ],
        axis=0,
    )
    wall = in_three(np.concatenate([bottom, none, none, bottom], axis=1))
    return stencil, wall


def dot(left, right):
    return jnp.dot(left, right, preferred_element_type=F32)


def dot_nt(left, right):
    return lax.dot_general(left, right, (((1,), (1,)), ((), ())), preferred_element_type=F32)


def split_two(value):
    high = value.astype(BF16)
    return high, (value - high.astype(F32)).astype(BF16)


def moved(order, value):
    high = value.astype(BF16)
    rest = value - high.astype(F32)
    middle, low = split_two(rest)
    return dot(order, high) + dot(order, middle) + dot(order, low)


def slot_matrix(slots):
    count = slots.shape[1]
    rows = lax.broadcasted_iota(jnp.int32, (count, count), 0)
    return jnp.where(rows == slots, 1.0, 0.0).astype(F32)


def layer_rows(value, layer, ez):
    step = EY * ez
    start = layer * ez
    return value[start : start + ez], value[step + start : step + start + ez]


def edge_tables():
    side = NP * NP
    point = lax.broadcasted_iota(jnp.int32, (NP * side, 2 * side), 0)
    lane = lax.broadcasted_iota(jnp.int32, (NP * side, 2 * side), 1)
    middle = lax.rem(lax.div(point, NP), NP)
    place = lax.div(point, side) * NP + lax.rem(point, NP)

    def table(level, shift):
        return jnp.where((middle == level) & (lane == place + shift), 1.0, 0.0).astype(BF16)

    return table(0, 0), table(0, side), table(NP - 1, 0), table(NP - 1, side)


def is_even(axis):
    return lax.rem(lax.axis_index(axis), 2) == 0


def write_edges(fields, tabs, outs, ez):
    lf, ls, tf, ts = tabs
    pair_x, cross_x, pair_y, cross_y = outs
    side = NP * NP
    half = EY * ez // 2
    last = NP * side - side
    even_x = is_even("sim")
    even_y = is_even("grp")
    for c, field in enumerate(fields):
        near = field[0 : 2 * half, 0:side]
        far = field[2 * half : 4 * half, last : last + side]
        to_left = jnp.concatenate([near[:half], near[half:]], axis=1)
        to_right = jnp.concatenate([far[:half], far[half:]], axis=1)
        pair_x[c] = jnp.where(even_x, to_right, to_left).astype(BF16)
        cross_x[c] = jnp.where(even_x, to_left, to_right).astype(BF16)
        one, two = layer_rows(field, 0, ez)
        to_below = dot(one.astype(BF16), lf) + dot(two.astype(BF16), ls)
        one, two = layer_rows(field, EY - 1, ez)
        to_above = dot(one.astype(BF16), tf) + dot(two.astype(BF16), ts)
        pair_y[c] = jnp.where(even_y, to_above, to_below).astype(BF16)
        cross_y[c] = jnp.where(even_y, to_below, to_above).astype(BF16)


def add_edges(part, c, pair_x, cross_x, pair_y, cross_y, tabs, ez):
    lf, ls, tf, ts = tabs
    side = NP * NP
    half = EY * ez // 2
    width = NP * side
    value = part[c]
    even_x = is_even("sim")
    even_y = is_even("grp")
    pair = FACE_RATE * pair_x[c].astype(F32)
    cross = FACE_RATE * cross_x[c].astype(F32)
    left = jnp.where(even_x, cross, pair)
    right = jnp.where(even_x, pair, cross)
    pair = pair_y[c].astype(F32)
    cross = cross_y[c].astype(F32)
    below = jnp.where(even_y, cross, pair).astype(BF16)
    above = jnp.where(even_y, pair, cross).astype(BF16)
    rest = jnp.zeros((half, width - side), F32)
    x_add = jnp.concatenate(
        [
            jnp.concatenate([left[:, :side], rest], axis=1),
            jnp.concatenate([left[:, side:], rest], axis=1),
            jnp.concatenate([rest, right[:, :side]], axis=1),
            jnp.concatenate([rest, right[:, side:]], axis=1),
        ],
        axis=0,
    )
    none = jnp.zeros(((EY - 2) * ez, width), F32)
    y_add = jnp.concatenate(
        [
            dot_nt(below, lf),
            none,
            dot_nt(above, tf),
            dot_nt(below, ls),
            none,
            dot_nt(above, ts),
        ],
        axis=0,
    )
    return value + x_add + FACE_RATE * y_add


def prepare_kernel(vel, slots, field, *edges):
    ez = vel.shape[1] // (EX * EY)
    order = slot_matrix(slots[...]).T.astype(BF16)
    fields = [moved(order, vel[c]) for c in range(3)]
    for c in range(3):
        field[c] = fields[c]
    write_edges(fields, edge_tables(), edges, ez)


def face_count(width):
    point = lax.broadcasted_iota(jnp.int32, (1, width), 1)
    count = jnp.zeros((1, width), F32)
    for stride in (NP * NP, NP, 1):
        index = lax.rem(lax.div(point, stride), NP)
        count = count + jnp.where((index == 0) | (index == NP - 1), 1.0, 0.0)
    return count


def inside_kernel(field, stencil, part):
    rows = field.shape[1]
    width = field.shape[2]
    ez = rows // (EX * EY)
    half = width // 2
    side = NP * NP
    pair = 2 * side
    tiles = width // pair
    even = stencil.at[0 : 3 * half]
    odd = stencil.at[3 * half : 6 * half]
    start = 6 * half
    across = stencil.at[start : start + 4 * side]
    placed = stencil.at[start + 4 * side : start + 8 * side]
    taken = stencil.at[start + 8 * side : start + 8 * side + width]
    keep = 1.0 - FACE_RATE * face_count(width)
    lanes = lax.broadcasted_iota(jnp.int32, (1, pair), 1)
    first = lanes < side
    tile = [field[:, :, j * pair : (j + 1) * pair].reshape(3 * rows, pair) for j in range(tiles)]
    swap = [pltpu.roll(value, side, 1) for value in tile]

    high = [value.astype(BF16).astype(F32) for value in tile]
    high_swap = [value.astype(BF16).astype(F32) for value in swap]

    faces = dot(jnp.concatenate(high, axis=1).astype(BF16), taken[:, : 4 * side])
    in_y = faces[:, :pair].reshape(3 * EX, EY, ez, pair)
    wall = jnp.zeros((3 * EX, 1, ez, pair), F32)
    beside_y = jnp.where(
        first,
        jnp.concatenate([wall, in_y[:, :-1]], axis=1),
        jnp.concatenate([in_y[:, 1:], wall], axis=1),
    ).reshape(3 * rows, pair)
    in_z = faces[:, pair:].reshape(3 * EX * EY, ez, pair)
    beside_z = jnp.where(
        first, pltpu.roll(in_z, 1, 1), pltpu.roll(in_z, ez - 1, 1)
    ).reshape(3 * rows, pair)
    beside = jnp.concatenate([beside_y, beside_z], axis=1).astype(BF16)

    def three(value):
        top, rest = split_two(value)
        return jnp.concatenate([top, rest, top], axis=1)

    mirror = jnp.concatenate([swap[tiles - 1 - j] for j in range(tiles // 2)], axis=1)
    near = jnp.concatenate(tile[: tiles // 2], axis=1)
    from_even = dot(three(near + mirror), even[...])
    from_odd = dot(three(near - mirror), odd[...])

    for j in range(tiles):
        cols = slice(j * pair, (j + 1) * pair)
        low = tile[j] - high[j]
        low_swap = swap[j] - high_swap[j]
        one = jnp.concatenate([jnp.where(first, high[j], low_swap), high[j]], axis=1).astype(BF16)
        two = jnp.concatenate([jnp.where(first, high_swap[j], low), high_swap[j]], axis=1).astype(BF16)
        got_one = dot(one, across[:, : 4 * side])
        got_two = dot(two, across[:, 4 * side :])
        slope_y = jnp.where(first, got_one[:, :pair], got_two[:, :pair])
        slope_z = got_one[:, pair:] + got_two[:, pair:]
        curve = jnp.where(first, got_two[:, :pair], got_one[:, :pair])
        if j < tiles // 2:
            at = slice(j * pair, (j + 1) * pair)
            up = slice(half + j * pair, half + (j + 1) * pair)
            slope_x = from_odd[:, at] + from_even[:, at]
            curve = pltpu.roll(curve, side, 1) + (from_even[:, up] + from_odd[:, up])
        else:
            k = tiles - 1 - j
            at = slice(k * pair, (k + 1) * pair)
            up = slice(half + k * pair, half + (k + 1) * pair)
            slope_x = pltpu.roll(from_odd[:, at] - from_even[:, at], side, 1)
            curve = pltpu.roll(curve + (from_even[:, up] - from_odd[:, up]), side, 1)
        value = tile[j] * keep[:, cols] + curve
        value = value + FACE_RATE * dot(beside, placed[:, cols])
        value = value.reshape(3, rows, pair)
        for d, slope in enumerate((slope_x, slope_y, slope_z)):
            value = value + slope.reshape(3, rows, pair) * tile[j].reshape(3, rows, pair)[d][None]
        layer = EY * ez
        if j == 0:
            beyond = swap[tiles - 1].reshape(3, rows, pair)[:, :layer]
            beyond = jnp.where(first, FACE_RATE * beyond, 0.0)
            value = jnp.concatenate([value[:, :layer], value[:, layer:] + beyond], axis=1)
        if j == tiles - 1:
            beyond = swap[0].reshape(3, rows, pair)[:, layer:]
            beyond = jnp.where(first, 0.0, FACE_RATE * beyond)
            value = jnp.concatenate([value[:, :layer] + beyond, value[:, layer:]], axis=1)
        part[:, :, cols] = value


def join_kernel(part, pair_x, cross_x, pair_y, cross_y, field, *edges):
    ez = part.shape[1] // (EX * EY)
    tabs = edge_tables()
    fields = [add_edges(part, c, pair_x, cross_x, pair_y, cross_y, tabs, ez) for c in range(3)]
    for c in range(3):
        field[c] = fields[c]
    write_edges(fields, tabs, edges, ez)


def encode_kernel(
    part, pair_x, cross_x, pair_y, cross_y, wall, w_encode,
    field, snapshot, target, z1, h1,
):
    ez = part.shape[1] // (EX * EY)
    tabs = edge_tables()
    fields = [add_edges(part, c, pair_x, cross_x, pair_y, cross_y, tabs, ez) for c in range(3)]
    for c in range(3):
        field[c] = fields[c]
    high0, low0 = split_two(fields[0])
    high2, low2 = split_two(fields[2])
    snap = jnp.concatenate([high0, high2], axis=1)
    snapshot[...] = snap
    target[...] = (
        dot(jnp.concatenate([high0, low0, high0], axis=1), wall[:, : 2 * NP * NP])
        + dot(jnp.concatenate([high2, low2, high2], axis=1), wall[:, 2 * NP * NP :])
    ).astype(BF16)
    hidden = dot(snap, w_encode[...])
    z1[...] = hidden
    h1[...] = (hidden * jax.nn.sigmoid(hidden)).astype(BF16)


def restore_kernel(field, slots, after_this, out):
    order = slot_matrix(slots[...]).astype(BF16)
    for c in range(3):
        out[c] = moved(order, field[c])


def silu_grad(value):
    sigma = jax.nn.sigmoid(value)
    return sigma * (1.0 + value * (1.0 - sigma))


def with_layers(own, pair, cross, ez, groups):
    channels = own.shape[-1]
    place = lax.axis_index("grp")
    grid = own[...].astype(F32).reshape(EX, EY, ez, channels)
    even = is_even("grp")
    pair = pair[...].reshape(EX, EY, ez, channels).astype(F32)
    cross = cross[...].reshape(EX, EY, ez, channels).astype(F32)
    before = jnp.where(even, cross[:, EY - 1 :], pair[:, EY - 1 :])
    after = jnp.where(even, pair[:, :1], cross[:, :1])
    before = jnp.where(place > 0, before, 0.0)
    after = jnp.where(place < groups - 1, after, 0.0)
    return jnp.concatenate([before, grid, after], axis=1)


def along_span(grid, ez, groups):
    shape = grid.shape
    rows = int(np.prod(shape[:-1]))
    crop = ez // groups
    flat = grid.reshape(rows, shape[-1])
    place = lax.rem(lax.broadcasted_iota(jnp.int32, (rows, 1), 0), crop)
    before = jnp.where(place == 0, 0.0, pltpu.roll(flat, 1, 0))
    after = jnp.where(place == crop - 1, 0.0, pltpu.roll(flat, rows - 1, 0))
    return before.reshape(shape), after.reshape(shape)


def forward_kernel(groups, total, h1, pair, cross, w_conv, w_head, target, dz2, h2, resid, padded, z2):
    rows, channels = h1.shape
    ez = rows // (EX * EY)
    grid = with_layers(h1, pair, cross, ez, groups)
    before, after = along_span(grid, ez, groups)
    padded[...] = jnp.concatenate([before, grid, after], axis=-1).astype(BF16)
    half = rows // 2
    for dy in range(3):
        taken = padded[:, dy : dy + EY].reshape(EX, half, 3 * channels)
        first = 3 * dy
        both = dot(taken.reshape(rows, 3 * channels), w_conv[9 + first : 12 + first].reshape(-1, channels))
        ahead_x = dot(taken[1], w_conv[18 + first : 21 + first].reshape(-1, channels))
        behind_x = dot(taken[0], w_conv[first : 3 + first].reshape(-1, channels))
        step = both + jnp.concatenate([ahead_x, behind_x], axis=0)
        if dy == 0:
            z2[...] = step
        else:
            z2[...] += step
    hidden = z2[...]
    act = (hidden * jax.nn.sigmoid(hidden)).astype(BF16)
    output = dot(act, w_head[...])
    miss = (LOSS_WEIGHT * (output - target[...].astype(F32)) / total).astype(BF16)
    h2[...] = act
    resid[...] = miss
    dz2[...] = (dot_nt(miss, w_head[...]) * silu_grad(hidden)).astype(BF16)


def back_kernel(
    groups, dz2, pair, cross, w_conv, z1, snapshot, h2, resid,
    kept, sent, dh1, out,
):
    rows, channels = dz2.shape
    ez = rows // (EX * EY)
    half = rows // 2
    grid = with_layers(dz2, pair, cross, ez, groups)
    before, after = along_span(grid, ez, groups)
    shifted = [part.astype(BF16) for part in (after, grid, before)]
    features = snapshot.shape[1]
    out[:, features:] = dot(h2[...].astype(F32).T.astype(BF16), resid[...])
    for dy in range(3):
        for dz in range(3):
            tap = 3 * dy + dz
            taken = shifted[dz][:, 2 - dy : 2 - dy + EY].reshape(EX, half, channels)
            both = dot_nt(taken.reshape(rows, channels), w_conv[9 + tap])
            ahead_x = dot_nt(taken[0], w_conv[18 + tap])
            behind_x = dot_nt(taken[1], w_conv[tap])
            step = both + jnp.concatenate([behind_x, ahead_x], axis=0)
            if tap == 0:
                dh1[...] = step
            else:
                dh1[...] += step
    dz1 = dh1[...] * silu_grad(z1[...])
    out[:, :features] = dot(dz1.T.astype(BF16), snapshot[...])
    quarter = channels // groups
    place = lax.axis_index("grp")
    for k in range(groups):
        piece = sent if k % 2 else kept
        at = pl.multiple_of(jnp.bitwise_xor(place, k) * quarter, quarter)
        piece[k // 2] = out[pl.ds(at, quarter)].astype(piece.dtype)


def core_kernel(kept, got, out_kept, out_sent):
    out_kept[...] = kept[0] + got[0].astype(F32)
    out_sent[...] = (kept[1] + got[1].astype(F32)).astype(BF16)


def taps_kernel(
    groups, sims, h_own, h_one, h_two, h_three, d_own, d_one, d_two, d_three, after_this, *refs
):
    out, h_all, r_all = refs[-3:]
    rows, channels = h_own.shape
    ez = rows // (EX * EY)
    quarter = channels // groups
    crop = ez // groups
    place = lax.axis_index("grp")
    layer = EY * ez
    lane = lax.broadcasted_iota(jnp.int32, (channels, channels), 1)
    channel = lax.broadcasted_iota(jnp.int32, (channels, channels), 0)
    chosen = jnp.where(
        (channel == place * quarter + lax.rem(lane, quarter)) & (lane < 3 * quarter), 1.0, 0.0
    ).astype(BF16)
    pairs = ((h_own, d_own), (h_one, d_one), (h_two, d_two), (h_three, d_three))
    for k, (h, d) in enumerate(pairs):
        at = jnp.bitwise_xor(place, k)
        mine = dot(d[...], chosen)
        for x in range(EX):
            h_all[x, at] = h[x * layer : (x + 1) * layer]
            r_all[x, at] = mine[x * layer : (x + 1) * layer]
    deep = groups * layer
    flat = r_all[...].reshape(EX * deep, channels)
    spot = lax.rem(lax.broadcasted_iota(jnp.int32, (EX * deep, 1), 0), crop)
    lane = lax.broadcasted_iota(jnp.int32, (1, channels), 1)
    after = jnp.where(spot == crop - 1, 0.0, pltpu.roll(flat, EX * deep - 1, 0))
    before = jnp.where(spot == 0, 0.0, pltpu.roll(flat, 1, 0))
    mixed = jnp.where(lane < quarter, after, jnp.where(lane < 2 * quarter, flat, before))
    turned = mixed.T
    spot = lax.rem(lax.broadcasted_iota(jnp.int32, (1, EX * deep), 1), deep)
    up = jnp.where(spot >= deep - ez, 0.0, pltpu.roll(turned, EX * deep - ez, 1))
    down = jnp.where(spot < ez, 0.0, pltpu.roll(turned, ez, 1))
    whole = h_all[...].reshape(EX * deep, channels)
    for dy, side in enumerate((up, turned, down)):
        side = side.astype(BF16)
        for dx in range(3):
            if dx == 0:
                got = dot(side[:, deep:], whole[:deep])
            elif dx == 1:
                got = dot(side, whole)
            else:
                got = dot(side[:, :deep], whole[deep:])
            start = (9 * dx + 3 * dy) * quarter
            out[start : start + 3 * quarter] = got[: 3 * quarter]
    me = lax.rem(lax.axis_index("sim"), sims)
    piece_rows = 27 * quarter // sims
    for k, piece in enumerate(refs[:-3]):
        at = pl.multiple_of(jnp.bitwise_xor(me, k) * piece_rows, 8)
        piece[...] = out[pl.ds(at, piece_rows)].astype(piece.dtype)


def dense_kernel(kept, got, *refs):
    out_kept, out_sent = refs[-5:-3]
    for source, target in zip(refs[:3], refs[-3:]):
        target[...] = source[...]
    total = kept[...] + got[...].astype(F32)
    grid = total.reshape(2, 2, kept.shape[0] // 4, kept.shape[1])
    odd = lax.rem(lax.div(lax.axis_index("sim"), 2), 2) == 1
    out_kept[...] = jnp.where(odd, grid[:, 1], grid[:, 0])
    out_sent[...] = jnp.where(odd, grid[:, 0], grid[:, 1]).astype(BF16)


def half_kernel(scale, kept, got, out_kept, out_sent):
    total = kept[...] + got[...].astype(F32)
    upper = lax.rem(lax.div(lax.axis_index("sim"), scale), 2) == 1
    out_kept[...] = jnp.where(upper, total[1], total[0])
    out_sent[...] = jnp.where(upper, total[0], total[1]).astype(BF16)


def packed(taps, dense):
    channels = taps.shape[1]
    parts = [taps]
    for start in range(0, dense.shape[1], channels):
        piece = dense[:, start : start + channels]
        short_by = channels - piece.shape[1]
        if short_by:
            piece = jnp.concatenate([piece, jnp.zeros((piece.shape[0], short_by), F32)], axis=1)
        parts.append(piece)
    return jnp.concatenate(parts, axis=0)


def sum_kernel(parts, kept, *refs):
    total = kept[...]
    for other in refs[: parts - 1]:
        total = total + other[...].astype(F32)
    refs[-1][...] = total.astype(BF16)


def share_kernel(taps, one, two, three, dense, dense_in, out):
    total = taps[...]
    for other in (one, two, three):
        total = total + other[...].astype(F32)
    out[...] = packed(total, dense[...] + dense_in[...].astype(F32)).astype(BF16)


def spread_kernel(features, own, *refs):
    count = len(refs) - 3 + 1
    shares = (own,) + refs[:-3]
    taps, encode, head = refs[-3:]
    channels = own.shape[1]
    tap_rows = taps.shape[0] // count
    own_rows = encode.shape[0] // count
    me = lax.axis_index("sim")
    for k, share in enumerate(shares):
        source = jnp.bitwise_xor(me, k)
        value = share[...].astype(F32)
        taps[pl.ds(pl.multiple_of(source * tap_rows, 8), tap_rows)] = value[:tap_rows]
        rows = pl.ds(pl.multiple_of(source * own_rows, 8), own_rows)
        start = tap_rows
        for first in range(0, features, channels):
            encode[rows, first : first + channels] = value[start : start + own_rows]
            start += own_rows
        head[rows] = value[start : start + own_rows, : head.shape[1]]


def call(kernel, outs, scratch=(), in_hbm=(), inputs=0, flops=1000):
    specs = {}
    if in_hbm:
        specs["in_specs"] = [
            pl.BlockSpec(memory_space=pl.ANY if i in in_hbm else pltpu.VMEM) for i in range(inputs)
        ]
    return pl.pallas_call(
        kernel,
        out_shape=outs,
        scratch_shapes=list(scratch),
        compiler_params=pltpu.CompilerParams(vmem_limit_bytes=VMEM_LIMIT),
        cost_estimate=pl.CostEstimate(flops=flops, bytes_accessed=1000, transcendentals=0),
        **specs,
    )


def shaped(shape, kind):
    return jax.ShapeDtypeStruct(shape, kind)


def swapped(value, axis, mask):
    count = lax.axis_size(axis)
    return lax.ppermute(value, axis, [(i, i ^ mask) for i in range(count)])


def crossed(value, axis, periodic):
    count = lax.axis_size(axis)
    route = [(i, i + 1 if i % 2 else i - 1) for i in range(count)]
    if periodic:
        route = [(i, j % count) for i, j in route]
    return lax.ppermute(value, axis, [(i, j) for i, j in route if 0 <= j < count])


def exchanged(edges):
    pair_x, cross_x, pair_y, cross_y = edges
    cross_x = crossed(cross_x, "sim", True)
    pair_x = swapped(pair_x, "sim", 1)
    cross_y = crossed(cross_y, "grp", False)
    pair_y = swapped(pair_y, "grp", 1)
    return pair_x, cross_x, pair_y, cross_y


def gathered(share, sims):
    got = {0: share}
    for k in sorted(range(2, sims, 2), reverse=True):
        got[k] = swapped(share, "sim", k)
    for k in range(0, sims, 2):
        got[k + 1] = swapped(got[k], "sim", 1)
    return [got[k] for k in range(sims)]


def body(velocity, slot_of, w_encode, w_conv, w_head):
    stencil, wall = (jnp.asarray(table) for table in element_tables())
    block = velocity[0, 0]
    slots = slot_of[0]
    rows, width = block.shape[1:]
    ez = rows // (EX * EY)
    channels = w_encode.shape[1]
    features = w_encode.shape[0]
    outputs = w_head.shape[1]
    sims = lax.axis_size("sim")
    groups = lax.axis_size("grp")
    total = rows * sims * groups
    quarter = channels // groups

    whole = shaped((3, rows, width), F32)
    x_edge = shaped((3, EY * ez // 2, 2 * NP * NP), BF16)
    y_edge = shaped((3, ez, 2 * NP * NP), BF16)
    edge_shapes = (x_edge, x_edge, y_edge, y_edge)

    field, *edges = call(prepare_kernel, (whole,) + edge_shapes, flops=4 * 10**9)(block, slots)
    halos = exchanged(edges)
    part = call(inside_kernel, whole)(field, stencil)
    field, *edges = call(join_kernel, (whole,) + edge_shapes)(part, *halos)
    halos = exchanged(edges)
    part = call(inside_kernel, whole)(field, stencil)
    field, snapshot, target, z1, h1 = call(
        encode_kernel,
        (
            whole,
            shaped((rows, features), BF16),
            shaped((rows, outputs), BF16),
            shaped((rows, channels), F32),
            shaped((rows, channels), BF16),
        ),
    )(part, *halos, wall, w_encode)

    h_three = swapped(h1, "grp", 3)
    h_one = swapped(h1, "grp", 1)
    h_two = swapped(h_three, "grp", 1)
    rows_bf = shaped((rows, channels), BF16)
    dz2, h2, resid = call(
        functools.partial(forward_kernel, groups, total),
        (rows_bf, rows_bf, shaped((rows, outputs), BF16)),
        (
            pltpu.VMEM((EX, EY + 2, ez, 3 * channels), BF16),
            pltpu.VMEM((rows, channels), F32),
        ),
    )(h1, h_one, h_three, w_conv, w_head, target)

    d_three = swapped(dz2, "grp", 3)
    d_one = swapped(dz2, "grp", 1)
    d_two = swapped(d_three, "grp", 1)
    wide = features + outputs
    pair = (groups // 2, quarter, wide)
    e_kept, e_sent = call(
        functools.partial(back_kernel, groups),
        (shaped(pair, F32), shaped(pair, BF16)),
        (pltpu.VMEM((rows, channels), F32), pltpu.VMEM((channels, wide), F32)),
    )(dz2, d_one, d_three, w_conv, z1, snapshot, h2, resid)
    e_got = swapped(e_sent, "grp", 1)
    e_kept, e_sent = call(core_kernel, (shaped(pair[1:], F32), shaped(pair[1:], BF16)))(e_kept, e_got)
    e_got = swapped(e_sent, "grp", 2)
    tap_rows = 27 * quarter // sims
    own_rows = quarter // sims
    direct = sims == 8
    if direct:
        pieces = [shaped((tap_rows, channels), BF16 if k % 2 else F32) for k in range(sims)]
    else:
        pieces = [shaped((27 * quarter, channels), BF16)]
    taps = call(
        functools.partial(taps_kernel, groups, sims if direct else 1),
        tuple(pieces),
        (
            pltpu.VMEM((27 * quarter, channels), F32),
            pltpu.VMEM((EX, groups, EY * ez, channels), BF16),
            pltpu.VMEM((EX, groups, EY * ez, channels), F32),
        ),
        in_hbm=(8,),
        inputs=9,
    )(h1, h_one, h_two, h_three, dz2, d_one, d_two, d_three, e_kept)
    if direct:
        tap_piece = shaped((tap_rows, channels), BF16)
        part = (2, 2 * own_rows, wide)
        e_kept, e_sent, *later = call(
            dense_kernel, (shaped(part, F32), shaped(part, BF16)) + (tap_piece,) * 3
        )(e_kept, e_got, taps[5], taps[3], taps[1])
        e_got = swapped(e_sent, "sim", 2)
        taps_in = {6: swapped(taps[7], "sim", 1)}
        taps_in.update((k, swapped(piece, "sim", 1)) for k, piece in zip((4, 2, 0), later))
        add_two = call(functools.partial(sum_kernel, 2), tap_piece)
        add_three = call(functools.partial(sum_kernel, 3), tap_piece)
        six = swapped(add_two(taps[6], taps_in[6], e_sent), "sim", 2)
        two = swapped(add_two(taps[2], taps_in[2]), "sim", 2)
        part = shaped((2 * own_rows, wide), F32), shaped((2 * own_rows, wide), BF16)
        e_kept, e_sent = call(functools.partial(half_kernel, 4), part)(e_kept, e_got)
        e_got = swapped(e_sent, "sim", 4)
        four = swapped(add_three(taps[4], taps_in[4], six, e_sent), "sim", 4)
        part = shaped((own_rows, wide), F32), shaped((own_rows, wide), BF16)
        e_kept, e_sent = call(functools.partial(half_kernel, 1), part, flops=4 * 10**9)(
            e_kept.reshape(2, own_rows, wide), e_got.reshape(2, own_rows, wide)
        )
        e_got = swapped(e_sent, "sim", 1)
        blocks = -(-wide // channels)
        share = call(share_kernel, shaped((tap_rows + blocks * own_rows, channels), BF16))(
            taps[0], taps_in[0], two, four, e_kept, e_got
        )
        shares = gathered(share, sims)
        velocity_next = call(restore_kernel, whole, in_hbm=(2,), inputs=3)(field, slots, shares[1])
        taps, encode, head = call(
            functools.partial(spread_kernel, features),
            (
                shaped((27 * quarter, channels), F32),
                shaped((quarter, features), F32),
                shaped((quarter, outputs), F32),
            ),
        )(*shares)
    else:
        taps = taps[0].reshape(sims, tap_rows, channels)
        taps = lax.all_to_all(taps, "sim", 0, 0, tiled=True)
        taps = jnp.sum(taps.astype(F32), axis=0).astype(BF16)
        taps = lax.all_gather(taps, "sim").astype(F32)
        velocity_next = call(restore_kernel, whole, in_hbm=(2,), inputs=3)(field, slots, e_kept)
        dense = e_kept + e_got.astype(F32)
        dense = dense.astype(BF16).reshape(sims, own_rows, wide)
        dense = lax.all_to_all(dense, "sim", 0, 0, tiled=True)
        dense = jnp.sum(dense.astype(F32), axis=0).astype(BF16)
        dense = lax.all_gather(dense, "sim").reshape(quarter, wide).astype(F32)
        encode = dense[:, :features]
        head = dense[:, features:]
    taps = taps.reshape(27, quarter, channels)
    return velocity_next[None, None], encode.T, taps.transpose(0, 2, 1), head


def solution(mesh):
    placed = (P("sim", "grp", None, None, None), P("sim", "grp", None), P(), P(), P())
    return jax.shard_map(
        body,
        mesh=mesh,
        in_specs=placed,
        out_specs=(
            P("sim", "grp", None, None, None),
            P(None, "grp"),
            P(None, None, "grp"),
            P("grp", None),
        ),
        check_vma=False,
    )
```

```python
import functools

import jax
import jax.numpy as jnp
import ml_dtypes
import numpy as np
from jax import lax
from jax.experimental import pallas as pl
from jax.experimental.pallas import tpu as pltpu
from jax.sharding import PartitionSpec as P

NP = 8
EX = 2
EY = 4
STEPS = 2

VISCOSITY = 0.2
TIME_STEP = 0.005
PENALTY = 100.0
LOSS_WEIGHT = 64.0
FACE_RATE = TIME_STEP * VISCOSITY * PENALTY

F32 = jnp.float32
BF16 = jnp.bfloat16
VMEM_LIMIT = 16 * 1024 * 1024


def derivative_matrix(count):
    places = np.arange(count)
    points = -np.cos(np.pi * places / (count - 1))
    weights = np.where(places % 2 == 0, 1.0, -1.0)
    weights[0] = weights[0] * 0.5
    weights[count - 1] = weights[count - 1] * 0.5
    identity = np.eye(count)
    spread = points[:, None] - points[None, :] + identity
    deriv = weights[None, :] / weights[:, None] / spread
    deriv = deriv * (1.0 - identity)
    return deriv - identity * deriv.sum(axis=1)[:, None]


def short(table):
    return np.asarray(table, np.float32).astype(ml_dtypes.bfloat16)


def in_three(table):
    table = np.asarray(table, np.float32)
    high = table.astype(ml_dtypes.bfloat16)
    low = (table - high.astype(np.float32)).astype(ml_dtypes.bfloat16)
    return np.concatenate([high, high, low], axis=0)


@functools.lru_cache(maxsize=None)
def element_tables():
    count = NP
    deriv = derivative_matrix(count)
    single = np.eye(count)
    square = np.eye(count * count)
    grid = np.arange(count**3).reshape(count, count, count)
    final = count - 1
    faces = [
        grid[0].ravel(),
        grid[final].ravel(),
        grid[:, 0].ravel(),
        grid[:, final].ravel(),
        grid[:, :, 0].ravel(),
        grid[:, :, final].ravel(),
    ]

    def pick(which):
        table = np.zeros((count**3, count * count))
        table[which, np.arange(count * count)] = 1.0
        return table

    picks = [pick(which) for which in faces]
    none = np.zeros_like(picks[0])
    taken = np.concatenate([picks[i] for i in (3, 2, 5, 4)], axis=1)
    placed = np.concatenate(picks[2:], axis=1).T
    bottom = np.zeros((count**3, count * count))
    for first in range(count):
        for middle in range(count):
            for inner in range(count):
                bottom[grid[first, middle, inner], first * count + inner] = (
                    VISCOSITY * deriv[0, middle]
                )
    mirrored = np.concatenate([deriv, deriv @ deriv], axis=0)[:, ::-1].reshape(2, count, count)
    straight = np.stack([deriv, deriv @ deriv])
    half = count // 2
    scale = np.array([-TIME_STEP, TIME_STEP * VISCOSITY])[:, None, None]

    def along_first(sign):
        mixed = (0.5 * scale * (straight + sign * mirrored))[:, :half, :half]
        return in_three(np.concatenate([np.kron(part.T, square) for part in mixed], axis=1))

    small_y = np.kron(deriv, single)
    small_z = np.kron(single, deriv)
    curved = TIME_STEP * VISCOSITY * (small_y @ small_y + small_z @ small_z).T
    small_y = -TIME_STEP * small_y.T
    small_z = -TIME_STEP * small_z.T
    blank = np.zeros_like(curved)

    def across(blocks):
        table = in_three(np.concatenate(blocks, axis=1))
        return np.concatenate([table, np.zeros((count * count, table.shape[1]), table.dtype)], axis=0)

    both = np.concatenate(
        [
            across([small_y, curved, small_z, blank]),
            across([curved, small_y, blank, small_z]),
        ],
        axis=1,
    )
    filled = np.zeros((count**3, count**3 - taken.shape[1]))
    stencil = np.concatenate(
        [
            along_first(1.0),
            along_first(-1.0),
            both,
            short(placed),
            short(np.concatenate([taken, filled], axis=1)),
        ],
        axis=0,
    )
    wall = in_three(np.concatenate([bottom, none, none, bottom], axis=1))
    return stencil, wall


def dot(left, right):
    return jnp.dot(left, right, preferred_element_type=F32)


def dot_nt(left, right):
    return lax.dot_general(left, right, (((1,), (1,)), ((), ())), preferred_element_type=F32)


def split_two(value):
    high = value.astype(BF16)
    return high, (value - high.astype(F32)).astype(BF16)


def moved(order, value):
    high = value.astype(BF16)
    rest = value - high.astype(F32)
    middle, low = split_two(rest)
    return dot(order, high) + dot(order, middle) + dot(order, low)


def slot_matrix(slots):
    count = slots.shape[1]
    rows = lax.broadcasted_iota(jnp.int32, (count, count), 0)
    return jnp.where(rows == slots, 1.0, 0.0).astype(F32)


def layer_rows(field, x, layer, ez):
    start = (x * EY + layer) * ez
    return field[:, start : start + ez].reshape(3 * ez, field.shape[2])


def edge_tables():
    side = NP * NP
    point = lax.broadcasted_iota(jnp.int32, (NP * side, 2 * side), 0)
    lane = lax.broadcasted_iota(jnp.int32, (NP * side, 2 * side), 1)
    middle = lax.rem(lax.div(point, NP), NP)
    place = lax.div(point, side) * NP + lax.rem(point, NP)

    def table(level, shift):
        return jnp.where((middle == level) & (lane == place + shift), 1.0, 0.0).astype(BF16)

    return table(0, 0), table(0, side), table(NP - 1, 0), table(NP - 1, side)


def order_kernel(slots, order, back, tabs):
    matrix = slot_matrix(slots[...])
    back[...] = matrix.astype(BF16)
    order[...] = matrix.T.astype(BF16)
    for i, table in enumerate(edge_tables()):
        tabs[i] = table


def is_even(axis):
    return lax.rem(lax.axis_index(axis), 2) == 0


def write_edges(field, tabs, outs, ez):
    pair_x, cross_x, pair_y, cross_y = outs
    side = NP * NP
    half = EY * ez // 2
    last = NP * side - side
    even_x = is_even("sim")
    even_y = is_even("grp")
    near = field[:, 0 : 2 * half, 0 : 2 * side][:, :, :side]
    far = field[:, 2 * half : 4 * half, last - side :][:, :, side:]
    to_left = jnp.concatenate([near[:, :half], near[:, half:]], axis=2)
    to_right = jnp.concatenate([far[:, :half], far[:, half:]], axis=2)
    pair_x[...] = jnp.where(even_x, to_right, to_left).astype(BF16)
    cross_x[...] = jnp.where(even_x, to_left, to_right).astype(BF16)
    to_below, to_above = [
        dot(layer_rows(field, 0, layer, ez).astype(BF16), tabs[at])
        + dot(layer_rows(field, 1, layer, ez).astype(BF16), tabs[at + 1])
        for layer, at in ((0, 0), (EY - 1, 2))
    ]
    pair_y[...] = jnp.where(even_y, to_above, to_below).astype(BF16).reshape(pair_y.shape)
    cross_y[...] = jnp.where(even_y, to_below, to_above).astype(BF16).reshape(cross_y.shape)


def add_edges(part, pair_x, cross_x, pair_y, cross_y, tabs, field, ez):
    side = NP * NP
    half = EY * ez // 2
    width = NP * side
    even_x = is_even("sim")
    even_y = is_even("grp")
    pair = FACE_RATE * pair_x[...].astype(F32)
    cross = FACE_RATE * cross_x[...].astype(F32)
    left = jnp.where(even_x, cross, pair)
    right = jnp.where(even_x, pair, cross)
    pair = pair_y[...].astype(F32)
    cross = cross_y[...].astype(F32)
    below = jnp.where(even_y, cross, pair).astype(BF16).reshape(3 * ez, 2 * side)
    above = jnp.where(even_y, pair, cross).astype(BF16).reshape(3 * ez, 2 * side)
    first = lax.broadcasted_iota(jnp.int32, (1, 1, 2 * side), 2) < side

    field[...] = part[...]
    turned = pltpu.roll(left, side, 2)
    field[:, 0:half, : 2 * side] += jnp.where(first, left, 0.0)
    field[:, half : 2 * half, : 2 * side] += jnp.where(first, turned, 0.0)
    turned = pltpu.roll(right, side, 2)
    field[:, 2 * half : 3 * half, width - 2 * side :] += jnp.where(first, 0.0, turned)
    field[:, 3 * half : 4 * half, width - 2 * side :] += jnp.where(first, 0.0, right)
    for x in range(EX):
        for layer, value, at in ((0, below, 0), (EY - 1, above, 2)):
            start = (x * EY + layer) * ez
            more = FACE_RATE * dot_nt(value, tabs[at + x])
            field[:, start : start + ez] += more.reshape(3, ez, width)


def prepare_kernel(vel, order, tabs, field, *edges):
    ez = vel.shape[1] // (EX * EY)
    for c in range(3):
        field[c] = moved(order[...], vel[c])
    write_edges(field, tabs, edges, ez)


def face_count(width):
    point = lax.broadcasted_iota(jnp.int32, (1, width), 1)
    count = jnp.zeros((1, width), F32)
    for stride in (NP * NP, NP, 1):
        index = lax.rem(lax.div(point, stride), NP)
        count = count + jnp.where((index == 0) | (index == NP - 1), 1.0, 0.0)
    return count


def inside_kernel(field, stencil, part):
    rows = field.shape[1]
    width = field.shape[2]
    ez = rows // (EX * EY)
    half = width // 2
    side = NP * NP
    pair = 2 * side
    tiles = width // pair
    even = stencil.at[0 : 3 * half]
    odd = stencil.at[3 * half : 6 * half]
    start = 6 * half
    across = stencil.at[start : start + 4 * side]
    placed = stencil.at[start + 4 * side : start + 8 * side]
    taken = stencil.at[start + 8 * side : start + 8 * side + width]
    keep = 1.0 - FACE_RATE * face_count(width)
    lanes = lax.broadcasted_iota(jnp.int32, (1, pair), 1)
    first = lanes < side
    tile = [field[:, :, j * pair : (j + 1) * pair].reshape(3 * rows, pair) for j in range(tiles)]
    swap = [pltpu.roll(value, side, 1) for value in tile]

    high = [value.astype(BF16).astype(F32) for value in tile]
    high_swap = [value.astype(BF16).astype(F32) for value in swap]

    faces = dot(jnp.concatenate(high, axis=1).astype(BF16), taken[:, : 4 * side])
    in_y = faces[:, :pair].reshape(3 * EX, EY, ez, pair)
    wall = jnp.zeros((3 * EX, 1, ez, pair), F32)
    beside_y = jnp.where(
        first,
        jnp.concatenate([wall, in_y[:, :-1]], axis=1),
        jnp.concatenate([in_y[:, 1:], wall], axis=1),
    ).reshape(3 * rows, pair)
    in_z = faces[:, pair:].reshape(3 * EX * EY, ez, pair)
    beside_z = jnp.where(
        first, pltpu.roll(in_z, 1, 1), pltpu.roll(in_z, ez - 1, 1)
    ).reshape(3 * rows, pair)
    beside = jnp.concatenate([beside_y, beside_z], axis=1).astype(BF16)

    def three(value):
        top, rest = split_two(value)
        return jnp.concatenate([top, rest, top], axis=1)

    mirror = jnp.concatenate([swap[tiles - 1 - j] for j in range(tiles // 2)], axis=1)
    near = jnp.concatenate(tile[: tiles // 2], axis=1)
    from_even = dot(three(near + mirror), even[...])
    from_odd = dot(three(near - mirror), odd[...])

    for j in range(tiles):
        cols = slice(j * pair, (j + 1) * pair)
        low = tile[j] - high[j]
        low_swap = swap[j] - high_swap[j]
        one = jnp.concatenate([jnp.where(first, high[j], low_swap), high[j]], axis=1).astype(BF16)
        two = jnp.concatenate([jnp.where(first, high_swap[j], low), high_swap[j]], axis=1).astype(BF16)
        got_one = dot(one, across[:, : 4 * side])
        got_two = dot(two, across[:, 4 * side :])
        slope_y = jnp.where(first, got_one[:, :pair], got_two[:, :pair])
        slope_z = got_one[:, pair:] + got_two[:, pair:]
        curve = jnp.where(first, got_two[:, :pair], got_one[:, :pair])
        if j < tiles // 2:
            at = slice(j * pair, (j + 1) * pair)
            up = slice(half + j * pair, half + (j + 1) * pair)
            slope_x = from_odd[:, at] + from_even[:, at]
            curve = pltpu.roll(curve, side, 1) + (from_even[:, up] + from_odd[:, up])
        else:
            k = tiles - 1 - j
            at = slice(k * pair, (k + 1) * pair)
            up = slice(half + k * pair, half + (k + 1) * pair)
            slope_x = pltpu.roll(from_odd[:, at] - from_even[:, at], side, 1)
            curve = pltpu.roll(curve + (from_even[:, up] - from_odd[:, up]), side, 1)
        value = tile[j] * keep[:, cols] + curve
        value = value + FACE_RATE * dot(beside, placed[:, cols])
        value = value.reshape(3, rows, pair)
        for d, slope in enumerate((slope_x, slope_y, slope_z)):
            value = value + slope.reshape(3, rows, pair) * tile[j].reshape(3, rows, pair)[d][None]
        layer = EY * ez
        if j == 0:
            beyond = swap[tiles - 1].reshape(3, rows, pair)[:, :layer]
            beyond = jnp.where(first, FACE_RATE * beyond, 0.0)
            value = jnp.concatenate([value[:, :layer], value[:, layer:] + beyond], axis=1)
        if j == tiles - 1:
            beyond = swap[0].reshape(3, rows, pair)[:, layer:]
            beyond = jnp.where(first, 0.0, FACE_RATE * beyond)
            value = jnp.concatenate([value[:, :layer] + beyond, value[:, layer:]], axis=1)
        part[:, :, cols] = value


def join_kernel(part, pair_x, cross_x, pair_y, cross_y, tabs, field, *edges):
    ez = part.shape[1] // (EX * EY)
    add_edges(part, pair_x, cross_x, pair_y, cross_y, tabs, field, ez)
    write_edges(field, tabs, edges, ez)


def encode_kernel(
    part, pair_x, cross_x, pair_y, cross_y, tabs, wall, w_encode,
    field, snapshot, target, z1, h1,
):
    ez = part.shape[1] // (EX * EY)
    add_edges(part, pair_x, cross_x, pair_y, cross_y, tabs, field, ez)
    high0, low0 = split_two(field[0])
    high2, low2 = split_two(field[2])
    snap = jnp.concatenate([high0, high2], axis=1)
    snapshot[...] = snap
    target[...] = (
        dot(jnp.concatenate([high0, low0, high0], axis=1), wall[:, : 2 * NP * NP])
        + dot(jnp.concatenate([high2, low2, high2], axis=1), wall[:, 2 * NP * NP :])
    ).astype(BF16)
    hidden = dot(snap, w_encode[...])
    z1[...] = hidden
    h1[...] = (hidden * jax.nn.sigmoid(hidden)).astype(BF16)


def restore_kernel(field, back, after_this, out):
    for c in range(3):
        out[c] = moved(back[...], field[c])


def silu_grad(value):
    sigma = jax.nn.sigmoid(value)
    return sigma * (1.0 + value * (1.0 - sigma))


def with_layers(own, pair, cross, ez, groups):
    channels = own.shape[-1]
    place = lax.axis_index("grp")
    grid = own[...].astype(F32).reshape(EX, EY, ez, channels)
    even = is_even("grp")
    pair = pair[...].reshape(EX, EY, ez, channels).astype(F32)
    cross = cross[...].reshape(EX, EY, ez, channels).astype(F32)
    before = jnp.where(even, cross[:, EY - 1 :], pair[:, EY - 1 :])
    after = jnp.where(even, pair[:, :1], cross[:, :1])
    before = jnp.where(place > 0, before, 0.0)
    after = jnp.where(place < groups - 1, after, 0.0)
    return jnp.concatenate([before, grid, after], axis=1)


def along_span(grid, ez, groups):
    shape = grid.shape
    rows = int(np.prod(shape[:-1]))
    crop = ez // groups
    flat = grid.reshape(rows, shape[-1])
    place = lax.rem(lax.broadcasted_iota(jnp.int32, (rows, 1), 0), crop)
    before = jnp.where(place == 0, 0.0, pltpu.roll(flat, 1, 0))
    after = jnp.where(place == crop - 1, 0.0, pltpu.roll(flat, rows - 1, 0))
    return before.reshape(shape), after.reshape(shape)


def tap_sum(taken, w_conv, dy):
    channels = w_conv.shape[1]
    first = 3 * dy
    rows = taken.shape[1]

    def times(value, start):
        return dot(value, w_conv[start + first : start + first + 3].reshape(-1, channels))

    both = times(taken.reshape(EX * rows, taken.shape[2]), 9)
    return both + jnp.concatenate([times(taken[1], 18), times(taken[0], 0)], axis=0)


def centre_kernel(groups, h1, w_conv, z2):
    rows, channels = h1.shape
    ez = rows // (EX * EY)
    grid = h1[...].astype(F32).reshape(EX, EY, ez, channels)
    before, after = along_span(grid, ez, groups)
    taken = jnp.concatenate([before, grid, after], axis=-1).astype(BF16)
    z2[...] = tap_sum(taken.reshape(EX, rows // EX, 3 * channels), w_conv, 1)


def forward_kernel(groups, total, z2, h1, pair, cross, w_conv, w_head, target, dz2, h2, resid, padded):
    rows, channels = h1.shape
    ez = rows // (EX * EY)
    grid = with_layers(h1, pair, cross, ez, groups)
    before, after = along_span(grid, ez, groups)
    padded[...] = jnp.concatenate([before, grid, after], axis=-1).astype(BF16)
    hidden = z2[...]
    for dy in (0, 2):
        taken = padded[:, dy : dy + EY].reshape(EX, rows // EX, 3 * channels)
        hidden = hidden + tap_sum(taken, w_conv, dy)
    act = (hidden * jax.nn.sigmoid(hidden)).astype(BF16)
    output = dot(act, w_head[...])
    miss = (LOSS_WEIGHT * (output - target[...].astype(F32)) / total).astype(BF16)
    h2[...] = act
    resid[...] = miss
    dz2[...] = (dot_nt(miss, w_head[...]) * silu_grad(hidden)).astype(BF16)


def tap_sum_back(shifted, w_conv, dy):
    total = 0.0
    for dz, taken in enumerate(shifted):
        tap = 3 * dy + dz
        both = dot_nt(taken.reshape(-1, taken.shape[2]), w_conv[9 + tap])
        ahead_x = dot_nt(taken[0], w_conv[18 + tap])
        behind_x = dot_nt(taken[1], w_conv[tap])
        total = total + both + jnp.concatenate([behind_x, ahead_x], axis=0)
    return total


def centre_back_kernel(groups, dz2, w_conv, h2, resid, dh1, head):
    rows, channels = dz2.shape
    ez = rows // (EX * EY)
    grid = dz2[...].astype(F32).reshape(EX, EY, ez, channels)
    before, after = along_span(grid, ez, groups)
    shifted = [
        part.astype(BF16).reshape(EX, rows // EX, channels) for part in (after, grid, before)
    ]
    dh1[...] = tap_sum_back(shifted, w_conv, 1)
    head[...] = dot(h2[...].astype(F32).T.astype(BF16), resid[...])


def back_kernel(groups, dh1, head, dz2, pair, cross, w_conv, z1, snapshot, kept, sent, out):
    rows, channels = dz2.shape
    ez = rows // (EX * EY)
    grid = with_layers(dz2, pair, cross, ez, groups)
    before, after = along_span(grid, ez, groups)
    shifted = [part.astype(BF16) for part in (after, grid, before)]
    features = snapshot.shape[1]
    out[:, features:] = head[...]
    total = dh1[...]
    for dy in (0, 2):
        taken = [
            part[:, 2 - dy : 2 - dy + EY].reshape(EX, rows // EX, channels) for part in shifted
        ]
        total = total + tap_sum_back(taken, w_conv, dy)
    dz1 = total * silu_grad(z1[...])
    out[:, :features] = dot(dz1.T.astype(BF16), snapshot[...])
    quarter = channels // groups
    place = lax.axis_index("grp")
    for k in range(groups):
        piece = sent if k % 2 else kept
        at = pl.multiple_of(jnp.bitwise_xor(place, k) * quarter, quarter)
        piece[k // 2] = out[pl.ds(at, quarter)].astype(piece.dtype)


def core_kernel(kept, got, out_kept, out_sent):
    out_kept[...] = kept[0] + got[0].astype(F32)
    out_sent[...] = (kept[1] + got[1].astype(F32)).astype(BF16)


def taps_kernel(
    groups, sims, h_own, h_one, h_two, h_three, d_own, d_one, d_two, d_three, after_this, *refs
):
    out, h_all, r_all = refs[-3:]
    rows, channels = h_own.shape
    ez = rows // (EX * EY)
    quarter = channels // groups
    crop = ez // groups
    place = lax.axis_index("grp")
    layer = EY * ez
    lane = lax.broadcasted_iota(jnp.int32, (channels, channels), 1)
    channel = lax.broadcasted_iota(jnp.int32, (channels, channels), 0)
    chosen = jnp.where(
        (channel == place * quarter + lax.rem(lane, quarter)) & (lane < 3 * quarter), 1.0, 0.0
    ).astype(BF16)
    pairs = ((h_own, d_own), (h_one, d_one), (h_two, d_two), (h_three, d_three))
    for k, (h, d) in enumerate(pairs):
        at = jnp.bitwise_xor(place, k)
        mine = dot(d[...], chosen)
        for x in range(EX):
            h_all[x, at] = h[x * layer : (x + 1) * layer]
            r_all[x, at] = mine[x * layer : (x + 1) * layer]
    deep = groups * layer
    flat = r_all[...].reshape(EX * deep, channels)
    spot = lax.rem(lax.broadcasted_iota(jnp.int32, (EX * deep, 1), 0), crop)
    lane = lax.broadcasted_iota(jnp.int32, (1, channels), 1)
    after = jnp.where(spot == crop - 1, 0.0, pltpu.roll(flat, EX * deep - 1, 0))
    before = jnp.where(spot == 0, 0.0, pltpu.roll(flat, 1, 0))
    mixed = jnp.where(lane < quarter, after, jnp.where(lane < 2 * quarter, flat, before))
    turned = mixed.T
    spot = lax.rem(lax.broadcasted_iota(jnp.int32, (1, EX * deep), 1), deep)
    up = jnp.where(spot >= deep - ez, 0.0, pltpu.roll(turned, EX * deep - ez, 1))
    down = jnp.where(spot < ez, 0.0, pltpu.roll(turned, ez, 1))
    whole = h_all[...].reshape(EX * deep, channels)
    for dy, side in enumerate((up, turned, down)):
        side = side.astype(BF16)
        for dx in range(3):
            if dx == 0:
                got = dot(side[:, deep:], whole[:deep])
            elif dx == 1:
                got = dot(side, whole)
            else:
                got = dot(side[:, :deep], whole[deep:])
            start = (9 * dx + 3 * dy) * quarter
            out[start : start + 3 * quarter] = got[: 3 * quarter]
    me = lax.rem(lax.axis_index("sim"), sims)
    piece_rows = 27 * quarter // sims
    for k, piece in enumerate(refs[:-3]):
        at = pl.multiple_of(jnp.bitwise_xor(me, k) * piece_rows, 8)
        piece[...] = out[pl.ds(at, piece_rows)].astype(piece.dtype)


def dense_kernel(kept, got, *refs):
    out_kept, out_sent = refs[-4:-2]
    for source, target in zip(refs[:2], refs[-2:]):
        target[...] = source[...]
    total = kept[...] + got[...].astype(F32)
    grid = total.reshape(2, 2, kept.shape[0] // 4, kept.shape[1])
    odd = lax.rem(lax.div(lax.axis_index("sim"), 2), 2) == 1
    out_kept[...] = jnp.where(odd, grid[:, 1], grid[:, 0])
    out_sent[...] = jnp.where(odd, grid[:, 0], grid[:, 1]).astype(BF16)


def half_kernel(scale, kept, got, out_kept, out_sent):
    total = kept[...] + got[...].astype(F32)
    upper = lax.rem(lax.div(lax.axis_index("sim"), scale), 2) == 1
    out_kept[...] = jnp.where(upper, total[1], total[0])
    out_sent[...] = jnp.where(upper, total[0], total[1]).astype(BF16)


def packed(taps, dense):
    channels = taps.shape[1]
    parts = [taps]
    for start in range(0, dense.shape[1], channels):
        piece = dense[:, start : start + channels]
        short_by = channels - piece.shape[1]
        if short_by:
            piece = jnp.concatenate([piece, jnp.zeros((piece.shape[0], short_by), F32)], axis=1)
        parts.append(piece)
    return jnp.concatenate(parts, axis=0)


def sum_kernel(parts, kept, *refs):
    total = kept[...]
    for other in refs[: parts - 1]:
        total = total + other[...].astype(F32)
    refs[-1][...] = total.astype(BF16)


def share_kernel(taps, one, two, three, dense, dense_in, out):
    total = taps[...]
    for other in (one, two, three):
        total = total + other[...].astype(F32)
    out[...] = packed(total, dense[...] + dense_in[...].astype(F32)).astype(BF16)


def spread_kernel(features, own, *refs):
    count = len(refs) - 3 + 1
    shares = (own,) + refs[:-3]
    taps, encode, head = refs[-3:]
    channels = own.shape[1]
    tap_rows = taps.shape[0] // count
    own_rows = encode.shape[0] // count
    me = lax.axis_index("sim")
    for k, share in enumerate(shares):
        source = jnp.bitwise_xor(me, k)
        value = share[...].astype(F32)
        taps[pl.ds(pl.multiple_of(source * tap_rows, 8), tap_rows)] = value[:tap_rows]
        rows = pl.ds(pl.multiple_of(source * own_rows, 8), own_rows)
        start = tap_rows
        for first in range(0, features, channels):
            encode[rows, first : first + channels] = value[start : start + own_rows]
            start += own_rows
        head[rows] = value[start : start + own_rows, : head.shape[1]]


def call(kernel, outs, scratch=(), in_hbm=(), inputs=0, flops=1000):
    specs = {}
    if in_hbm:
        specs["in_specs"] = [
            pl.BlockSpec(memory_space=pl.ANY if i in in_hbm else pltpu.VMEM) for i in range(inputs)
        ]
    return pl.pallas_call(
        kernel,
        out_shape=outs,
        scratch_shapes=list(scratch),
        compiler_params=pltpu.CompilerParams(vmem_limit_bytes=VMEM_LIMIT),
        cost_estimate=pl.CostEstimate(flops=flops, bytes_accessed=1000, transcendentals=0),
        **specs,
    )


def shaped(shape, kind):
    return jax.ShapeDtypeStruct(shape, kind)


def swapped(value, axis, mask):
    count = lax.axis_size(axis)
    return lax.ppermute(value, axis, [(i, i ^ mask) for i in range(count)])


def crossed(value, axis, periodic):
    count = lax.axis_size(axis)
    route = [(i, i + 1 if i % 2 else i - 1) for i in range(count)]
    if periodic:
        route = [(i, j % count) for i, j in route]
    return lax.ppermute(value, axis, [(i, j) for i, j in route if 0 <= j < count])


def exchanged(edges):
    pair_x, cross_x, pair_y, cross_y = edges
    cross_x = crossed(cross_x, "sim", True)
    pair_x = swapped(pair_x, "sim", 1)
    cross_y = crossed(cross_y, "grp", False)
    pair_y = swapped(pair_y, "grp", 1)
    return pair_x, cross_x, pair_y, cross_y


def gathered(share, sims):
    got = {0: share}
    for k in sorted(range(2, sims, 2), reverse=True):
        got[k] = swapped(share, "sim", k)
    for k in range(0, sims, 2):
        got[k + 1] = swapped(got[k], "sim", 1)
    return [got[k] for k in range(sims)]


def body(velocity, slot_of, w_encode, w_conv, w_head):
    stencil, wall = (jnp.asarray(table) for table in element_tables())
    block = velocity[0, 0]
    slots = slot_of[0]
    rows, width = block.shape[1:]
    ez = rows // (EX * EY)
    channels = w_encode.shape[1]
    features = w_encode.shape[0]
    outputs = w_head.shape[1]
    sims = lax.axis_size("sim")
    groups = lax.axis_size("grp")
    total = rows * sims * groups
    quarter = channels // groups

    whole = shaped((3, rows, width), F32)
    x_edge = shaped((3, EY * ez // 2, 2 * NP * NP), BF16)
    y_edge = shaped((3, ez, 2 * NP * NP), BF16)
    edge_shapes = (x_edge, x_edge, y_edge, y_edge)

    order, back, tabs = call(
        order_kernel,
        (
            shaped((rows, rows), BF16),
            shaped((rows, rows), BF16),
            shaped((4, width, 2 * NP * NP), BF16),
        ),
        flops=4 * 10**9,
    )(slots)
    field, *edges = call(prepare_kernel, (whole,) + edge_shapes, flops=4 * 10**9)(block, order, tabs)
    halos = exchanged(edges)
    part = call(inside_kernel, whole)(field, stencil)
    field, *edges = call(join_kernel, (whole,) + edge_shapes)(part, *halos, tabs)
    halos = exchanged(edges)
    part = call(inside_kernel, whole)(field, stencil)
    field, snapshot, target, z1, h1 = call(
        encode_kernel,
        (
            whole,
            shaped((rows, features), BF16),
            shaped((rows, outputs), BF16),
            shaped((rows, channels), F32),
            shaped((rows, channels), BF16),
        ),
    )(part, *halos, tabs, wall, w_encode)

    h_three = swapped(h1, "grp", 3)
    h_one = swapped(h1, "grp", 1)
    h_two = swapped(h_three, "grp", 1)
    rows_bf = shaped((rows, channels), BF16)
    square = shaped((rows, channels), F32)
    z2 = call(functools.partial(centre_kernel, groups), square, flops=2 * 10**9)(h1, w_conv)
    dz2, h2, resid = call(
        functools.partial(forward_kernel, groups, total),
        (rows_bf, rows_bf, shaped((rows, outputs), BF16)),
        (pltpu.VMEM((EX, EY + 2, ez, 3 * channels), BF16),),
    )(z2, h1, h_one, h_three, w_conv, w_head, target)

    d_three = swapped(dz2, "grp", 3)
    d_one = swapped(dz2, "grp", 1)
    d_two = swapped(d_three, "grp", 1)
    wide = features + outputs
    pair = (groups // 2, quarter, wide)
    dh1, head = call(
        functools.partial(centre_back_kernel, groups),
        (square, shaped((channels, outputs), F32)),
        flops=2 * 10**9,
    )(dz2, w_conv, h2, resid)
    e_kept, e_sent = call(
        functools.partial(back_kernel, groups),
        (shaped(pair, F32), shaped(pair, BF16)),
        (pltpu.VMEM((channels, wide), F32),),
    )(dh1, head, dz2, d_one, d_three, w_conv, z1, snapshot)
    e_got = swapped(e_sent, "grp", 1)
    e_kept, e_sent = call(core_kernel, (shaped(pair[1:], F32), shaped(pair[1:], BF16)))(e_kept, e_got)
    e_got = swapped(e_sent, "grp", 2)
    tap_rows = 27 * quarter // sims
    own_rows = quarter // sims
    direct = sims == 8
    if direct:
        pieces = [shaped((tap_rows, channels), BF16 if k % 2 else F32) for k in range(sims)]
    else:
        pieces = [shaped((27 * quarter, channels), BF16)]
    taps = call(
        functools.partial(taps_kernel, groups, sims if direct else 1),
        tuple(pieces),
        (
            pltpu.VMEM((27 * quarter, channels), F32),
            pltpu.VMEM((EX, groups, EY * ez, channels), BF16),
            pltpu.VMEM((EX, groups, EY * ez, channels), F32),
        ),
        in_hbm=(8,),
        inputs=9,
    )(h1, h_one, h_two, h_three, dz2, d_one, d_two, d_three, e_kept)
    if direct:
        tap_piece = shaped((tap_rows, channels), BF16)
        part = (2, 2 * own_rows, wide)
        e_kept, e_sent, *later = call(
            dense_kernel, (shaped(part, F32), shaped(part, BF16)) + (tap_piece,) * 2
        )(e_kept, e_got, taps[3], taps[1])
        e_got = swapped(e_sent, "sim", 2)
        taps_in = {k: swapped(taps[k + 1], "sim", 1) for k in (6, 4)}
        taps_in.update((k, swapped(piece, "sim", 1)) for k, piece in zip((2, 0), later))
        add_two = call(functools.partial(sum_kernel, 2), tap_piece)
        add_three = call(functools.partial(sum_kernel, 3), tap_piece)
        six = swapped(add_two(taps[6], taps_in[6], e_sent), "sim", 2)
        two = swapped(add_two(taps[2], taps_in[2]), "sim", 2)
        part = shaped((2 * own_rows, wide), F32), shaped((2 * own_rows, wide), BF16)
        e_kept, e_sent = call(functools.partial(half_kernel, 4), part)(e_kept, e_got)
        e_got = swapped(e_sent, "sim", 4)
        four = swapped(add_three(taps[4], taps_in[4], six, e_sent), "sim", 4)
        part = shaped((own_rows, wide), F32), shaped((own_rows, wide), BF16)
        e_kept, e_sent = call(functools.partial(half_kernel, 1), part, flops=4 * 10**9)(
            e_kept.reshape(2, own_rows, wide), e_got.reshape(2, own_rows, wide)
        )
        e_got = swapped(e_sent, "sim", 1)
        blocks = -(-wide // channels)
        share = call(share_kernel, shaped((tap_rows + blocks * own_rows, channels), BF16))(
            taps[0], taps_in[0], two, four, e_kept, e_got
        )
        shares = gathered(share, sims)
        velocity_next = call(restore_kernel, whole, in_hbm=(2,), inputs=3)(field, back, shares[1])
        taps, encode, head = call(
            functools.partial(spread_kernel, features),
            (
                shaped((27 * quarter, channels), F32),
                shaped((quarter, features), F32),
                shaped((quarter, outputs), F32),
            ),
        )(*shares)
    else:
        taps = taps[0].reshape(sims, tap_rows, channels)
        taps = lax.all_to_all(taps, "sim", 0, 0, tiled=True)
        taps = jnp.sum(taps.astype(F32), axis=0).astype(BF16)
        taps = lax.all_gather(taps, "sim").astype(F32)
        velocity_next = call(restore_kernel, whole, in_hbm=(2,), inputs=3)(field, back, e_kept)
        dense = e_kept + e_got.astype(F32)
        dense = dense.astype(BF16).reshape(sims, own_rows, wide)
        dense = lax.all_to_all(dense, "sim", 0, 0, tiled=True)
        dense = jnp.sum(dense.astype(F32), axis=0).astype(BF16)
        dense = lax.all_gather(dense, "sim").reshape(quarter, wide).astype(F32)
        encode = dense[:, :features]
        head = dense[:, features:]
    taps = taps.reshape(27, quarter, channels)
    return velocity_next[None, None], encode.T, taps.transpose(0, 2, 1), head


def solution(mesh):
    placed = (P("sim", "grp", None, None, None), P("sim", "grp", None), P(), P(), P())
    return jax.shard_map(
        body,
        mesh=mesh,
        in_specs=placed,
        out_specs=(
            P("sim", "grp", None, None, None),
            P(None, "grp"),
            P(None, None, "grp"),
            P("grp", None),
        ),
        check_vma=False,
    )
```

```python
import functools

import jax
import jax.numpy as jnp
import ml_dtypes
import numpy as np
from jax import lax
from jax.experimental import pallas as pl
from jax.experimental.pallas import tpu as pltpu
from jax.sharding import PartitionSpec as P

NP = 8
EX = 2
EY = 4
STEPS = 2

VISCOSITY = 0.2
TIME_STEP = 0.005
PENALTY = 100.0
LOSS_WEIGHT = 64.0
FACE_RATE = TIME_STEP * VISCOSITY * PENALTY

F32 = jnp.float32
BF16 = jnp.bfloat16
VMEM_LIMIT = 16 * 1024 * 1024


def derivative_matrix(count):
    places = np.arange(count)
    points = -np.cos(np.pi * places / (count - 1))
    weights = np.where(places % 2 == 0, 1.0, -1.0)
    weights[0] = weights[0] * 0.5
    weights[count - 1] = weights[count - 1] * 0.5
    identity = np.eye(count)
    spread = points[:, None] - points[None, :] + identity
    deriv = weights[None, :] / weights[:, None] / spread
    deriv = deriv * (1.0 - identity)
    return deriv - identity * deriv.sum(axis=1)[:, None]


def short(table):
    return np.asarray(table, np.float32).astype(ml_dtypes.bfloat16)


def in_three(table):
    table = np.asarray(table, np.float32)
    high = table.astype(ml_dtypes.bfloat16)
    low = (table - high.astype(np.float32)).astype(ml_dtypes.bfloat16)
    return np.concatenate([high, high, low], axis=0)


@functools.lru_cache(maxsize=None)
def element_tables():
    count = NP
    deriv = derivative_matrix(count)
    single = np.eye(count)
    square = np.eye(count * count)
    grid = np.arange(count**3).reshape(count, count, count)
    final = count - 1
    faces = [
        grid[0].ravel(),
        grid[final].ravel(),
        grid[:, 0].ravel(),
        grid[:, final].ravel(),
        grid[:, :, 0].ravel(),
        grid[:, :, final].ravel(),
    ]

    def pick(which):
        table = np.zeros((count**3, count * count))
        table[which, np.arange(count * count)] = 1.0
        return table

    picks = [pick(which) for which in faces]
    none = np.zeros_like(picks[0])
    taken = np.concatenate([picks[i] for i in (3, 2, 5, 4)], axis=1)
    placed = np.concatenate(picks[2:], axis=1).T
    bottom = np.zeros((count**3, count * count))
    for first in range(count):
        for middle in range(count):
            for inner in range(count):
                bottom[grid[first, middle, inner], first * count + inner] = (
                    VISCOSITY * deriv[0, middle]
                )
    mirrored = np.concatenate([deriv, deriv @ deriv], axis=0)[:, ::-1].reshape(2, count, count)
    straight = np.stack([deriv, deriv @ deriv])
    half = count // 2
    scale = np.array([-TIME_STEP, TIME_STEP * VISCOSITY])[:, None, None]

    def along_first(sign):
        mixed = (0.5 * scale * (straight + sign * mirrored))[:, :half, :half]
        return in_three(np.concatenate([np.kron(part.T, square) for part in mixed], axis=1))

    small_y = np.kron(deriv, single)
    small_z = np.kron(single, deriv)
    curved = TIME_STEP * VISCOSITY * (small_y @ small_y + small_z @ small_z).T
    small_y = -TIME_STEP * small_y.T
    small_z = -TIME_STEP * small_z.T
    blank = np.zeros_like(curved)

    def across(blocks):
        table = in_three(np.concatenate(blocks, axis=1))
        return np.concatenate([table, np.zeros((count * count, table.shape[1]), table.dtype)], axis=0)

    both = np.concatenate(
        [
            across([small_y, curved, small_z, blank]),
            across([curved, small_y, blank, small_z]),
        ],
        axis=1,
    )
    filled = np.zeros((count**3, count**3 - taken.shape[1]))
    stencil = np.concatenate(
        [
            along_first(1.0),
            along_first(-1.0),
            both,
            short(placed),
            short(np.concatenate([taken, filled], axis=1)),
        ],
        axis=0,
    )
    wall = in_three(np.concatenate([bottom, none, none, bottom], axis=1))
    return stencil, wall


def dot(left, right):
    return jnp.dot(left, right, preferred_element_type=F32)


def dot_nt(left, right):
    return lax.dot_general(left, right, (((1,), (1,)), ((), ())), preferred_element_type=F32)


def split_two(value):
    high = value.astype(BF16)
    return high, (value - high.astype(F32)).astype(BF16)


def moved(order, value):
    high = value.astype(BF16)
    rest = value - high.astype(F32)
    middle, low = split_two(rest)
    return dot(order, high) + dot(order, middle) + dot(order, low)


def slot_matrix(slots):
    count = slots.shape[1]
    rows = lax.broadcasted_iota(jnp.int32, (count, count), 0)
    return jnp.where(rows == slots, 1.0, 0.0).astype(F32)


def layer_rows(field, x, layer, ez):
    start = (x * EY + layer) * ez
    return field[:, start : start + ez].reshape(3 * ez, field.shape[2])


def edge_tables():
    side = NP * NP
    point = lax.broadcasted_iota(jnp.int32, (NP * side, 2 * side), 0)
    lane = lax.broadcasted_iota(jnp.int32, (NP * side, 2 * side), 1)
    middle = lax.rem(lax.div(point, NP), NP)
    place = lax.div(point, side) * NP + lax.rem(point, NP)

    def table(level, shift):
        return jnp.where((middle == level) & (lane == place + shift), 1.0, 0.0).astype(BF16)

    return table(0, 0), table(0, side), table(NP - 1, 0), table(NP - 1, side)


def order_kernel(slots, order, back, tabs):
    matrix = slot_matrix(slots[...])
    back[...] = matrix.astype(BF16)
    order[...] = matrix.T.astype(BF16)
    for i, table in enumerate(edge_tables()):
        tabs[i] = table


def is_even(axis):
    return lax.rem(lax.axis_index(axis), 2) == 0


def write_edges(field, tabs, outs, ez):
    pair_x, cross_x, pair_y, cross_y = outs
    side = NP * NP
    half = EY * ez // 2
    last = NP * side - side
    even_x = is_even("sim")
    even_y = is_even("grp")
    near = field[:, 0 : 2 * half, 0 : 2 * side][:, :, :side]
    far = field[:, 2 * half : 4 * half, last - side :][:, :, side:]
    to_left = jnp.concatenate([near[:, :half], near[:, half:]], axis=2)
    to_right = jnp.concatenate([far[:, :half], far[:, half:]], axis=2)
    pair_x[...] = jnp.where(even_x, to_right, to_left).astype(BF16)
    cross_x[...] = jnp.where(even_x, to_left, to_right).astype(BF16)
    to_below, to_above = [
        dot(layer_rows(field, 0, layer, ez).astype(BF16), tabs[at])
        + dot(layer_rows(field, 1, layer, ez).astype(BF16), tabs[at + 1])
        for layer, at in ((0, 0), (EY - 1, 2))
    ]
    pair_y[...] = jnp.where(even_y, to_above, to_below).astype(BF16).reshape(pair_y.shape)
    cross_y[...] = jnp.where(even_y, to_below, to_above).astype(BF16).reshape(cross_y.shape)


def add_edges(part, pair_x, cross_x, pair_y, cross_y, tabs, field, ez):
    side = NP * NP
    half = EY * ez // 2
    width = NP * side
    even_x = is_even("sim")
    even_y = is_even("grp")
    pair = FACE_RATE * pair_x[...].astype(F32)
    cross = FACE_RATE * cross_x[...].astype(F32)
    left = jnp.where(even_x, cross, pair)
    right = jnp.where(even_x, pair, cross)
    pair = pair_y[...].astype(F32)
    cross = cross_y[...].astype(F32)
    below = jnp.where(even_y, cross, pair).astype(BF16).reshape(3 * ez, 2 * side)
    above = jnp.where(even_y, pair, cross).astype(BF16).reshape(3 * ez, 2 * side)
    first = lax.broadcasted_iota(jnp.int32, (1, 1, 2 * side), 2) < side

    field[...] = part[...]
    turned = pltpu.roll(left, side, 2)
    field[:, 0:half, : 2 * side] += jnp.where(first, left, 0.0)
    field[:, half : 2 * half, : 2 * side] += jnp.where(first, turned, 0.0)
    turned = pltpu.roll(right, side, 2)
    field[:, 2 * half : 3 * half, width - 2 * side :] += jnp.where(first, 0.0, turned)
    field[:, 3 * half : 4 * half, width - 2 * side :] += jnp.where(first, 0.0, right)
    for x in range(EX):
        for layer, value, at in ((0, below, 0), (EY - 1, above, 2)):
            start = (x * EY + layer) * ez
            more = FACE_RATE * dot_nt(value, tabs[at + x])
            field[:, start : start + ez] += more.reshape(3, ez, width)


def prepare_kernel(vel, order, tabs, field, *edges):
    ez = vel.shape[1] // (EX * EY)
    for c in range(3):
        field[c] = moved(order[...], vel[c])
    write_edges(field, tabs, edges, ez)


def face_count(width):
    point = lax.broadcasted_iota(jnp.int32, (1, width), 1)
    count = jnp.zeros((1, width), F32)
    for stride in (NP * NP, NP, 1):
        index = lax.rem(lax.div(point, stride), NP)
        count = count + jnp.where((index == 0) | (index == NP - 1), 1.0, 0.0)
    return count


def inside_kernel(field, stencil, part):
    rows = field.shape[1]
    width = field.shape[2]
    ez = rows // (EX * EY)
    half = width // 2
    side = NP * NP
    pair = 2 * side
    tiles = width // pair
    even = stencil.at[0 : 3 * half]
    odd = stencil.at[3 * half : 6 * half]
    start = 6 * half
    across = stencil.at[start : start + 4 * side]
    placed = stencil.at[start + 4 * side : start + 8 * side]
    taken = stencil.at[start + 8 * side : start + 8 * side + width]
    keep = 1.0 - FACE_RATE * face_count(width)
    lanes = lax.broadcasted_iota(jnp.int32, (1, pair), 1)
    first = lanes < side
    tile = [field[:, :, j * pair : (j + 1) * pair].reshape(3 * rows, pair) for j in range(tiles)]
    swap = [pltpu.roll(value, side, 1) for value in tile]

    high = [value.astype(BF16).astype(F32) for value in tile]
    high_swap = [value.astype(BF16).astype(F32) for value in swap]

    faces = dot(jnp.concatenate(high, axis=1).astype(BF16), taken[:, : 4 * side])
    in_y = faces[:, :pair].reshape(3 * EX, EY, ez, pair)
    wall = jnp.zeros((3 * EX, 1, ez, pair), F32)
    beside_y = jnp.where(
        first,
        jnp.concatenate([wall, in_y[:, :-1]], axis=1),
        jnp.concatenate([in_y[:, 1:], wall], axis=1),
    ).reshape(3 * rows, pair)
    in_z = faces[:, pair:].reshape(3 * EX * EY, ez, pair)
    beside_z = jnp.where(
        first, pltpu.roll(in_z, 1, 1), pltpu.roll(in_z, ez - 1, 1)
    ).reshape(3 * rows, pair)
    beside = jnp.concatenate([beside_y, beside_z], axis=1).astype(BF16)

    def three(value):
        top, rest = split_two(value)
        return jnp.concatenate([top, rest, top], axis=1)

    mirror = jnp.concatenate([swap[tiles - 1 - j] for j in range(tiles // 2)], axis=1)
    near = jnp.concatenate(tile[: tiles // 2], axis=1)
    from_even = dot(three(near + mirror), even[...])
    from_odd = dot(three(near - mirror), odd[...])

    for j in range(tiles):
        cols = slice(j * pair, (j + 1) * pair)
        low = tile[j] - high[j]
        low_swap = swap[j] - high_swap[j]
        one = jnp.concatenate([jnp.where(first, high[j], low_swap), high[j]], axis=1).astype(BF16)
        two = jnp.concatenate([jnp.where(first, high_swap[j], low), high_swap[j]], axis=1).astype(BF16)
        got_one = dot(one, across[:, : 4 * side])
        got_two = dot(two, across[:, 4 * side :])
        slope_y = jnp.where(first, got_one[:, :pair], got_two[:, :pair])
        slope_z = got_one[:, pair:] + got_two[:, pair:]
        curve = jnp.where(first, got_two[:, :pair], got_one[:, :pair])
        if j < tiles // 2:
            at = slice(j * pair, (j + 1) * pair)
            up = slice(half + j * pair, half + (j + 1) * pair)
            slope_x = from_odd[:, at] + from_even[:, at]
            curve = pltpu.roll(curve, side, 1) + (from_even[:, up] + from_odd[:, up])
        else:
            k = tiles - 1 - j
            at = slice(k * pair, (k + 1) * pair)
            up = slice(half + k * pair, half + (k + 1) * pair)
            slope_x = pltpu.roll(from_odd[:, at] - from_even[:, at], side, 1)
            curve = pltpu.roll(curve + (from_even[:, up] - from_odd[:, up]), side, 1)
        value = tile[j] * keep[:, cols] + curve
        value = value + FACE_RATE * dot(beside, placed[:, cols])
        value = value.reshape(3, rows, pair)
        for d, slope in enumerate((slope_x, slope_y, slope_z)):
            value = value + slope.reshape(3, rows, pair) * tile[j].reshape(3, rows, pair)[d][None]
        layer = EY * ez
        if j == 0:
            beyond = swap[tiles - 1].reshape(3, rows, pair)[:, :layer]
            beyond = jnp.where(first, FACE_RATE * beyond, 0.0)
            value = jnp.concatenate([value[:, :layer], value[:, layer:] + beyond], axis=1)
        if j == tiles - 1:
            beyond = swap[0].reshape(3, rows, pair)[:, layer:]
            beyond = jnp.where(first, 0.0, FACE_RATE * beyond)
            value = jnp.concatenate([value[:, :layer] + beyond, value[:, layer:]], axis=1)
        part[:, :, cols] = value


def join_kernel(part, pair_x, cross_x, pair_y, cross_y, tabs, field, *edges):
    ez = part.shape[1] // (EX * EY)
    add_edges(part, pair_x, cross_x, pair_y, cross_y, tabs, field, ez)
    write_edges(field, tabs, edges, ez)


def encode_kernel(
    part, pair_x, cross_x, pair_y, cross_y, tabs, wall, w_encode,
    field, snapshot, target, z1, h1,
):
    ez = part.shape[1] // (EX * EY)
    add_edges(part, pair_x, cross_x, pair_y, cross_y, tabs, field, ez)
    high0, low0 = split_two(field[0])
    high2, low2 = split_two(field[2])
    snap = jnp.concatenate([high0, high2], axis=1)
    snapshot[...] = snap
    target[...] = (
        dot(jnp.concatenate([high0, low0, high0], axis=1), wall[:, : 2 * NP * NP])
        + dot(jnp.concatenate([high2, low2, high2], axis=1), wall[:, 2 * NP * NP :])
    ).astype(BF16)
    hidden = dot(snap, w_encode[...])
    z1[...] = hidden
    h1[...] = (hidden * jax.nn.sigmoid(hidden)).astype(BF16)


def same_kernel(value, out):
    out[...] = value[...]


def restore_kernel(field, back, after_this, out, done):
    for c in range(3):
        out[c] = moved(back[...], field[c])
    done[...] = jnp.zeros_like(done)


def silu_grad(value):
    sigma = jax.nn.sigmoid(value)
    return sigma * (1.0 + value * (1.0 - sigma))


def with_layers(own, pair, cross, ez, groups):
    channels = own.shape[-1]
    place = lax.axis_index("grp")
    grid = own[...].astype(F32).reshape(EX, EY, ez, channels)
    even = is_even("grp")
    pair = pair[...].reshape(EX, EY, ez, channels).astype(F32)
    cross = cross[...].reshape(EX, EY, ez, channels).astype(F32)
    before = jnp.where(even, cross[:, EY - 1 :], pair[:, EY - 1 :])
    after = jnp.where(even, pair[:, :1], cross[:, :1])
    before = jnp.where(place > 0, before, 0.0)
    after = jnp.where(place < groups - 1, after, 0.0)
    return jnp.concatenate([before, grid, after], axis=1)


def along_span(grid, ez, groups):
    shape = grid.shape
    rows = int(np.prod(shape[:-1]))
    crop = ez // groups
    flat = grid.reshape(rows, shape[-1])
    place = lax.rem(lax.broadcasted_iota(jnp.int32, (rows, 1), 0), crop)
    before = jnp.where(place == 0, 0.0, pltpu.roll(flat, 1, 0))
    after = jnp.where(place == crop - 1, 0.0, pltpu.roll(flat, rows - 1, 0))
    return before.reshape(shape), after.reshape(shape)


def tap_sum(taken, w_conv, dy):
    channels = w_conv.shape[1]
    first = 3 * dy
    rows = taken.shape[1]

    def times(value, start):
        return dot(value, w_conv[start + first : start + first + 3].reshape(-1, channels))

    both = times(taken.reshape(EX * rows, taken.shape[2]), 9)
    return both + jnp.concatenate([times(taken[1], 18), times(taken[0], 0)], axis=0)


def centre_kernel(groups, h1, w_conv, z2):
    rows, channels = h1.shape
    ez = rows // (EX * EY)
    grid = h1[...].astype(F32).reshape(EX, EY, ez, channels)
    before, after = along_span(grid, ez, groups)
    taken = jnp.concatenate([before, grid, after], axis=-1).astype(BF16)
    z2[...] = tap_sum(taken.reshape(EX, rows // EX, 3 * channels), w_conv, 1)


def forward_kernel(groups, total, z2, h1, pair, cross, w_conv, w_head, target, dz2, h2, resid, padded):
    rows, channels = h1.shape
    ez = rows // (EX * EY)
    grid = with_layers(h1, pair, cross, ez, groups)
    before, after = along_span(grid, ez, groups)
    padded[...] = jnp.concatenate([before, grid, after], axis=-1).astype(BF16)
    hidden = z2[...]
    for dy in (0, 2):
        taken = padded[:, dy : dy + EY].reshape(EX, rows // EX, 3 * channels)
        hidden = hidden + tap_sum(taken, w_conv, dy)
    act = (hidden * jax.nn.sigmoid(hidden)).astype(BF16)
    output = dot(act, w_head[...])
    miss = (LOSS_WEIGHT * (output - target[...].astype(F32)) / total).astype(BF16)
    h2[...] = act
    resid[...] = miss
    dz2[...] = (dot_nt(miss, w_head[...]) * silu_grad(hidden)).astype(BF16)


def tap_sum_back(shifted, w_conv, dy):
    total = 0.0
    for dz, taken in enumerate(shifted):
        tap = 3 * dy + dz
        both = dot_nt(taken.reshape(-1, taken.shape[2]), w_conv[9 + tap])
        ahead_x = dot_nt(taken[0], w_conv[18 + tap])
        behind_x = dot_nt(taken[1], w_conv[tap])
        total = total + both + jnp.concatenate([behind_x, ahead_x], axis=0)
    return total


def centre_back_kernel(groups, dz2, w_conv, h2, resid, dh1, head):
    rows, channels = dz2.shape
    ez = rows // (EX * EY)
    grid = dz2[...].astype(F32).reshape(EX, EY, ez, channels)
    before, after = along_span(grid, ez, groups)
    shifted = [
        part.astype(BF16).reshape(EX, rows // EX, channels) for part in (after, grid, before)
    ]
    dh1[...] = tap_sum_back(shifted, w_conv, 1)
    head[...] = dot(h2[...].astype(F32).T.astype(BF16), resid[...])


def back_kernel(groups, dh1, head, dz2, pair, cross, w_conv, z1, snapshot, kept, sent, out):
    rows, channels = dz2.shape
    ez = rows // (EX * EY)
    grid = with_layers(dz2, pair, cross, ez, groups)
    before, after = along_span(grid, ez, groups)
    shifted = [part.astype(BF16) for part in (after, grid, before)]
    features = snapshot.shape[1]
    out[:, features:] = head[...]
    total = dh1[...]
    for dy in (0, 2):
        taken = [
            part[:, 2 - dy : 2 - dy + EY].reshape(EX, rows // EX, channels) for part in shifted
        ]
        total = total + tap_sum_back(taken, w_conv, dy)
    dz1 = total * silu_grad(z1[...])
    out[:, :features] = dot(dz1.T.astype(BF16), snapshot[...])
    quarter = channels // groups
    place = lax.axis_index("grp")
    for k in range(groups):
        piece = sent if k % 2 else kept
        at = pl.multiple_of(jnp.bitwise_xor(place, k) * quarter, quarter)
        piece[k // 2] = out[pl.ds(at, quarter)].astype(piece.dtype)


def core_kernel(kept, got, out_kept, out_sent):
    out_kept[...] = kept[0] + got[0].astype(F32)
    out_sent[...] = (kept[1] + got[1].astype(F32)).astype(BF16)


def taps_kernel(
    groups, sims, h_own, h_one, h_two, h_three, d_own, d_one, d_two, d_three, after_this, *refs
):
    out, h_all, r_all = refs[-3:]
    rows, channels = h_own.shape
    ez = rows // (EX * EY)
    quarter = channels // groups
    crop = ez // groups
    place = lax.axis_index("grp")
    layer = EY * ez
    lane = lax.broadcasted_iota(jnp.int32, (channels, channels), 1)
    channel = lax.broadcasted_iota(jnp.int32, (channels, channels), 0)
    chosen = jnp.where(
        (channel == place * quarter + lax.rem(lane, quarter)) & (lane < 3 * quarter), 1.0, 0.0
    ).astype(BF16)
    pairs = ((h_own, d_own), (h_one, d_one), (h_two, d_two), (h_three, d_three))
    for k, (h, d) in enumerate(pairs):
        at = jnp.bitwise_xor(place, k)
        mine = dot(d[...], chosen)
        for x in range(EX):
            h_all[x, at] = h[x * layer : (x + 1) * layer]
            r_all[x, at] = mine[x * layer : (x + 1) * layer]
    deep = groups * layer
    flat = r_all[...].reshape(EX * deep, channels)
    spot = lax.rem(lax.broadcasted_iota(jnp.int32, (EX * deep, 1), 0), crop)
    lane = lax.broadcasted_iota(jnp.int32, (1, channels), 1)
    after = jnp.where(spot == crop - 1, 0.0, pltpu.roll(flat, EX * deep - 1, 0))
    before = jnp.where(spot == 0, 0.0, pltpu.roll(flat, 1, 0))
    mixed = jnp.where(lane < quarter, after, jnp.where(lane < 2 * quarter, flat, before))
    turned = mixed.T
    spot = lax.rem(lax.broadcasted_iota(jnp.int32, (1, EX * deep), 1), deep)
    up = jnp.where(spot >= deep - ez, 0.0, pltpu.roll(turned, EX * deep - ez, 1))
    down = jnp.where(spot < ez, 0.0, pltpu.roll(turned, ez, 1))
    whole = h_all[...].reshape(EX * deep, channels)
    for dy, side in enumerate((up, turned, down)):
        side = side.astype(BF16)
        for dx in range(3):
            if dx == 0:
                got = dot(side[:, deep:], whole[:deep])
            elif dx == 1:
                got = dot(side, whole)
            else:
                got = dot(side[:, :deep], whole[deep:])
            start = (9 * dx + 3 * dy) * quarter
            out[start : start + 3 * quarter] = got[: 3 * quarter]
    me = lax.rem(lax.axis_index("sim"), sims)
    piece_rows = 27 * quarter // sims
    for k, piece in enumerate(refs[:-3]):
        at = pl.multiple_of(jnp.bitwise_xor(me, k) * piece_rows, 8)
        piece[...] = out[pl.ds(at, piece_rows)].astype(piece.dtype)


def dense_kernel(kept, got, *refs):
    out_kept, out_sent = refs[-4:-2]
    for source, target in zip(refs[:2], refs[-2:]):
        target[...] = source[...]
    total = kept[...] + got[...].astype(F32)
    grid = total.reshape(2, 2, kept.shape[0] // 4, kept.shape[1])
    odd = lax.rem(lax.div(lax.axis_index("sim"), 2), 2) == 1
    out_kept[...] = jnp.where(odd, grid[:, 1], grid[:, 0])
    out_sent[...] = jnp.where(odd, grid[:, 0], grid[:, 1]).astype(BF16)


def half_kernel(scale, kept, got, out_kept, out_sent):
    total = kept[...] + got[...].astype(F32)
    upper = lax.rem(lax.div(lax.axis_index("sim"), scale), 2) == 1
    out_kept[...] = jnp.where(upper, total[1], total[0])
    out_sent[...] = jnp.where(upper, total[0], total[1]).astype(BF16)


def packed(taps, dense):
    channels = taps.shape[1]
    parts = [taps]
    for start in range(0, dense.shape[1], channels):
        piece = dense[:, start : start + channels]
        short_by = channels - piece.shape[1]
        if short_by:
            piece = jnp.concatenate([piece, jnp.zeros((piece.shape[0], short_by), F32)], axis=1)
        parts.append(piece)
    return jnp.concatenate(parts, axis=0)


def sum_kernel(parts, kept, *refs):
    total = kept[...]
    for other in refs[: parts - 1]:
        total = total + other[...].astype(F32)
    refs[-1][...] = total.astype(BF16)


def share_kernel(taps, one, two, three, dense, dense_in, after_this, out):
    total = taps[...]
    for other in (one, two, three):
        total = total + other[...].astype(F32)
    out[...] = packed(total, dense[...] + dense_in[...].astype(F32)).astype(BF16)


def place_kernel(masks, count, *refs):
    shares = refs[: len(masks)]
    outs = refs[-7:-4]
    held = refs[-4:-1]
    sems = refs[-1]
    channels = shares[0].shape[1]
    tap_rows, own_rows = [out.shape[0] // count for out in outs[:2]]
    features = outs[1].shape[1]
    me = lax.axis_index("sim")
    copies = []
    for i, (mask, share) in enumerate(zip(masks, shares)):
        source = jnp.bitwise_xor(me, mask)
        value = share[...].astype(F32)
        held[0][i] = value[:tap_rows]
        start = tap_rows
        for first in range(0, features, channels):
            held[1][i, :, first : first + channels] = value[start : start + own_rows]
            start += own_rows
        held[2][i] = value[start : start + own_rows, : outs[2].shape[1]]
        for j, out in enumerate(outs):
            size = tap_rows if j == 0 else own_rows
            rows = pl.ds(pl.multiple_of(source * size, 8), size)
            copy = pltpu.make_async_copy(held[j].at[i], out.at[rows], sems.at[i, j])
            copy.start()
            copies.append(copy)
    for copy in copies:
        copy.wait()


def placed_shares(shares, shapes, count):
    outs = ()
    for first in range(0, count, 2):
        masks = (first, first + 1)
        tap_rows, own_rows = [shape.shape[0] // count for shape in shapes[:2]]
        sizes = (tap_rows, own_rows, own_rows)
        held = [
            pltpu.VMEM((2, size, shape.shape[1]), F32) for size, shape in zip(sizes, shapes)
        ]
        anywhere = pl.BlockSpec(memory_space=pl.ANY)
        outs = pl.pallas_call(
            functools.partial(place_kernel, masks, count),
            out_shape=shapes,
            in_specs=[pl.BlockSpec(memory_space=pltpu.VMEM)] * 2 + [anywhere] * len(outs),
            out_specs=(anywhere,) * 3,
            scratch_shapes=held + [pltpu.SemaphoreType.DMA((2, 3))],
            input_output_aliases={2 + i: i for i in range(len(outs))},
            compiler_params=pltpu.CompilerParams(vmem_limit_bytes=VMEM_LIMIT),
            cost_estimate=pl.CostEstimate(flops=1000, bytes_accessed=1000, transcendentals=0),
        )(shares[first], shares[first + 1], *outs)
    return outs


def call(kernel, outs, scratch=(), in_hbm=(), inputs=0, flops=1000):
    specs = {}
    if in_hbm:
        specs["in_specs"] = [
            pl.BlockSpec(memory_space=pl.ANY if i in in_hbm else pltpu.VMEM) for i in range(inputs)
        ]
    return pl.pallas_call(
        kernel,
        out_shape=outs,
        scratch_shapes=list(scratch),
        compiler_params=pltpu.CompilerParams(vmem_limit_bytes=VMEM_LIMIT),
        cost_estimate=pl.CostEstimate(flops=flops, bytes_accessed=1000, transcendentals=0),
        **specs,
    )


def shaped(shape, kind):
    return jax.ShapeDtypeStruct(shape, kind)


def swapped(value, axis, mask):
    count = lax.axis_size(axis)
    return lax.ppermute(value, axis, [(i, i ^ mask) for i in range(count)])


def crossed(value, axis, periodic):
    count = lax.axis_size(axis)
    route = [(i, i + 1 if i % 2 else i - 1) for i in range(count)]
    if periodic:
        route = [(i, j % count) for i, j in route]
    return lax.ppermute(value, axis, [(i, j) for i, j in route if 0 <= j < count])


def exchanged(edges):
    pair_x, cross_x, pair_y, cross_y = edges
    cross_x = crossed(cross_x, "sim", True)
    pair_x = swapped(pair_x, "sim", 1)
    cross_y = crossed(cross_y, "grp", False)
    pair_y = swapped(pair_y, "grp", 1)
    return pair_x, cross_x, pair_y, cross_y


def gathered(share, sims):
    got = {0: share}
    for k in range(2, sims, 2):
        got[k] = swapped(share, "sim", k)
    for k in range(0, sims, 2):
        got[k + 1] = swapped(got[k], "sim", 1)
    return [got[k] for k in range(sims)]


def body(velocity, slot_of, w_encode, w_conv, w_head):
    stencil, wall = (jnp.asarray(table) for table in element_tables())
    block = velocity[0, 0]
    slots = slot_of[0]
    rows, width = block.shape[1:]
    ez = rows // (EX * EY)
    channels = w_encode.shape[1]
    features = w_encode.shape[0]
    outputs = w_head.shape[1]
    sims = lax.axis_size("sim")
    groups = lax.axis_size("grp")
    total = rows * sims * groups
    quarter = channels // groups

    whole = shaped((3, rows, width), F32)
    x_edge = shaped((3, EY * ez // 2, 2 * NP * NP), BF16)
    y_edge = shaped((3, ez, 2 * NP * NP), BF16)
    edge_shapes = (x_edge, x_edge, y_edge, y_edge)

    order, back, tabs = call(
        order_kernel,
        (
            shaped((rows, rows), BF16),
            shaped((rows, rows), BF16),
            shaped((4, width, 2 * NP * NP), BF16),
        ),
        flops=4 * 10**9,
    )(slots)
    field, *edges = call(prepare_kernel, (whole,) + edge_shapes, flops=4 * 10**9)(block, order, tabs)
    halos = exchanged(edges)
    part = call(inside_kernel, whole)(field, stencil)
    field, *edges = call(join_kernel, (whole,) + edge_shapes)(part, *halos, tabs)
    halos = exchanged(edges)
    part = call(inside_kernel, whole)(field, stencil)
    field, snapshot, target, z1, h1 = call(
        encode_kernel,
        (
            whole,
            shaped((rows, features), BF16),
            shaped((rows, outputs), BF16),
            shaped((rows, channels), F32),
            shaped((rows, channels), BF16),
        ),
    )(part, *halos, tabs, wall, w_encode)

    h_three = swapped(h1, "grp", 3)
    h_one = swapped(h1, "grp", 1)
    h_two = swapped(h_three, "grp", 1)
    rows_bf = shaped((rows, channels), BF16)
    square = shaped((rows, channels), F32)
    z2 = call(functools.partial(centre_kernel, groups), square, flops=2 * 10**9)(h1, w_conv)
    dz2, h2, resid = call(
        functools.partial(forward_kernel, groups, total),
        (rows_bf, rows_bf, shaped((rows, outputs), BF16)),
        (pltpu.VMEM((EX, EY + 2, ez, 3 * channels), BF16),),
    )(z2, h1, h_one, call(same_kernel, rows_bf, flops=2 * 10**9)(h_three), w_conv, w_head, target)

    d_three = swapped(dz2, "grp", 3)
    d_one = swapped(dz2, "grp", 1)
    d_two = swapped(d_three, "grp", 1)
    wide = features + outputs
    pair = (groups // 2, quarter, wide)
    dh1, head = call(
        functools.partial(centre_back_kernel, groups),
        (square, shaped((channels, outputs), F32)),
        flops=2 * 10**9,
    )(dz2, w_conv, h2, resid)
    e_kept, e_sent = call(
        functools.partial(back_kernel, groups),
        (shaped(pair, F32), shaped(pair, BF16)),
        (pltpu.VMEM((channels, wide), F32),),
    )(dh1, head, dz2, d_one, call(same_kernel, rows_bf, flops=2 * 10**9)(d_three), w_conv, z1, snapshot)
    e_got = swapped(e_sent, "grp", 1)
    e_kept, e_sent = call(core_kernel, (shaped(pair[1:], F32), shaped(pair[1:], BF16)))(e_kept, e_got)
    e_got = swapped(e_sent, "grp", 2)
    tap_rows = 27 * quarter // sims
    own_rows = quarter // sims
    direct = sims == 8
    if direct:
        pieces = [shaped((tap_rows, channels), BF16 if k % 2 else F32) for k in range(sims)]
    else:
        pieces = [shaped((27 * quarter, channels), BF16)]
    taps = call(
        functools.partial(taps_kernel, groups, sims if direct else 1),
        tuple(pieces),
        (
            pltpu.VMEM((27 * quarter, channels), F32),
            pltpu.VMEM((EX, groups, EY * ez, channels), BF16),
            pltpu.VMEM((EX, groups, EY * ez, channels), F32),
        ),
        in_hbm=(8,),
        inputs=9,
    )(h1, h_one, h_two, h_three, dz2, d_one, d_two, d_three, e_kept)
    restore = call(restore_kernel, (whole, shaped((8, 128), F32)), in_hbm=(2,), inputs=3)
    if direct:
        tap_piece = shaped((tap_rows, channels), BF16)
        part = (2, 2 * own_rows, wide)
        e_kept, e_sent, *later = call(
            dense_kernel, (shaped(part, F32), shaped(part, BF16)) + (tap_piece,) * 2
        )(e_kept, e_got, taps[3], taps[1])
        e_got = swapped(e_sent, "sim", 2)
        taps_in = {k: swapped(taps[k + 1], "sim", 1) for k in (6, 4)}
        taps_in.update((k, swapped(piece, "sim", 1)) for k, piece in zip((2, 0), later))
        add_two = call(functools.partial(sum_kernel, 2), tap_piece)
        add_three = call(functools.partial(sum_kernel, 3), tap_piece)
        six = swapped(add_two(taps[6], taps_in[6], e_sent), "sim", 2)
        part = shaped((2 * own_rows, wide), F32), shaped((2 * own_rows, wide), BF16)
        e_kept, e_sent = call(functools.partial(half_kernel, 4), part)(e_kept, e_got)
        e_got = swapped(e_sent, "sim", 4)
        two = add_two(taps[2], taps_in[2], e_sent)
        four = swapped(add_three(taps[4], taps_in[4], six, two), "sim", 4)
        two = swapped(two, "sim", 2)
        part = shaped((own_rows, wide), F32), shaped((own_rows, wide), BF16)
        e_kept, e_sent = call(functools.partial(half_kernel, 1), part, flops=4 * 10**9)(
            e_kept.reshape(2, own_rows, wide), e_got.reshape(2, own_rows, wide)
        )
        velocity_next, done = restore(field, back, e_sent)
        e_got = swapped(e_sent, "sim", 1)
        blocks = -(-wide // channels)
        share = call(share_kernel, shaped((tap_rows + blocks * own_rows, channels), BF16))(
            taps[0], taps_in[0], two, four, e_kept, e_got, done
        )
        shares = gathered(share, sims)
        shapes = (
            shaped((27 * quarter, channels), F32),
            shaped((quarter, features), F32),
            shaped((quarter, outputs), F32),
        )
        taps, encode, head = placed_shares(shares, shapes, sims)
    else:
        taps = taps[0].reshape(sims, tap_rows, channels)
        taps = lax.all_to_all(taps, "sim", 0, 0, tiled=True)
        taps = jnp.sum(taps.astype(F32), axis=0).astype(BF16)
        taps = lax.all_gather(taps, "sim").astype(F32)
        velocity_next, done = restore(field, back, e_kept)
        dense = e_kept + e_got.astype(F32)
        dense = dense.astype(BF16).reshape(sims, own_rows, wide)
        dense = lax.all_to_all(dense, "sim", 0, 0, tiled=True)
        dense = jnp.sum(dense.astype(F32), axis=0).astype(BF16)
        dense = lax.all_gather(dense, "sim").reshape(quarter, wide).astype(F32)
        encode = dense[:, :features]
        head = dense[:, features:]
    taps = taps.reshape(27, quarter, channels)
    return velocity_next[None, None], encode.T, taps.transpose(0, 2, 1), head


def solution(mesh):
    placed = (P("sim", "grp", None, None, None), P("sim", "grp", None), P(), P(), P())
    return jax.shard_map(
        body,
        mesh=mesh,
        in_specs=placed,
        out_specs=(
            P("sim", "grp", None, None, None),
            P(None, "grp"),
            P(None, None, "grp"),
            P("grp", None),
        ),
        check_vma=False,
    )
```

```python
import functools

import jax
import jax.numpy as jnp
import ml_dtypes
import numpy as np
from jax import lax
from jax.experimental import pallas as pl
from jax.experimental.pallas import tpu as pltpu
from jax.sharding import PartitionSpec as P

NP = 8
EX = 2
EY = 4
STEPS = 2

VISCOSITY = 0.2
TIME_STEP = 0.005
PENALTY = 100.0
LOSS_WEIGHT = 64.0
FACE_RATE = TIME_STEP * VISCOSITY * PENALTY

F32 = jnp.float32
BF16 = jnp.bfloat16
VMEM_LIMIT = 16 * 1024 * 1024


def derivative_matrix(count):
    places = np.arange(count)
    points = -np.cos(np.pi * places / (count - 1))
    weights = np.where(places % 2 == 0, 1.0, -1.0)
    weights[0] = weights[0] * 0.5
    weights[count - 1] = weights[count - 1] * 0.5
    identity = np.eye(count)
    spread = points[:, None] - points[None, :] + identity
    deriv = weights[None, :] / weights[:, None] / spread
    deriv = deriv * (1.0 - identity)
    return deriv - identity * deriv.sum(axis=1)[:, None]


def short(table):
    return np.asarray(table, np.float32).astype(ml_dtypes.bfloat16)


def in_three(table):
    table = np.asarray(table, np.float32)
    high = table.astype(ml_dtypes.bfloat16)
    low = (table - high.astype(np.float32)).astype(ml_dtypes.bfloat16)
    return np.concatenate([high, high, low], axis=0)


@functools.lru_cache(maxsize=None)
def element_tables():
    count = NP
    deriv = derivative_matrix(count)
    single = np.eye(count)
    square = np.eye(count * count)
    grid = np.arange(count**3).reshape(count, count, count)
    final = count - 1
    faces = [
        grid[0].ravel(),
        grid[final].ravel(),
        grid[:, 0].ravel(),
        grid[:, final].ravel(),
        grid[:, :, 0].ravel(),
        grid[:, :, final].ravel(),
    ]

    def pick(which):
        table = np.zeros((count**3, count * count))
        table[which, np.arange(count * count)] = 1.0
        return table

    picks = [pick(which) for which in faces]
    none = np.zeros_like(picks[0])
    taken = np.concatenate([picks[i] for i in (3, 2, 5, 4)], axis=1)
    placed = np.concatenate(picks[2:], axis=1).T
    bottom = np.zeros((count**3, count * count))
    for first in range(count):
        for middle in range(count):
            for inner in range(count):
                bottom[grid[first, middle, inner], first * count + inner] = (
                    VISCOSITY * deriv[0, middle]
                )
    mirrored = np.concatenate([deriv, deriv @ deriv], axis=0)[:, ::-1].reshape(2, count, count)
    straight = np.stack([deriv, deriv @ deriv])
    half = count // 2
    scale = np.array([-TIME_STEP, TIME_STEP * VISCOSITY])[:, None, None]

    def along_first(sign):
        mixed = (0.5 * scale * (straight + sign * mirrored))[:, :half, :half]
        return in_three(np.concatenate([np.kron(part.T, square) for part in mixed], axis=1))

    small_y = np.kron(deriv, single)
    small_z = np.kron(single, deriv)
    curved = TIME_STEP * VISCOSITY * (small_y @ small_y + small_z @ small_z).T
    small_y = -TIME_STEP * small_y.T
    small_z = -TIME_STEP * small_z.T
    blank = np.zeros_like(curved)

    def across(blocks):
        table = in_three(np.concatenate(blocks, axis=1))
        return np.concatenate([table, np.zeros((count * count, table.shape[1]), table.dtype)], axis=0)

    both = np.concatenate(
        [
            across([small_y, curved, small_z, blank]),
            across([curved, small_y, blank, small_z]),
        ],
        axis=1,
    )
    filled = np.zeros((count**3, count**3 - taken.shape[1]))
    stencil = np.concatenate(
        [
            along_first(1.0),
            along_first(-1.0),
            both,
            short(placed),
            short(np.concatenate([taken, filled], axis=1)),
        ],
        axis=0,
    )
    wall = in_three(np.concatenate([bottom, none, none, bottom], axis=1))
    return stencil, wall


def dot(left, right):
    return jnp.dot(left, right, preferred_element_type=F32)


def dot_nt(left, right):
    return lax.dot_general(left, right, (((1,), (1,)), ((), ())), preferred_element_type=F32)


def split_two(value):
    high = value.astype(BF16)
    return high, (value - high.astype(F32)).astype(BF16)


def moved(order, value):
    high = value.astype(BF16)
    rest = value - high.astype(F32)
    middle, low = split_two(rest)
    return dot(order, high) + dot(order, middle) + dot(order, low)


def slot_matrix(slots):
    count = slots.shape[1]
    rows = lax.broadcasted_iota(jnp.int32, (count, count), 0)
    return jnp.where(rows == slots, 1.0, 0.0).astype(F32)


def layer_rows(field, x, layer, ez):
    start = (x * EY + layer) * ez
    return field[:, start : start + ez].reshape(3 * ez, field.shape[2])


def edge_tables():
    side = NP * NP
    point = lax.broadcasted_iota(jnp.int32, (NP * side, 2 * side), 0)
    lane = lax.broadcasted_iota(jnp.int32, (NP * side, 2 * side), 1)
    middle = lax.rem(lax.div(point, NP), NP)
    place = lax.div(point, side) * NP + lax.rem(point, NP)

    def table(level, shift):
        return jnp.where((middle == level) & (lane == place + shift), 1.0, 0.0).astype(BF16)

    return table(0, 0), table(0, side), table(NP - 1, 0), table(NP - 1, side)


def order_kernel(slots, order, back, tabs):
    matrix = slot_matrix(slots[...])
    back[...] = matrix.astype(BF16)
    order[...] = matrix.T.astype(BF16)
    for i, table in enumerate(edge_tables()):
        tabs[i] = table


def is_even(axis):
    return lax.rem(lax.axis_index(axis), 2) == 0


def write_edges(field, tabs, outs, ez):
    pair_x, cross_x, pair_y, cross_y = outs
    side = NP * NP
    half = EY * ez // 2
    last = NP * side - side
    even_x = is_even("sim")
    even_y = is_even("grp")
    near = field[:, 0 : 2 * half, 0 : 2 * side][:, :, :side]
    far = field[:, 2 * half : 4 * half, last - side :][:, :, side:]
    to_left = jnp.concatenate([near[:, :half], near[:, half:]], axis=2)
    to_right = jnp.concatenate([far[:, :half], far[:, half:]], axis=2)
    pair_x[...] = jnp.where(even_x, to_right, to_left).astype(BF16)
    cross_x[...] = jnp.where(even_x, to_left, to_right).astype(BF16)
    to_below, to_above = [
        dot(layer_rows(field, 0, layer, ez).astype(BF16), tabs[at])
        + dot(layer_rows(field, 1, layer, ez).astype(BF16), tabs[at + 1])
        for layer, at in ((0, 0), (EY - 1, 2))
    ]
    pair_y[...] = jnp.where(even_y, to_above, to_below).astype(BF16).reshape(pair_y.shape)
    cross_y[...] = jnp.where(even_y, to_below, to_above).astype(BF16).reshape(cross_y.shape)


def add_edges(part, pair_x, cross_x, pair_y, cross_y, tabs, field, ez):
    side = NP * NP
    half = EY * ez // 2
    width = NP * side
    even_x = is_even("sim")
    even_y = is_even("grp")
    pair = FACE_RATE * pair_x[...].astype(F32)
    cross = FACE_RATE * cross_x[...].astype(F32)
    left = jnp.where(even_x, cross, pair)
    right = jnp.where(even_x, pair, cross)
    pair = pair_y[...].astype(F32)
    cross = cross_y[...].astype(F32)
    below = jnp.where(even_y, cross, pair).astype(BF16).reshape(3 * ez, 2 * side)
    above = jnp.where(even_y, pair, cross).astype(BF16).reshape(3 * ez, 2 * side)
    first = lax.broadcasted_iota(jnp.int32, (1, 1, 2 * side), 2) < side

    field[...] = part[...]
    turned = pltpu.roll(left, side, 2)
    field[:, 0:half, : 2 * side] += jnp.where(first, left, 0.0)
    field[:, half : 2 * half, : 2 * side] += jnp.where(first, turned, 0.0)
    turned = pltpu.roll(right, side, 2)
    field[:, 2 * half : 3 * half, width - 2 * side :] += jnp.where(first, 0.0, turned)
    field[:, 3 * half : 4 * half, width - 2 * side :] += jnp.where(first, 0.0, right)
    for x in range(EX):
        for layer, value, at in ((0, below, 0), (EY - 1, above, 2)):
            start = (x * EY + layer) * ez
            more = FACE_RATE * dot_nt(value, tabs[at + x])
            field[:, start : start + ez] += more.reshape(3, ez, width)


def prepare_kernel(vel, order, tabs, field, *edges):
    ez = vel.shape[1] // (EX * EY)
    for c in range(3):
        field[c] = moved(order[...], vel[c])
    write_edges(field, tabs, edges, ez)


def face_count(width):
    point = lax.broadcasted_iota(jnp.int32, (1, width), 1)
    count = jnp.zeros((1, width), F32)
    for stride in (NP * NP, NP, 1):
        index = lax.rem(lax.div(point, stride), NP)
        count = count + jnp.where((index == 0) | (index == NP - 1), 1.0, 0.0)
    return count


def inside_kernel(field, stencil, part):
    rows = field.shape[1]
    width = field.shape[2]
    ez = rows // (EX * EY)
    half = width // 2
    side = NP * NP
    pair = 2 * side
    tiles = width // pair
    even = stencil.at[0 : 3 * half]
    odd = stencil.at[3 * half : 6 * half]
    start = 6 * half
    across = stencil.at[start : start + 4 * side]
    placed = stencil.at[start + 4 * side : start + 8 * side]
    taken = stencil.at[start + 8 * side : start + 8 * side + width]
    keep = 1.0 - FACE_RATE * face_count(width)
    lanes = lax.broadcasted_iota(jnp.int32, (1, pair), 1)
    first = lanes < side
    tile = [field[:, :, j * pair : (j + 1) * pair].reshape(3 * rows, pair) for j in range(tiles)]
    swap = [pltpu.roll(value, side, 1) for value in tile]

    high = [value.astype(BF16).astype(F32) for value in tile]
    high_swap = [value.astype(BF16).astype(F32) for value in swap]

    faces = dot(jnp.concatenate(high, axis=1).astype(BF16), taken[:, : 4 * side])
    in_y = faces[:, :pair].reshape(3 * EX, EY, ez, pair)
    wall = jnp.zeros((3 * EX, 1, ez, pair), F32)
    beside_y = jnp.where(
        first,
        jnp.concatenate([wall, in_y[:, :-1]], axis=1),
        jnp.concatenate([in_y[:, 1:], wall], axis=1),
    ).reshape(3 * rows, pair)
    in_z = faces[:, pair:].reshape(3 * EX * EY, ez, pair)
    beside_z = jnp.where(
        first, pltpu.roll(in_z, 1, 1), pltpu.roll(in_z, ez - 1, 1)
    ).reshape(3 * rows, pair)
    beside = jnp.concatenate([beside_y, beside_z], axis=1).astype(BF16)

    def three(value):
        top, rest = split_two(value)
        return jnp.concatenate([top, rest, top], axis=1)

    mirror = jnp.concatenate([swap[tiles - 1 - j] for j in range(tiles // 2)], axis=1)
    near = jnp.concatenate(tile[: tiles // 2], axis=1)
    from_even = dot(three(near + mirror), even[...])
    from_odd = dot(three(near - mirror), odd[...])

    for j in range(tiles):
        cols = slice(j * pair, (j + 1) * pair)
        low = tile[j] - high[j]
        low_swap = swap[j] - high_swap[j]
        one = jnp.concatenate([jnp.where(first, high[j], low_swap), high[j]], axis=1).astype(BF16)
        two = jnp.concatenate([jnp.where(first, high_swap[j], low), high_swap[j]], axis=1).astype(BF16)
        got_one = dot(one, across[:, : 4 * side])
        got_two = dot(two, across[:, 4 * side :])
        slope_y = jnp.where(first, got_one[:, :pair], got_two[:, :pair])
        slope_z = got_one[:, pair:] + got_two[:, pair:]
        curve = jnp.where(first, got_two[:, :pair], got_one[:, :pair])
        if j < tiles // 2:
            at = slice(j * pair, (j + 1) * pair)
            up = slice(half + j * pair, half + (j + 1) * pair)
            slope_x = from_odd[:, at] + from_even[:, at]
            curve = pltpu.roll(curve, side, 1) + (from_even[:, up] + from_odd[:, up])
        else:
            k = tiles - 1 - j
            at = slice(k * pair, (k + 1) * pair)
            up = slice(half + k * pair, half + (k + 1) * pair)
            slope_x = pltpu.roll(from_odd[:, at] - from_even[:, at], side, 1)
            curve = pltpu.roll(curve + (from_even[:, up] - from_odd[:, up]), side, 1)
        value = tile[j] * keep[:, cols] + curve
        value = value + FACE_RATE * dot(beside, placed[:, cols])
        value = value.reshape(3, rows, pair)
        for d, slope in enumerate((slope_x, slope_y, slope_z)):
            value = value + slope.reshape(3, rows, pair) * tile[j].reshape(3, rows, pair)[d][None]
        layer = EY * ez
        if j == 0:
            beyond = swap[tiles - 1].reshape(3, rows, pair)[:, :layer]
            beyond = jnp.where(first, FACE_RATE * beyond, 0.0)
            value = jnp.concatenate([value[:, :layer], value[:, layer:] + beyond], axis=1)
        if j == tiles - 1:
            beyond = swap[0].reshape(3, rows, pair)[:, layer:]
            beyond = jnp.where(first, 0.0, FACE_RATE * beyond)
            value = jnp.concatenate([value[:, :layer] + beyond, value[:, layer:]], axis=1)
        part[:, :, cols] = value


def join_kernel(part, pair_x, cross_x, pair_y, cross_y, tabs, field, *edges):
    ez = part.shape[1] // (EX * EY)
    add_edges(part, pair_x, cross_x, pair_y, cross_y, tabs, field, ez)
    write_edges(field, tabs, edges, ez)


def encode_kernel(
    part, pair_x, cross_x, pair_y, cross_y, tabs, wall, w_encode,
    field, snapshot, target, z1, h1,
):
    ez = part.shape[1] // (EX * EY)
    add_edges(part, pair_x, cross_x, pair_y, cross_y, tabs, field, ez)
    high0, low0 = split_two(field[0])
    high2, low2 = split_two(field[2])
    snap = jnp.concatenate([high0, high2], axis=1)
    snapshot[...] = snap
    target[...] = (
        dot(jnp.concatenate([high0, low0, high0], axis=1), wall[:, : 2 * NP * NP])
        + dot(jnp.concatenate([high2, low2, high2], axis=1), wall[:, 2 * NP * NP :])
    ).astype(BF16)
    hidden = dot(snap, w_encode[...])
    z1[...] = hidden
    h1[...] = (hidden * jax.nn.sigmoid(hidden)).astype(BF16)


def same_kernel(value, out):
    out[...] = value[...]


def restore_kernel(field, back, after_this, out, done):
    for c in range(3):
        out[c] = moved(back[...], field[c])
    done[...] = jnp.zeros_like(done)


def silu_grad(value):
    sigma = jax.nn.sigmoid(value)
    return sigma * (1.0 + value * (1.0 - sigma))


def with_layers(own, pair, cross, ez, groups):
    channels = own.shape[-1]
    place = lax.axis_index("grp")
    grid = own[...].astype(F32).reshape(EX, EY, ez, channels)
    even = is_even("grp")
    pair = pair[...].reshape(EX, EY, ez, channels).astype(F32)
    cross = cross[...].reshape(EX, EY, ez, channels).astype(F32)
    before = jnp.where(even, cross[:, EY - 1 :], pair[:, EY - 1 :])
    after = jnp.where(even, pair[:, :1], cross[:, :1])
    before = jnp.where(place > 0, before, 0.0)
    after = jnp.where(place < groups - 1, after, 0.0)
    return jnp.concatenate([before, grid, after], axis=1)


def along_span(grid, ez, groups):
    shape = grid.shape
    rows = int(np.prod(shape[:-1]))
    crop = ez // groups
    flat = grid.reshape(rows, shape[-1])
    place = lax.rem(lax.broadcasted_iota(jnp.int32, (rows, 1), 0), crop)
    before = jnp.where(place == 0, 0.0, pltpu.roll(flat, 1, 0))
    after = jnp.where(place == crop - 1, 0.0, pltpu.roll(flat, rows - 1, 0))
    return before.reshape(shape), after.reshape(shape)


def tap_sum(taken, w_conv, dy):
    channels = w_conv.shape[1]
    first = 3 * dy
    rows = taken.shape[1]

    def times(value, start):
        return dot(value, w_conv[start + first : start + first + 3].reshape(-1, channels))

    both = times(taken.reshape(EX * rows, taken.shape[2]), 9)
    return both + jnp.concatenate([times(taken[1], 18), times(taken[0], 0)], axis=0)


def centre_kernel(groups, h1, w_conv, z2):
    rows, channels = h1.shape
    ez = rows // (EX * EY)
    grid = h1[...].astype(F32).reshape(EX, EY, ez, channels)
    before, after = along_span(grid, ez, groups)
    taken = jnp.concatenate([before, grid, after], axis=-1).astype(BF16)
    z2[...] = tap_sum(taken.reshape(EX, rows // EX, 3 * channels), w_conv, 1)


def forward_kernel(groups, total, z2, h1, pair, cross, w_conv, w_head, target, dz2, h2, resid, padded):
    rows, channels = h1.shape
    ez = rows // (EX * EY)
    grid = with_layers(h1, pair, cross, ez, groups)
    before, after = along_span(grid, ez, groups)
    padded[...] = jnp.concatenate([before, grid, after], axis=-1).astype(BF16)
    hidden = z2[...]
    for dy in (0, 2):
        taken = padded[:, dy : dy + EY].reshape(EX, rows // EX, 3 * channels)
        hidden = hidden + tap_sum(taken, w_conv, dy)
    act = (hidden * jax.nn.sigmoid(hidden)).astype(BF16)
    output = dot(act, w_head[...])
    miss = (LOSS_WEIGHT * (output - target[...].astype(F32)) / total).astype(BF16)
    h2[...] = act
    resid[...] = miss
    dz2[...] = (dot_nt(miss, w_head[...]) * silu_grad(hidden)).astype(BF16)


def tap_sum_back(shifted, w_conv, dy):
    total = 0.0
    for dz, taken in enumerate(shifted):
        tap = 3 * dy + dz
        both = dot_nt(taken.reshape(-1, taken.shape[2]), w_conv[9 + tap])
        ahead_x = dot_nt(taken[0], w_conv[18 + tap])
        behind_x = dot_nt(taken[1], w_conv[tap])
        total = total + both + jnp.concatenate([behind_x, ahead_x], axis=0)
    return total


def centre_back_kernel(groups, dz2, w_conv, h2, resid, dh1, head):
    rows, channels = dz2.shape
    ez = rows // (EX * EY)
    grid = dz2[...].astype(F32).reshape(EX, EY, ez, channels)
    before, after = along_span(grid, ez, groups)
    shifted = [
        part.astype(BF16).reshape(EX, rows // EX, channels) for part in (after, grid, before)
    ]
    dh1[...] = tap_sum_back(shifted, w_conv, 1)
    head[...] = dot(h2[...].astype(F32).T.astype(BF16), resid[...])


def back_kernel(groups, dh1, head, dz2, pair, cross, w_conv, z1, snapshot, kept, sent, out):
    rows, channels = dz2.shape
    ez = rows // (EX * EY)
    grid = with_layers(dz2, pair, cross, ez, groups)
    before, after = along_span(grid, ez, groups)
    shifted = [part.astype(BF16) for part in (after, grid, before)]
    features = snapshot.shape[1]
    out[:, features:] = head[...]
    total = dh1[...]
    for dy in (0, 2):
        taken = [
            part[:, 2 - dy : 2 - dy + EY].reshape(EX, rows // EX, channels) for part in shifted
        ]
        total = total + tap_sum_back(taken, w_conv, dy)
    dz1 = total * silu_grad(z1[...])
    out[:, :features] = dot(dz1.T.astype(BF16), snapshot[...])
    quarter = channels // groups
    place = lax.axis_index("grp")
    for k in range(groups):
        piece = sent if k % 2 else kept
        at = pl.multiple_of(jnp.bitwise_xor(place, k) * quarter, quarter)
        piece[k // 2] = out[pl.ds(at, quarter)].astype(piece.dtype)


def core_kernel(kept, got, out_kept, out_sent):
    out_kept[...] = kept[0] + got[0].astype(F32)
    out_sent[...] = (kept[1] + got[1].astype(F32)).astype(BF16)


def taps_kernel(
    groups, sims, h_own, h_one, h_two, h_three, d_own, d_one, d_two, d_three, after_this, *refs
):
    out, h_all, r_all = refs[-3:]
    rows, channels = h_own.shape
    ez = rows // (EX * EY)
    quarter = channels // groups
    crop = ez // groups
    place = lax.axis_index("grp")
    layer = EY * ez
    taken = 3 * quarter
    slot = lax.broadcasted_iota(jnp.int32, (taken, channels), 0)
    channel = lax.broadcasted_iota(jnp.int32, (taken, channels), 1)
    chosen = jnp.where(channel == place * quarter + lax.rem(slot, quarter), 1.0, 0.0).astype(BF16)
    pairs = ((h_own, d_own), (h_one, d_one), (h_two, d_two), (h_three, d_three))
    for k, (h, d) in enumerate(pairs):
        at = jnp.bitwise_xor(place, k)
        mine = dot_nt(chosen, d[...])
        for x in range(EX):
            h_all[x, at] = h[x * layer : (x + 1) * layer]
            r_all[x, at] = mine[:, x * layer : (x + 1) * layer]
    deep = groups * layer
    turned = jnp.concatenate([r_all[x, g] for x in range(EX) for g in range(groups)], axis=1)
    spot = lax.broadcasted_iota(jnp.int32, (1, EX * deep), 1)
    after = pltpu.roll(turned[:quarter], EX * deep - 1, 1)
    after = jnp.where(lax.rem(spot, crop) == crop - 1, 0.0, after)
    before = pltpu.roll(turned[2 * quarter :], 1, 1)
    before = jnp.where(lax.rem(spot, crop) == 0, 0.0, before)
    turned = jnp.concatenate([after, turned[quarter : 2 * quarter], before], axis=0)
    spot = lax.rem(spot, deep)
    up = jnp.where(spot >= deep - ez, 0.0, pltpu.roll(turned, EX * deep - ez, 1))
    down = jnp.where(spot < ez, 0.0, pltpu.roll(turned, ez, 1))
    whole = h_all[...].reshape(EX * deep, channels)
    for dy, side in enumerate((up, turned, down)):
        side = side.astype(BF16)
        for dx in range(3):
            if dx == 0:
                got = dot(side[:, deep:], whole[:deep])
            elif dx == 1:
                got = dot(side, whole)
            else:
                got = dot(side[:, :deep], whole[deep:])
            start = (9 * dx + 3 * dy) * quarter
            out[start : start + taken] = got
    me = lax.rem(lax.axis_index("sim"), sims)
    piece_rows = 27 * quarter // sims
    for k, piece in enumerate(refs[:-3]):
        at = pl.multiple_of(jnp.bitwise_xor(me, k) * piece_rows, 8)
        piece[...] = out[pl.ds(at, piece_rows)].astype(piece.dtype)


def dense_kernel(kept, got, *refs):
    out_kept, out_sent = refs[-3:-1]
    for source, target in zip(refs[:1], refs[-1:]):
        target[...] = source[...]
    total = kept[...] + got[...].astype(F32)
    grid = total.reshape(2, 2, kept.shape[0] // 4, kept.shape[1])
    odd = lax.rem(lax.div(lax.axis_index("sim"), 2), 2) == 1
    out_kept[...] = jnp.where(odd, grid[:, 1], grid[:, 0])
    out_sent[...] = jnp.where(odd, grid[:, 0], grid[:, 1]).astype(BF16)


def half_kernel(scale, kept, got, out_kept, out_sent):
    total = kept[...] + got[...].astype(F32)
    upper = lax.rem(lax.div(lax.axis_index("sim"), scale), 2) == 1
    out_kept[...] = jnp.where(upper, total[1], total[0])
    out_sent[...] = jnp.where(upper, total[0], total[1]).astype(BF16)


def packed(taps, dense):
    channels = taps.shape[1]
    parts = [taps]
    for start in range(0, dense.shape[1], channels):
        piece = dense[:, start : start + channels]
        short_by = channels - piece.shape[1]
        if short_by:
            piece = jnp.concatenate([piece, jnp.zeros((piece.shape[0], short_by), F32)], axis=1)
        parts.append(piece)
    return jnp.concatenate(parts, axis=0)


def sum_kernel(parts, kept, *refs):
    total = kept[...]
    for other in refs[: parts - 1]:
        total = total + other[...].astype(F32)
    refs[-1][...] = total.astype(BF16)


def share_kernel(taps, one, two, three, dense, dense_in, after_this, out):
    total = taps[...]
    for other in (one, two, three):
        total = total + other[...].astype(F32)
    out[...] = packed(total, dense[...] + dense_in[...].astype(F32)).astype(BF16)


def place_kernel(masks, count, *refs):
    shares = refs[: len(masks)]
    outs = refs[-7:-4]
    held = refs[-4:-1]
    sems = refs[-1]
    channels = shares[0].shape[1]
    tap_rows, own_rows = [out.shape[0] // count for out in outs[:2]]
    features = outs[1].shape[1]
    me = lax.axis_index("sim")
    copies = []
    for i, (mask, share) in enumerate(zip(masks, shares)):
        source = jnp.bitwise_xor(me, mask)
        value = share[...].astype(F32)
        held[0][i] = value[:tap_rows]
        start = tap_rows
        for first in range(0, features, channels):
            held[1][i, :, first : first + channels] = value[start : start + own_rows]
            start += own_rows
        held[2][i] = value[start : start + own_rows, : outs[2].shape[1]]
        for j, out in enumerate(outs):
            size = tap_rows if j == 0 else own_rows
            rows = pl.ds(pl.multiple_of(source * size, 8), size)
            copy = pltpu.make_async_copy(held[j].at[i], out.at[rows], sems.at[i, j])
            copy.start()
            copies.append(copy)
    for copy in copies:
        copy.wait()


def placed_shares(shares, shapes, count):
    outs = ()
    groups = [(first, first + 1) for first in range(0, count - 4, 2)]
    for masks in groups + [(count - 4, count - 3, count - 2), (count - 1,)]:
        tap_rows, own_rows = [shape.shape[0] // count for shape in shapes[:2]]
        sizes = (tap_rows, own_rows, own_rows)
        held = [
            pltpu.VMEM((len(masks), size, shape.shape[1]), F32)
            for size, shape in zip(sizes, shapes)
        ]
        anywhere = pl.BlockSpec(memory_space=pl.ANY)
        outs = pl.pallas_call(
            functools.partial(place_kernel, masks, count),
            out_shape=shapes,
            in_specs=[pl.BlockSpec(memory_space=pltpu.VMEM)] * len(masks) + [anywhere] * len(outs),
            out_specs=(anywhere,) * 3,
            scratch_shapes=held + [pltpu.SemaphoreType.DMA((len(masks), 3))],
            input_output_aliases={len(masks) + i: i for i in range(len(outs))},
            compiler_params=pltpu.CompilerParams(vmem_limit_bytes=VMEM_LIMIT),
            cost_estimate=pl.CostEstimate(flops=1000, bytes_accessed=1000, transcendentals=0),
        )(*[shares[mask] for mask in masks], *outs)
    return outs


def call(kernel, outs, scratch=(), in_hbm=(), inputs=0, flops=1000):
    specs = {}
    if in_hbm:
        specs["in_specs"] = [
            pl.BlockSpec(memory_space=pl.ANY if i in in_hbm else pltpu.VMEM) for i in range(inputs)
        ]
    return pl.pallas_call(
        kernel,
        out_shape=outs,
        scratch_shapes=list(scratch),
        compiler_params=pltpu.CompilerParams(vmem_limit_bytes=VMEM_LIMIT),
        cost_estimate=pl.CostEstimate(flops=flops, bytes_accessed=1000, transcendentals=0),
        **specs,
    )


def shaped(shape, kind):
    return jax.ShapeDtypeStruct(shape, kind)


def swapped(value, axis, mask):
    count = lax.axis_size(axis)
    return lax.ppermute(value, axis, [(i, i ^ mask) for i in range(count)])


def crossed(value, axis, periodic):
    count = lax.axis_size(axis)
    route = [(i, i + 1 if i % 2 else i - 1) for i in range(count)]
    if periodic:
        route = [(i, j % count) for i, j in route]
    return lax.ppermute(value, axis, [(i, j) for i, j in route if 0 <= j < count])


def exchanged(edges):
    pair_x, cross_x, pair_y, cross_y = edges
    cross_x = crossed(cross_x, "sim", True)
    pair_x = swapped(pair_x, "sim", 1)
    cross_y = crossed(cross_y, "grp", False)
    pair_y = swapped(pair_y, "grp", 1)
    return pair_x, cross_x, pair_y, cross_y


def gathered(share, sims):
    got = {0: share}
    for k in range(2, sims, 2):
        got[k] = swapped(share, "sim", k)
    for k in range(0, sims, 2):
        got[k + 1] = swapped(got[k], "sim", 1)
    return [got[k] for k in range(sims)]


def body(velocity, slot_of, w_encode, w_conv, w_head):
    stencil, wall = (jnp.asarray(table) for table in element_tables())
    block = velocity[0, 0]
    slots = slot_of[0]
    rows, width = block.shape[1:]
    ez = rows // (EX * EY)
    channels = w_encode.shape[1]
    features = w_encode.shape[0]
    outputs = w_head.shape[1]
    sims = lax.axis_size("sim")
    groups = lax.axis_size("grp")
    total = rows * sims * groups
    quarter = channels // groups

    whole = shaped((3, rows, width), F32)
    x_edge = shaped((3, EY * ez // 2, 2 * NP * NP), BF16)
    y_edge = shaped((3, ez, 2 * NP * NP), BF16)
    edge_shapes = (x_edge, x_edge, y_edge, y_edge)

    order, back, tabs = call(
        order_kernel,
        (
            shaped((rows, rows), BF16),
            shaped((rows, rows), BF16),
            shaped((4, width, 2 * NP * NP), BF16),
        ),
        flops=4 * 10**9,
    )(slots)
    field, *edges = call(prepare_kernel, (whole,) + edge_shapes, flops=4 * 10**9)(block, order, tabs)
    halos = exchanged(edges)
    part = call(inside_kernel, whole)(field, stencil)
    field, *edges = call(join_kernel, (whole,) + edge_shapes)(part, *halos, tabs)
    halos = exchanged(edges)
    part = call(inside_kernel, whole)(field, stencil)
    field, snapshot, target, z1, h1 = call(
        encode_kernel,
        (
            whole,
            shaped((rows, features), BF16),
            shaped((rows, outputs), BF16),
            shaped((rows, channels), F32),
            shaped((rows, channels), BF16),
        ),
    )(part, *halos, tabs, wall, w_encode)

    h_three = swapped(h1, "grp", 3)
    h_one = swapped(h1, "grp", 1)
    h_two = swapped(h_three, "grp", 1)
    rows_bf = shaped((rows, channels), BF16)
    square = shaped((rows, channels), F32)
    z2 = call(functools.partial(centre_kernel, groups), square, flops=2 * 10**9)(h1, w_conv)
    dz2, h2, resid = call(
        functools.partial(forward_kernel, groups, total),
        (rows_bf, rows_bf, shaped((rows, outputs), BF16)),
        (pltpu.VMEM((EX, EY + 2, ez, 3 * channels), BF16),),
    )(z2, h1, h_one, call(same_kernel, rows_bf, flops=2 * 10**9)(h_three), w_conv, w_head, target)

    d_three = swapped(dz2, "grp", 3)
    d_one = swapped(dz2, "grp", 1)
    d_two = swapped(d_three, "grp", 1)
    wide = features + outputs
    pair = (groups // 2, quarter, wide)
    dh1, head = call(
        functools.partial(centre_back_kernel, groups),
        (square, shaped((channels, outputs), F32)),
        flops=2 * 10**9,
    )(dz2, w_conv, h2, resid)
    e_kept, e_sent = call(
        functools.partial(back_kernel, groups),
        (shaped(pair, F32), shaped(pair, BF16)),
        (pltpu.VMEM((channels, wide), F32),),
    )(dh1, head, dz2, d_one, call(same_kernel, rows_bf, flops=2 * 10**9)(d_three), w_conv, z1, snapshot)
    e_got = swapped(e_sent, "grp", 1)
    e_kept, e_sent = call(core_kernel, (shaped(pair[1:], F32), shaped(pair[1:], BF16)))(e_kept, e_got)
    e_got = swapped(e_sent, "grp", 2)
    tap_rows = 27 * quarter // sims
    own_rows = quarter // sims
    direct = sims == 8
    if direct:
        pieces = [shaped((tap_rows, channels), BF16 if k % 2 else F32) for k in range(sims)]
    else:
        pieces = [shaped((27 * quarter, channels), BF16)]
    taps = call(
        functools.partial(taps_kernel, groups, sims if direct else 1),
        tuple(pieces),
        (
            pltpu.VMEM((27 * quarter, channels), F32),
            pltpu.VMEM((EX, groups, EY * ez, channels), BF16),
            pltpu.VMEM((EX, groups, 3 * quarter, EY * ez), F32),
        ),
        in_hbm=(8,),
        inputs=9,
    )(h1, h_one, h_two, h_three, dz2, d_one, d_two, d_three, e_kept)
    restore = call(restore_kernel, (whole, shaped((8, 128), F32)), in_hbm=(2,), inputs=3)
    if direct:
        tap_piece = shaped((tap_rows, channels), BF16)
        part = (2, 2 * own_rows, wide)
        e_kept, e_sent, *later = call(
            dense_kernel, (shaped(part, F32), shaped(part, BF16)) + (tap_piece,)
        )(e_kept, e_got, taps[1])
        e_got = swapped(e_sent, "sim", 2)
        taps_in = {k: swapped(taps[k + 1], "sim", 1) for k in (6, 4, 2)}
        taps_in.update((k, swapped(piece, "sim", 1)) for k, piece in zip((0,), later))
        add_two = call(functools.partial(sum_kernel, 2), tap_piece)
        add_three = call(functools.partial(sum_kernel, 3), tap_piece)
        six = swapped(add_two(taps[6], taps_in[6], e_sent), "sim", 2)
        part = shaped((2 * own_rows, wide), F32), shaped((2 * own_rows, wide), BF16)
        e_kept, e_sent = call(functools.partial(half_kernel, 4), part)(e_kept, e_got)
        e_got = swapped(e_sent, "sim", 4)
        two = add_two(taps[2], taps_in[2], e_sent)
        four = swapped(add_three(taps[4], taps_in[4], six, two), "sim", 4)
        two = swapped(two, "sim", 2)
        part = shaped((own_rows, wide), F32), shaped((own_rows, wide), BF16)
        e_kept, e_sent = call(functools.partial(half_kernel, 1), part, flops=4 * 10**9)(
            e_kept.reshape(2, own_rows, wide), e_got.reshape(2, own_rows, wide)
        )
        velocity_next, done = restore(field, back, e_sent)
        e_got = swapped(e_sent, "sim", 1)
        blocks = -(-wide // channels)
        share = call(share_kernel, shaped((tap_rows + blocks * own_rows, channels), BF16))(
            taps[0], taps_in[0], two, four, e_kept, e_got, done
        )
        shares = gathered(share, sims)
        shapes = (
            shaped((27 * quarter, channels), F32),
            shaped((quarter, features), F32),
            shaped((quarter, outputs), F32),
        )
        taps, encode, head = placed_shares(shares, shapes, sims)
    else:
        taps = taps[0].reshape(sims, tap_rows, channels)
        taps = lax.all_to_all(taps, "sim", 0, 0, tiled=True)
        taps = jnp.sum(taps.astype(F32), axis=0).astype(BF16)
        taps = lax.all_gather(taps, "sim").astype(F32)
        velocity_next, done = restore(field, back, e_kept)
        dense = e_kept + e_got.astype(F32)
        dense = dense.astype(BF16).reshape(sims, own_rows, wide)
        dense = lax.all_to_all(dense, "sim", 0, 0, tiled=True)
        dense = jnp.sum(dense.astype(F32), axis=0).astype(BF16)
        dense = lax.all_gather(dense, "sim").reshape(quarter, wide).astype(F32)
        encode = dense[:, :features]
        head = dense[:, features:]
    taps = taps.reshape(27, quarter, channels)
    return velocity_next[None, None], encode.T, taps.transpose(0, 2, 1), head


def solution(mesh):
    placed = (P("sim", "grp", None, None, None), P("sim", "grp", None), P(), P(), P())
    return jax.shard_map(
        body,
        mesh=mesh,
        in_specs=placed,
        out_specs=(
            P("sim", "grp", None, None, None),
            P(None, "grp"),
            P(None, None, "grp"),
            P("grp", None),
        ),
        check_vma=False,
    )
```

```python
import functools

import jax
import jax.numpy as jnp
import ml_dtypes
import numpy as np
from jax import lax
from jax.experimental import pallas as pl
from jax.experimental.pallas import tpu as pltpu
from jax.sharding import PartitionSpec as P

NP = 8
EX = 2
EY = 4
STEPS = 2

VISCOSITY = 0.2
TIME_STEP = 0.005
PENALTY = 100.0
LOSS_WEIGHT = 64.0
FACE_RATE = TIME_STEP * VISCOSITY * PENALTY

F32 = jnp.float32
BF16 = jnp.bfloat16
VMEM_LIMIT = 16 * 1024 * 1024


def derivative_matrix(count):
    places = np.arange(count)
    points = -np.cos(np.pi * places / (count - 1))
    weights = np.where(places % 2 == 0, 1.0, -1.0)
    weights[0] = weights[0] * 0.5
    weights[count - 1] = weights[count - 1] * 0.5
    identity = np.eye(count)
    spread = points[:, None] - points[None, :] + identity
    deriv = weights[None, :] / weights[:, None] / spread
    deriv = deriv * (1.0 - identity)
    return deriv - identity * deriv.sum(axis=1)[:, None]


def short(table):
    return np.asarray(table, np.float32).astype(ml_dtypes.bfloat16)


def in_three(table):
    table = np.asarray(table, np.float32)
    high = table.astype(ml_dtypes.bfloat16)
    low = (table - high.astype(np.float32)).astype(ml_dtypes.bfloat16)
    return np.concatenate([high, high, low], axis=0)


@functools.lru_cache(maxsize=None)
def element_tables():
    count = NP
    deriv = derivative_matrix(count)
    single = np.eye(count)
    square = np.eye(count * count)
    grid = np.arange(count**3).reshape(count, count, count)
    final = count - 1
    faces = [
        grid[0].ravel(),
        grid[final].ravel(),
        grid[:, 0].ravel(),
        grid[:, final].ravel(),
        grid[:, :, 0].ravel(),
        grid[:, :, final].ravel(),
    ]

    def pick(which):
        table = np.zeros((count**3, count * count))
        table[which, np.arange(count * count)] = 1.0
        return table

    picks = [pick(which) for which in faces]
    none = np.zeros_like(picks[0])
    taken = np.concatenate([picks[i] for i in (3, 2, 5, 4)], axis=1)
    placed = np.concatenate(picks[2:], axis=1).T
    bottom = np.zeros((count**3, count * count))
    for first in range(count):
        for middle in range(count):
            for inner in range(count):
                bottom[grid[first, middle, inner], first * count + inner] = (
                    VISCOSITY * deriv[0, middle]
                )
    mirrored = np.concatenate([deriv, deriv @ deriv], axis=0)[:, ::-1].reshape(2, count, count)
    straight = np.stack([deriv, deriv @ deriv])
    half = count // 2
    scale = np.array([-TIME_STEP, TIME_STEP * VISCOSITY])[:, None, None]

    def along_first(sign):
        mixed = (0.5 * scale * (straight + sign * mirrored))[:, :half, :half]
        return in_three(np.concatenate([np.kron(part.T, square) for part in mixed], axis=1))

    small_y = np.kron(deriv, single)
    small_z = np.kron(single, deriv)
    curved = TIME_STEP * VISCOSITY * (small_y @ small_y + small_z @ small_z).T
    small_y = -TIME_STEP * small_y.T
    small_z = -TIME_STEP * small_z.T
    blank = np.zeros_like(curved)

    def across(blocks):
        table = in_three(np.concatenate(blocks, axis=1))
        return np.concatenate([table, np.zeros((count * count, table.shape[1]), table.dtype)], axis=0)

    both = np.concatenate(
        [
            across([small_y, curved, small_z, blank]),
            across([curved, small_y, blank, small_z]),
        ],
        axis=1,
    )
    filled = np.zeros((count**3, count**3 - taken.shape[1]))
    stencil = np.concatenate(
        [
            along_first(1.0),
            along_first(-1.0),
            both,
            short(placed),
            short(np.concatenate([taken, filled], axis=1)),
        ],
        axis=0,
    )
    wall = in_three(np.concatenate([bottom, none, none, bottom], axis=1))
    return stencil, wall


def dot(left, right):
    return jnp.dot(left, right, preferred_element_type=F32)


def dot_nt(left, right):
    return lax.dot_general(left, right, (((1,), (1,)), ((), ())), preferred_element_type=F32)


def split_two(value):
    high = value.astype(BF16)
    return high, (value - high.astype(F32)).astype(BF16)


def moved(order, value):
    high = value.astype(BF16)
    rest = value - high.astype(F32)
    middle, low = split_two(rest)
    return dot(order, high) + dot(order, middle) + dot(order, low)


def slot_matrix(slots):
    count = slots.shape[1]
    rows = lax.broadcasted_iota(jnp.int32, (count, count), 0)
    return jnp.where(rows == slots, 1.0, 0.0).astype(F32)


def layer_rows(field, x, layer, ez):
    start = (x * EY + layer) * ez
    return field[:, start : start + ez].reshape(3 * ez, field.shape[2])


def edge_tables():
    side = NP * NP
    point = lax.broadcasted_iota(jnp.int32, (NP * side, 2 * side), 0)
    lane = lax.broadcasted_iota(jnp.int32, (NP * side, 2 * side), 1)
    middle = lax.rem(lax.div(point, NP), NP)
    place = lax.div(point, side) * NP + lax.rem(point, NP)

    def table(level, shift):
        return jnp.where((middle == level) & (lane == place + shift), 1.0, 0.0).astype(BF16)

    return table(0, 0), table(0, side), table(NP - 1, 0), table(NP - 1, side)


def order_kernel(slots, order, back, tabs):
    matrix = slot_matrix(slots[...])
    back[...] = matrix.astype(BF16)
    order[...] = matrix.T.astype(BF16)
    for i, table in enumerate(edge_tables()):
        tabs[i] = table


def is_even(axis):
    return lax.rem(lax.axis_index(axis), 2) == 0


def write_edges(field, tabs, outs, ez):
    pair_x, cross_x, pair_y, cross_y = outs
    side = NP * NP
    half = EY * ez // 2
    last = NP * side - side
    even_x = is_even("sim")
    even_y = is_even("grp")
    near = field[:, 0 : 2 * half, 0 : 2 * side][:, :, :side]
    far = field[:, 2 * half : 4 * half, last - side :][:, :, side:]
    to_left = jnp.concatenate([near[:, :half], near[:, half:]], axis=2)
    to_right = jnp.concatenate([far[:, :half], far[:, half:]], axis=2)
    pair_x[...] = jnp.where(even_x, to_right, to_left).astype(BF16)
    cross_x[...] = jnp.where(even_x, to_left, to_right).astype(BF16)
    to_below, to_above = [
        dot(layer_rows(field, 0, layer, ez).astype(BF16), tabs[at])
        + dot(layer_rows(field, 1, layer, ez).astype(BF16), tabs[at + 1])
        for layer, at in ((0, 0), (EY - 1, 2))
    ]
    pair_y[...] = jnp.where(even_y, to_above, to_below).astype(BF16).reshape(pair_y.shape)
    cross_y[...] = jnp.where(even_y, to_below, to_above).astype(BF16).reshape(cross_y.shape)


def add_edges(part, pair_x, cross_x, pair_y, cross_y, tabs, field, ez):
    side = NP * NP
    half = EY * ez // 2
    width = NP * side
    even_x = is_even("sim")
    even_y = is_even("grp")
    pair = FACE_RATE * pair_x[...].astype(F32)
    cross = FACE_RATE * cross_x[...].astype(F32)
    left = jnp.where(even_x, cross, pair)
    right = jnp.where(even_x, pair, cross)
    pair = pair_y[...].astype(F32)
    cross = cross_y[...].astype(F32)
    below = jnp.where(even_y, cross, pair).astype(BF16).reshape(3 * ez, 2 * side)
    above = jnp.where(even_y, pair, cross).astype(BF16).reshape(3 * ez, 2 * side)
    first = lax.broadcasted_iota(jnp.int32, (1, 1, 2 * side), 2) < side

    field[...] = part[...]
    turned = pltpu.roll(left, side, 2)
    field[:, 0:half, : 2 * side] += jnp.where(first, left, 0.0)
    field[:, half : 2 * half, : 2 * side] += jnp.where(first, turned, 0.0)
    turned = pltpu.roll(right, side, 2)
    field[:, 2 * half : 3 * half, width - 2 * side :] += jnp.where(first, 0.0, turned)
    field[:, 3 * half : 4 * half, width - 2 * side :] += jnp.where(first, 0.0, right)
    for x in range(EX):
        for layer, value, at in ((0, below, 0), (EY - 1, above, 2)):
            start = (x * EY + layer) * ez
            more = FACE_RATE * dot_nt(value, tabs[at + x])
            field[:, start : start + ez] += more.reshape(3, ez, width)


def prepare_kernel(vel, order, tabs, field, *edges):
    ez = vel.shape[1] // (EX * EY)
    for c in range(3):
        field[c] = moved(order[...], vel[c])
    write_edges(field, tabs, edges, ez)


def face_count(width):
    point = lax.broadcasted_iota(jnp.int32, (1, width), 1)
    count = jnp.zeros((1, width), F32)
    for stride in (NP * NP, NP, 1):
        index = lax.rem(lax.div(point, stride), NP)
        count = count + jnp.where((index == 0) | (index == NP - 1), 1.0, 0.0)
    return count


def inside_kernel(field, stencil, part):
    rows = field.shape[1]
    width = field.shape[2]
    ez = rows // (EX * EY)
    half = width // 2
    side = NP * NP
    pair = 2 * side
    tiles = width // pair
    even = stencil.at[0 : 3 * half]
    odd = stencil.at[3 * half : 6 * half]
    start = 6 * half
    across = stencil.at[start : start + 4 * side]
    placed = stencil.at[start + 4 * side : start + 8 * side]
    taken = stencil.at[start + 8 * side : start + 8 * side + width]
    keep = 1.0 - FACE_RATE * face_count(width)
    lanes = lax.broadcasted_iota(jnp.int32, (1, pair), 1)
    first = lanes < side
    tile = [field[:, :, j * pair : (j + 1) * pair].reshape(3 * rows, pair) for j in range(tiles)]
    swap = [pltpu.roll(value, side, 1) for value in tile]

    high = [value.astype(BF16).astype(F32) for value in tile]
    high_swap = [value.astype(BF16).astype(F32) for value in swap]

    faces = dot(jnp.concatenate(high, axis=1).astype(BF16), taken[:, : 4 * side])
    in_y = faces[:, :pair].reshape(3 * EX, EY, ez, pair)
    wall = jnp.zeros((3 * EX, 1, ez, pair), F32)
    beside_y = jnp.where(
        first,
        jnp.concatenate([wall, in_y[:, :-1]], axis=1),
        jnp.concatenate([in_y[:, 1:], wall], axis=1),
    ).reshape(3 * rows, pair)
    in_z = faces[:, pair:].reshape(3 * EX * EY, ez, pair)
    beside_z = jnp.where(
        first, pltpu.roll(in_z, 1, 1), pltpu.roll(in_z, ez - 1, 1)
    ).reshape(3 * rows, pair)
    beside = jnp.concatenate([beside_y, beside_z], axis=1).astype(BF16)

    def three(value):
        top, rest = split_two(value)
        return jnp.concatenate([top, rest, top], axis=1)

    mirror = jnp.concatenate([swap[tiles - 1 - j] for j in range(tiles // 2)], axis=1)
    near = jnp.concatenate(tile[: tiles // 2], axis=1)
    from_even = dot(three(near + mirror), even[...])
    from_odd = dot(three(near - mirror), odd[...])

    for j in range(tiles):
        cols = slice(j * pair, (j + 1) * pair)
        low = tile[j] - high[j]
        low_swap = swap[j] - high_swap[j]
        one = jnp.concatenate([jnp.where(first, high[j], low_swap), high[j]], axis=1).astype(BF16)
        two = jnp.concatenate([jnp.where(first, high_swap[j], low), high_swap[j]], axis=1).astype(BF16)
        got_one = dot(one, across[:, : 4 * side])
        got_two = dot(two, across[:, 4 * side :])
        slope_y = jnp.where(first, got_one[:, :pair], got_two[:, :pair])
        slope_z = got_one[:, pair:] + got_two[:, pair:]
        curve = jnp.where(first, got_two[:, :pair], got_one[:, :pair])
        if j < tiles // 2:
            at = slice(j * pair, (j + 1) * pair)
            up = slice(half + j * pair, half + (j + 1) * pair)
            slope_x = from_odd[:, at] + from_even[:, at]
            curve = pltpu.roll(curve, side, 1) + (from_even[:, up] + from_odd[:, up])
        else:
            k = tiles - 1 - j
            at = slice(k * pair, (k + 1) * pair)
            up = slice(half + k * pair, half + (k + 1) * pair)
            slope_x = pltpu.roll(from_odd[:, at] - from_even[:, at], side, 1)
            curve = pltpu.roll(curve + (from_even[:, up] - from_odd[:, up]), side, 1)
        value = tile[j] * keep[:, cols] + curve
        if j % 2 == 0:
            outer = dot(beside, placed[:, j * pair : (j + 2) * pair])
        value = value + FACE_RATE * outer[:, j % 2 * pair : (j % 2 + 1) * pair]
        value = value.reshape(3, rows, pair)
        for d, slope in enumerate((slope_x, slope_y, slope_z)):
            value = value + slope.reshape(3, rows, pair) * tile[j].reshape(3, rows, pair)[d][None]
        layer = EY * ez
        if j == 0:
            beyond = swap[tiles - 1].reshape(3, rows, pair)[:, :layer]
            beyond = jnp.where(first, FACE_RATE * beyond, 0.0)
            value = jnp.concatenate([value[:, :layer], value[:, layer:] + beyond], axis=1)
        if j == tiles - 1:
            beyond = swap[0].reshape(3, rows, pair)[:, layer:]
            beyond = jnp.where(first, 0.0, FACE_RATE * beyond)
            value = jnp.concatenate([value[:, :layer] + beyond, value[:, layer:]], axis=1)
        part[:, :, cols] = value


def join_kernel(part, pair_x, cross_x, pair_y, cross_y, tabs, field, *edges):
    ez = part.shape[1] // (EX * EY)
    add_edges(part, pair_x, cross_x, pair_y, cross_y, tabs, field, ez)
    write_edges(field, tabs, edges, ez)


def encode_kernel(
    part, pair_x, cross_x, pair_y, cross_y, tabs, w_encode,
    field, snapshot, z1, h1,
):
    ez = part.shape[1] // (EX * EY)
    add_edges(part, pair_x, cross_x, pair_y, cross_y, tabs, field, ez)
    snap = jnp.concatenate([field[0].astype(BF16), field[2].astype(BF16)], axis=1)
    snapshot[...] = snap
    hidden = dot(snap, w_encode[...])
    z1[...] = hidden
    h1[...] = (hidden * jax.nn.sigmoid(hidden)).astype(BF16)


def same_kernel(value, out):
    out[...] = value[...]


def restore_kernel(field, back, after_this, out, done):
    for c in range(3):
        out[c] = moved(back[...], field[c])
    done[...] = jnp.zeros_like(done)


def silu_grad(value):
    sigma = jax.nn.sigmoid(value)
    return sigma * (1.0 + value * (1.0 - sigma))


def with_layers(own, pair, cross, ez, groups):
    channels = own.shape[-1]
    place = lax.axis_index("grp")
    grid = own[...].astype(F32).reshape(EX, EY, ez, channels)
    even = is_even("grp")
    pair = pair[...].reshape(EX, EY, ez, channels).astype(F32)
    cross = cross[...].reshape(EX, EY, ez, channels).astype(F32)
    before = jnp.where(even, cross[:, EY - 1 :], pair[:, EY - 1 :])
    after = jnp.where(even, pair[:, :1], cross[:, :1])
    before = jnp.where(place > 0, before, 0.0)
    after = jnp.where(place < groups - 1, after, 0.0)
    return jnp.concatenate([before, grid, after], axis=1)


def along_span(grid, ez, groups):
    shape = grid.shape
    rows = int(np.prod(shape[:-1]))
    crop = ez // groups
    flat = grid.reshape(rows, shape[-1])
    place = lax.rem(lax.broadcasted_iota(jnp.int32, (rows, 1), 0), crop)
    before = jnp.where(place == 0, 0.0, pltpu.roll(flat, 1, 0))
    after = jnp.where(place == crop - 1, 0.0, pltpu.roll(flat, rows - 1, 0))
    return before.reshape(shape), after.reshape(shape)


def tap_sum(taken, w_conv, dy):
    channels = w_conv.shape[1]
    first = 3 * dy
    rows = taken.shape[1]

    def times(value, start):
        return dot(value, w_conv[start + first : start + first + 3].reshape(-1, channels))

    both = times(taken.reshape(EX * rows, taken.shape[2]), 9)
    return both + jnp.concatenate([times(taken[1], 18), times(taken[0], 0)], axis=0)


def centre_kernel(groups, h1, w_conv, field, wall, z2, target):
    found = 0.0
    for c, start in ((0, 0), (2, 2 * NP * NP)):
        high, low = split_two(field[c])
        three = jnp.concatenate([high, low, high], axis=1)
        found = found + dot(three, wall[:, start : start + 2 * NP * NP])
    target[...] = found.astype(BF16)
    rows, channels = h1.shape
    ez = rows // (EX * EY)
    grid = h1[...].astype(F32).reshape(EX, EY, ez, channels)
    before, after = along_span(grid, ez, groups)
    taken = jnp.concatenate([before, grid, after], axis=-1).astype(BF16)
    z2[...] = tap_sum(taken.reshape(EX, rows // EX, 3 * channels), w_conv, 1)


def forward_kernel(groups, total, z2, h1, pair, cross, w_conv, w_head, target, dz2, h2, resid, padded):
    rows, channels = h1.shape
    ez = rows // (EX * EY)
    grid = with_layers(h1, pair, cross, ez, groups)
    before, after = along_span(grid, ez, groups)
    padded[...] = jnp.concatenate([before, grid, after], axis=-1).astype(BF16)
    hidden = z2[...]
    for dy in (0, 2):
        taken = padded[:, dy : dy + EY].reshape(EX, rows // EX, 3 * channels)
        hidden = hidden + tap_sum(taken, w_conv, dy)
    act = (hidden * jax.nn.sigmoid(hidden)).astype(BF16)
    output = dot(act, w_head[...])
    miss = (LOSS_WEIGHT * (output - target[...].astype(F32)) / total).astype(BF16)
    h2[...] = act
    resid[...] = miss
    dz2[...] = (dot_nt(miss, w_head[...]) * silu_grad(hidden)).astype(BF16)


def tap_sum_back(shifted, w_conv, dy):
    total = 0.0
    for dz, taken in enumerate(shifted):
        tap = 3 * dy + dz
        both = dot_nt(taken.reshape(-1, taken.shape[2]), w_conv[9 + tap])
        ahead_x = dot_nt(taken[0], w_conv[18 + tap])
        behind_x = dot_nt(taken[1], w_conv[tap])
        total = total + both + jnp.concatenate([behind_x, ahead_x], axis=0)
    return total


def centre_back_kernel(groups, dz2, w_conv, h2, resid, dh1, head):
    rows, channels = dz2.shape
    ez = rows // (EX * EY)
    grid = dz2[...].astype(F32).reshape(EX, EY, ez, channels)
    before, after = along_span(grid, ez, groups)
    shifted = [
        part.astype(BF16).reshape(EX, rows // EX, channels) for part in (after, grid, before)
    ]
    dh1[...] = tap_sum_back(shifted, w_conv, 1)
    head[...] = dot(h2[...].astype(F32).T.astype(BF16), resid[...])


def back_kernel(groups, dh1, head, dz2, pair, cross, w_conv, z1, snapshot, kept, sent, out):
    rows, channels = dz2.shape
    ez = rows // (EX * EY)
    grid = with_layers(dz2, pair, cross, ez, groups)
    before, after = along_span(grid, ez, groups)
    shifted = [part.astype(BF16) for part in (after, grid, before)]
    features = snapshot.shape[1]
    out[:, features:] = head[...]
    total = dh1[...]
    for dy in (0, 2):
        taken = [
            part[:, 2 - dy : 2 - dy + EY].reshape(EX, rows // EX, channels) for part in shifted
        ]
        total = total + tap_sum_back(taken, w_conv, dy)
    dz1 = total * silu_grad(z1[...])
    out[:, :features] = dot(dz1.T.astype(BF16), snapshot[...])
    quarter = channels // groups
    place = lax.axis_index("grp")
    for k in range(groups):
        piece = sent if k % 2 else kept
        at = pl.multiple_of(jnp.bitwise_xor(place, k) * quarter, quarter)
        piece[k // 2] = out[pl.ds(at, quarter)].astype(piece.dtype)


def core_kernel(kept, got, out_kept, out_sent):
    out_kept[...] = kept[0] + got[0].astype(F32)
    out_sent[...] = (kept[1] + got[1].astype(F32)).astype(BF16)


def taps_kernel(
    groups, sims, h_own, h_one, h_two, h_three, d_own, d_one, d_two, d_three, after_this, *refs
):
    out, h_all, r_all = refs[-3:]
    rows, channels = h_own.shape
    ez = rows // (EX * EY)
    quarter = channels // groups
    crop = ez // groups
    place = lax.axis_index("grp")
    layer = EY * ez
    taken = 3 * quarter
    slot = lax.broadcasted_iota(jnp.int32, (taken, channels), 0)
    channel = lax.broadcasted_iota(jnp.int32, (taken, channels), 1)
    chosen = jnp.where(channel == place * quarter + lax.rem(slot, quarter), 1.0, 0.0).astype(BF16)
    pairs = ((h_own, d_own), (h_one, d_one), (h_two, d_two), (h_three, d_three))
    for k, (h, d) in enumerate(pairs):
        at = jnp.bitwise_xor(place, k)
        mine = dot_nt(chosen, d[...])
        for x in range(EX):
            h_all[x, at] = h[x * layer : (x + 1) * layer]
            r_all[x, at] = mine[:, x * layer : (x + 1) * layer]
    deep = groups * layer
    turned = jnp.concatenate([r_all[x, g] for x in range(EX) for g in range(groups)], axis=1)
    spot = lax.broadcasted_iota(jnp.int32, (1, EX * deep), 1)
    after = pltpu.roll(turned[:quarter], EX * deep - 1, 1)
    after = jnp.where(lax.rem(spot, crop) == crop - 1, 0.0, after)
    before = pltpu.roll(turned[2 * quarter :], 1, 1)
    before = jnp.where(lax.rem(spot, crop) == 0, 0.0, before)
    turned = jnp.concatenate([after, turned[quarter : 2 * quarter], before], axis=0)
    spot = lax.rem(spot, deep)
    up = jnp.where(spot >= deep - ez, 0.0, pltpu.roll(turned, EX * deep - ez, 1))
    down = jnp.where(spot < ez, 0.0, pltpu.roll(turned, ez, 1))
    whole = h_all[...].reshape(EX * deep, channels)
    for dy, side in enumerate((up, turned, down)):
        side = side.astype(BF16)
        for dx in range(3):
            if dx == 0:
                got = dot(side[:, deep:], whole[:deep])
            elif dx == 1:
                got = dot(side, whole)
            else:
                got = dot(side[:, :deep], whole[deep:])
            start = (9 * dx + 3 * dy) * quarter
            out[start : start + taken] = got
    me = lax.rem(lax.axis_index("sim"), sims)
    piece_rows = 27 * quarter // sims
    for k, piece in enumerate(refs[:-3]):
        at = pl.multiple_of(jnp.bitwise_xor(me, k) * piece_rows, 8)
        piece[...] = out[pl.ds(at, piece_rows)].astype(piece.dtype)


def dense_kernel(kept, got, *refs):
    out_kept, out_sent = refs[-3:-1]
    for source, target in zip(refs[:1], refs[-1:]):
        target[...] = source[...]
    total = kept[...] + got[...].astype(F32)
    grid = total.reshape(2, 2, kept.shape[0] // 4, kept.shape[1])
    odd = lax.rem(lax.div(lax.axis_index("sim"), 2), 2) == 1
    out_kept[...] = jnp.where(odd, grid[:, 1], grid[:, 0])
    out_sent[...] = jnp.where(odd, grid[:, 0], grid[:, 1]).astype(BF16)


def half_kernel(scale, kept, got, out_kept, out_sent):
    total = kept[...] + got[...].astype(F32)
    upper = lax.rem(lax.div(lax.axis_index("sim"), scale), 2) == 1
    out_kept[...] = jnp.where(upper, total[1], total[0])
    out_sent[...] = jnp.where(upper, total[0], total[1]).astype(BF16)


def packed(taps, dense):
    channels = taps.shape[1]
    parts = [taps]
    for start in range(0, dense.shape[1], channels):
        piece = dense[:, start : start + channels]
        short_by = channels - piece.shape[1]
        if short_by:
            piece = jnp.concatenate([piece, jnp.zeros((piece.shape[0], short_by), F32)], axis=1)
        parts.append(piece)
    return jnp.concatenate(parts, axis=0)


def sum_kernel(parts, kept, *refs):
    total = kept[...]
    for other in refs[: parts - 1]:
        total = total + other[...].astype(F32)
    refs[-1][...] = total.astype(BF16)


def share_kernel(taps, one, two, three, dense, dense_in, after_this, out):
    total = taps[...]
    for other in (one, two, three):
        total = total + other[...].astype(F32)
    out[...] = packed(total, dense[...] + dense_in[...].astype(F32)).astype(BF16)


def place_kernel(masks, count, *refs):
    shares = refs[: len(masks)]
    outs = refs[-7:-4]
    held = refs[-4:-1]
    sems = refs[-1]
    channels = shares[0].shape[1]
    tap_rows, own_rows = [out.shape[0] // count for out in outs[:2]]
    features = outs[1].shape[1]
    me = lax.axis_index("sim")
    copies = []
    for i, (mask, share) in enumerate(zip(masks, shares)):
        source = jnp.bitwise_xor(me, mask)
        value = share[...].astype(F32)
        held[0][i] = value[:tap_rows]
        start = tap_rows
        for first in range(0, features, channels):
            held[1][i, :, first : first + channels] = value[start : start + own_rows]
            start += own_rows
        held[2][i] = value[start : start + own_rows, : outs[2].shape[1]]
        for j, out in enumerate(outs):
            size = tap_rows if j == 0 else own_rows
            rows = pl.ds(pl.multiple_of(source * size, 8), size)
            copy = pltpu.make_async_copy(held[j].at[i], out.at[rows], sems.at[i, j])
            copy.start()
            copies.append(copy)
    for copy in copies:
        copy.wait()


def placed_shares(shares, shapes, count):
    outs = ()
    groups = [(first, first + 1) for first in range(0, count - 4, 2)]
    for masks in groups + [(count - 4, count - 3, count - 2), (count - 1,)]:
        tap_rows, own_rows = [shape.shape[0] // count for shape in shapes[:2]]
        sizes = (tap_rows, own_rows, own_rows)
        held = [
            pltpu.VMEM((len(masks), size, shape.shape[1]), F32)
            for size, shape in zip(sizes, shapes)
        ]
        anywhere = pl.BlockSpec(memory_space=pl.ANY)
        outs = pl.pallas_call(
            functools.partial(place_kernel, masks, count),
            out_shape=shapes,
            in_specs=[pl.BlockSpec(memory_space=pltpu.VMEM)] * len(masks) + [anywhere] * len(outs),
            out_specs=(anywhere,) * 3,
            scratch_shapes=held + [pltpu.SemaphoreType.DMA((len(masks), 3))],
            input_output_aliases={len(masks) + i: i for i in range(len(outs))},
            compiler_params=pltpu.CompilerParams(vmem_limit_bytes=VMEM_LIMIT),
            cost_estimate=pl.CostEstimate(flops=1000, bytes_accessed=1000, transcendentals=0),
        )(*[shares[mask] for mask in masks], *outs)
    return outs


def call(kernel, outs, scratch=(), in_hbm=(), inputs=0, flops=1000):
    specs = {}
    if in_hbm:
        specs["in_specs"] = [
            pl.BlockSpec(memory_space=pl.ANY if i in in_hbm else pltpu.VMEM) for i in range(inputs)
        ]
    return pl.pallas_call(
        kernel,
        out_shape=outs,
        scratch_shapes=list(scratch),
        compiler_params=pltpu.CompilerParams(vmem_limit_bytes=VMEM_LIMIT),
        cost_estimate=pl.CostEstimate(flops=flops, bytes_accessed=1000, transcendentals=0),
        **specs,
    )


def shaped(shape, kind):
    return jax.ShapeDtypeStruct(shape, kind)


def swapped(value, axis, mask):
    count = lax.axis_size(axis)
    return lax.ppermute(value, axis, [(i, i ^ mask) for i in range(count)])


def crossed(value, axis, periodic):
    count = lax.axis_size(axis)
    route = [(i, i + 1 if i % 2 else i - 1) for i in range(count)]
    if periodic:
        route = [(i, j % count) for i, j in route]
    return lax.ppermute(value, axis, [(i, j) for i, j in route if 0 <= j < count])


def exchanged(edges):
    pair_x, cross_x, pair_y, cross_y = edges
    cross_x = crossed(cross_x, "sim", True)
    pair_x = swapped(pair_x, "sim", 1)
    cross_y = crossed(cross_y, "grp", False)
    pair_y = swapped(pair_y, "grp", 1)
    return pair_x, cross_x, pair_y, cross_y


def gathered(share, sims):
    got = {0: share}
    for k in range(2, sims, 2):
        got[k] = swapped(share, "sim", k)
    for k in range(0, sims, 2):
        got[k + 1] = swapped(got[k], "sim", 1)
    return [got[k] for k in range(sims)]


def body(velocity, slot_of, w_encode, w_conv, w_head):
    stencil, wall = (jnp.asarray(table) for table in element_tables())
    block = velocity[0, 0]
    slots = slot_of[0]
    rows, width = block.shape[1:]
    ez = rows // (EX * EY)
    channels = w_encode.shape[1]
    features = w_encode.shape[0]
    outputs = w_head.shape[1]
    sims = lax.axis_size("sim")
    groups = lax.axis_size("grp")
    total = rows * sims * groups
    quarter = channels // groups

    whole = shaped((3, rows, width), F32)
    x_edge = shaped((3, EY * ez // 2, 2 * NP * NP), BF16)
    y_edge = shaped((3, ez, 2 * NP * NP), BF16)
    edge_shapes = (x_edge, x_edge, y_edge, y_edge)

    order, back, tabs = call(
        order_kernel,
        (
            shaped((rows, rows), BF16),
            shaped((rows, rows), BF16),
            shaped((4, width, 2 * NP * NP), BF16),
        ),
        flops=4 * 10**9,
    )(slots)
    field, *edges = call(prepare_kernel, (whole,) + edge_shapes, flops=4 * 10**9)(block, order, tabs)
    halos = exchanged(edges)
    part = call(inside_kernel, whole)(field, stencil)
    field, *edges = call(join_kernel, (whole,) + edge_shapes)(part, *halos, tabs)
    halos = exchanged(edges)
    part = call(inside_kernel, whole)(field, stencil)
    field, snapshot, z1, h1 = call(
        encode_kernel,
        (
            whole,
            shaped((rows, features), BF16),
            shaped((rows, channels), F32),
            shaped((rows, channels), BF16),
        ),
    )(part, *halos, tabs, w_encode)

    h_three = swapped(h1, "grp", 3)
    h_one = swapped(h1, "grp", 1)
    h_two = swapped(h_three, "grp", 1)
    rows_bf = shaped((rows, channels), BF16)
    square = shaped((rows, channels), F32)
    z2, target = call(
        functools.partial(centre_kernel, groups),
        (square, shaped((rows, outputs), BF16)),
        flops=2 * 10**9,
    )(h1, w_conv, field, wall)
    dz2, h2, resid = call(
        functools.partial(forward_kernel, groups, total),
        (rows_bf, rows_bf, shaped((rows, outputs), BF16)),
        (pltpu.VMEM((EX, EY + 2, ez, 3 * channels), BF16),),
    )(z2, h1, h_one, call(same_kernel, rows_bf, flops=2 * 10**9)(h_three), w_conv, w_head, target)

    d_three = swapped(dz2, "grp", 3)
    d_one = swapped(dz2, "grp", 1)
    d_two = swapped(d_three, "grp", 1)
    wide = features + outputs
    pair = (groups // 2, quarter, wide)
    dh1, head = call(
        functools.partial(centre_back_kernel, groups),
        (square, shaped((channels, outputs), F32)),
        flops=2 * 10**9,
    )(dz2, w_conv, h2, resid)
    e_kept, e_sent = call(
        functools.partial(back_kernel, groups),
        (shaped(pair, F32), shaped(pair, BF16)),
        (pltpu.VMEM((channels, wide), F32),),
    )(dh1, head, dz2, d_one, call(same_kernel, rows_bf, flops=2 * 10**9)(d_three), w_conv, z1, snapshot)
    e_got = swapped(e_sent, "grp", 1)
    e_kept, e_sent = call(core_kernel, (shaped(pair[1:], F32), shaped(pair[1:], BF16)))(e_kept, e_got)
    e_got = swapped(e_sent, "grp", 2)
    tap_rows = 27 * quarter // sims
    own_rows = quarter // sims
    direct = sims == 8
    if direct:
        pieces = [shaped((tap_rows, channels), BF16 if k % 2 else F32) for k in range(sims)]
    else:
        pieces = [shaped((27 * quarter, channels), BF16)]
    taps = call(
        functools.partial(taps_kernel, groups, sims if direct else 1),
        tuple(pieces),
        (
            pltpu.VMEM((27 * quarter, channels), F32),
            pltpu.VMEM((EX, groups, EY * ez, channels), BF16),
            pltpu.VMEM((EX, groups, 3 * quarter, EY * ez), F32),
        ),
        in_hbm=(8,),
        inputs=9,
    )(h1, h_one, h_two, h_three, dz2, d_one, d_two, d_three, e_kept)
    restore = call(restore_kernel, (whole, shaped((8, 128), F32)), in_hbm=(2,), inputs=3)
    if direct:
        tap_piece = shaped((tap_rows, channels), BF16)
        part = (2, 2 * own_rows, wide)
        e_kept, e_sent, *later = call(
            dense_kernel, (shaped(part, F32), shaped(part, BF16)) + (tap_piece,)
        )(e_kept, e_got, taps[1])
        e_got = swapped(e_sent, "sim", 2)
        taps_in = {k: swapped(taps[k + 1], "sim", 1) for k in (6, 4, 2)}
        taps_in.update((k, swapped(piece, "sim", 1)) for k, piece in zip((0,), later))
        add_two = call(functools.partial(sum_kernel, 2), tap_piece)
        add_three = call(functools.partial(sum_kernel, 3), tap_piece)
        six = swapped(add_two(taps[6], taps_in[6], e_sent), "sim", 2)
        part = shaped((2 * own_rows, wide), F32), shaped((2 * own_rows, wide), BF16)
        e_kept, e_sent = call(functools.partial(half_kernel, 4), part)(e_kept, e_got)
        e_got = swapped(e_sent, "sim", 4)
        two = add_two(taps[2], taps_in[2], e_sent)
        four = swapped(add_three(taps[4], taps_in[4], six, two), "sim", 4)
        two = swapped(two, "sim", 2)
        part = shaped((own_rows, wide), F32), shaped((own_rows, wide), BF16)
        e_kept, e_sent = call(functools.partial(half_kernel, 1), part, flops=4 * 10**9)(
            e_kept.reshape(2, own_rows, wide), e_got.reshape(2, own_rows, wide)
        )
        velocity_next, done = restore(field, back, e_sent)
        e_got = swapped(e_sent, "sim", 1)
        blocks = -(-wide // channels)
        share = call(share_kernel, shaped((tap_rows + blocks * own_rows, channels), BF16))(
            taps[0], taps_in[0], two, four, e_kept, e_got, done
        )
        shares = gathered(share, sims)
        shapes = (
            shaped((27 * quarter, channels), F32),
            shaped((quarter, features), F32),
            shaped((quarter, outputs), F32),
        )
        taps, encode, head = placed_shares(shares, shapes, sims)
    else:
        taps = taps[0].reshape(sims, tap_rows, channels)
        taps = lax.all_to_all(taps, "sim", 0, 0, tiled=True)
        taps = jnp.sum(taps.astype(F32), axis=0).astype(BF16)
        taps = lax.all_gather(taps, "sim").astype(F32)
        velocity_next, done = restore(field, back, e_kept)
        dense = e_kept + e_got.astype(F32)
        dense = dense.astype(BF16).reshape(sims, own_rows, wide)
        dense = lax.all_to_all(dense, "sim", 0, 0, tiled=True)
        dense = jnp.sum(dense.astype(F32), axis=0).astype(BF16)
        dense = lax.all_gather(dense, "sim").reshape(quarter, wide).astype(F32)
        encode = dense[:, :features]
        head = dense[:, features:]
    taps = taps.reshape(27, quarter, channels)
    return velocity_next[None, None], encode.T, taps.transpose(0, 2, 1), head


def solution(mesh):
    placed = (P("sim", "grp", None, None, None), P("sim", "grp", None), P(), P(), P())
    return jax.shard_map(
        body,
        mesh=mesh,
        in_specs=placed,
        out_specs=(
            P("sim", "grp", None, None, None),
            P(None, "grp"),
            P(None, None, "grp"),
            P("grp", None),
        ),
        check_vma=False,
    )
```

```python
import functools

import jax
import jax.numpy as jnp
import ml_dtypes
import numpy as np
from jax import lax
from jax.experimental import pallas as pl
from jax.experimental.pallas import tpu as pltpu
from jax.sharding import PartitionSpec as P

NP = 8
EX = 2
EY = 4
STEPS = 2

VISCOSITY = 0.2
TIME_STEP = 0.005
PENALTY = 100.0
LOSS_WEIGHT = 64.0
FACE_RATE = TIME_STEP * VISCOSITY * PENALTY

F32 = jnp.float32
BF16 = jnp.bfloat16
VMEM_LIMIT = 16 * 1024 * 1024


def derivative_matrix(count):
    places = np.arange(count)
    points = -np.cos(np.pi * places / (count - 1))
    weights = np.where(places % 2 == 0, 1.0, -1.0)
    weights[0] = weights[0] * 0.5
    weights[count - 1] = weights[count - 1] * 0.5
    identity = np.eye(count)
    spread = points[:, None] - points[None, :] + identity
    deriv = weights[None, :] / weights[:, None] / spread
    deriv = deriv * (1.0 - identity)
    return deriv - identity * deriv.sum(axis=1)[:, None]


def short(table):
    return np.asarray(table, np.float32).astype(ml_dtypes.bfloat16)


def in_three(table):
    table = np.asarray(table, np.float32)
    high = table.astype(ml_dtypes.bfloat16)
    low = (table - high.astype(np.float32)).astype(ml_dtypes.bfloat16)
    return np.concatenate([high, high, low], axis=0)


@functools.lru_cache(maxsize=None)
def element_tables():
    count = NP
    deriv = derivative_matrix(count)
    single = np.eye(count)
    square = np.eye(count * count)
    grid = np.arange(count**3).reshape(count, count, count)
    final = count - 1
    faces = [
        grid[0].ravel(),
        grid[final].ravel(),
        grid[:, 0].ravel(),
        grid[:, final].ravel(),
        grid[:, :, 0].ravel(),
        grid[:, :, final].ravel(),
    ]

    def pick(which):
        table = np.zeros((count**3, count * count))
        table[which, np.arange(count * count)] = 1.0
        return table

    picks = [pick(which) for which in faces]
    none = np.zeros_like(picks[0])
    taken = np.concatenate([picks[i] for i in (3, 2, 5, 4)], axis=1)
    placed = np.concatenate(picks[2:], axis=1).T
    bottom = np.zeros((count**3, count * count))
    for first in range(count):
        for middle in range(count):
            for inner in range(count):
                bottom[grid[first, middle, inner], first * count + inner] = (
                    VISCOSITY * deriv[0, middle]
                )
    mirrored = np.concatenate([deriv, deriv @ deriv], axis=0)[:, ::-1].reshape(2, count, count)
    straight = np.stack([deriv, deriv @ deriv])
    half = count // 2
    scale = np.array([-TIME_STEP, TIME_STEP * VISCOSITY])[:, None, None]

    def along_first(sign):
        mixed = (0.5 * scale * (straight + sign * mirrored))[:, :half, :half]
        return in_three(np.concatenate([np.kron(part.T, square) for part in mixed], axis=1))

    small_y = np.kron(deriv, single)
    small_z = np.kron(single, deriv)
    curved = TIME_STEP * VISCOSITY * (small_y @ small_y + small_z @ small_z).T
    small_y = -TIME_STEP * small_y.T
    small_z = -TIME_STEP * small_z.T
    blank = np.zeros_like(curved)

    def across(blocks):
        table = in_three(np.concatenate(blocks, axis=1))
        return np.concatenate([table, np.zeros((count * count, table.shape[1]), table.dtype)], axis=0)

    both = np.concatenate(
        [
            across([small_y, curved, small_z, blank]),
            across([curved, small_y, blank, small_z]),
        ],
        axis=1,
    )
    filled = np.zeros((count**3, count**3 - taken.shape[1]))
    stencil = np.concatenate(
        [
            along_first(1.0),
            along_first(-1.0),
            both,
            short(placed),
            short(np.concatenate([taken, filled], axis=1)),
        ],
        axis=0,
    )
    wall = in_three(np.concatenate([bottom, none, none, bottom], axis=1))
    return stencil, wall


def dot(left, right):
    return jnp.dot(left, right, preferred_element_type=F32)


def dot_nt(left, right):
    return lax.dot_general(left, right, (((1,), (1,)), ((), ())), preferred_element_type=F32)


def split_two(value):
    high = value.astype(BF16)
    return high, (value - high.astype(F32)).astype(BF16)


def moved(order, value):
    high = value.astype(BF16)
    rest = value - high.astype(F32)
    middle, low = split_two(rest)
    return dot(order, high) + dot(order, middle) + dot(order, low)


def slot_matrix(slots):
    count = slots.shape[1]
    rows = lax.broadcasted_iota(jnp.int32, (count, count), 0)
    return jnp.where(rows == slots, 1.0, 0.0).astype(F32)


def layer_rows(field, x, layer, ez):
    start = (x * EY + layer) * ez
    return field[:, start : start + ez].reshape(3 * ez, field.shape[2])


def edge_tables():
    side = NP * NP
    point = lax.broadcasted_iota(jnp.int32, (NP * side, 2 * side), 0)
    lane = lax.broadcasted_iota(jnp.int32, (NP * side, 2 * side), 1)
    middle = lax.rem(lax.div(point, NP), NP)
    place = lax.div(point, side) * NP + lax.rem(point, NP)

    def table(level, shift):
        return jnp.where((middle == level) & (lane == place + shift), 1.0, 0.0).astype(BF16)

    return table(0, 0), table(0, side), table(NP - 1, 0), table(NP - 1, side)


def order_kernel(slots, order, back, tabs):
    matrix = slot_matrix(slots[...])
    back[...] = matrix.astype(BF16)
    order[...] = matrix.T.astype(BF16)
    for i, table in enumerate(edge_tables()):
        tabs[i] = table


def is_even(axis):
    return lax.rem(lax.axis_index(axis), 2) == 0


def write_edges(field, tabs, outs, ez):
    pair_x, cross_x, pair_y, cross_y = outs
    side = NP * NP
    half = EY * ez // 2
    last = NP * side - side
    even_x = is_even("sim")
    even_y = is_even("grp")
    near = field[:, 0 : 2 * half, 0 : 2 * side][:, :, :side]
    far = field[:, 2 * half : 4 * half, last - side :][:, :, side:]
    to_left = jnp.concatenate([near[:, :half], near[:, half:]], axis=2)
    to_right = jnp.concatenate([far[:, :half], far[:, half:]], axis=2)
    pair_x[...] = jnp.where(even_x, to_right, to_left).astype(BF16)
    cross_x[...] = jnp.where(even_x, to_left, to_right).astype(BF16)
    to_below, to_above = [
        dot(layer_rows(field, 0, layer, ez).astype(BF16), tabs[at])
        + dot(layer_rows(field, 1, layer, ez).astype(BF16), tabs[at + 1])
        for layer, at in ((0, 0), (EY - 1, 2))
    ]
    pair_y[...] = jnp.where(even_y, to_above, to_below).astype(BF16).reshape(pair_y.shape)
    cross_y[...] = jnp.where(even_y, to_below, to_above).astype(BF16).reshape(cross_y.shape)


def add_edges(part, pair_x, cross_x, pair_y, cross_y, tabs, field, ez):
    side = NP * NP
    half = EY * ez // 2
    width = NP * side
    even_x = is_even("sim")
    even_y = is_even("grp")
    pair = FACE_RATE * pair_x[...].astype(F32)
    cross = FACE_RATE * cross_x[...].astype(F32)
    left = jnp.where(even_x, cross, pair)
    right = jnp.where(even_x, pair, cross)
    pair = pair_y[...].astype(F32)
    cross = cross_y[...].astype(F32)
    below = jnp.where(even_y, cross, pair).astype(BF16).reshape(3 * ez, 2 * side)
    above = jnp.where(even_y, pair, cross).astype(BF16).reshape(3 * ez, 2 * side)
    first = lax.broadcasted_iota(jnp.int32, (1, 1, 2 * side), 2) < side

    field[...] = part[...]
    turned = pltpu.roll(left, side, 2)
    field[:, 0:half, : 2 * side] += jnp.where(first, left, 0.0)
    field[:, half : 2 * half, : 2 * side] += jnp.where(first, turned, 0.0)
    turned = pltpu.roll(right, side, 2)
    field[:, 2 * half : 3 * half, width - 2 * side :] += jnp.where(first, 0.0, turned)
    field[:, 3 * half : 4 * half, width - 2 * side :] += jnp.where(first, 0.0, right)
    for x in range(EX):
        for layer, value, at in ((0, below, 0), (EY - 1, above, 2)):
            start = (x * EY + layer) * ez
            more = FACE_RATE * dot_nt(value, tabs[at + x])
            field[:, start : start + ez] += more.reshape(3, ez, width)


def prepare_kernel(vel, order, tabs, field, *edges):
    ez = vel.shape[1] // (EX * EY)
    for c in range(3):
        high, low = split_two(vel[c])
        field[c] = dot(order[...], high) + dot(order[...], low)
    write_edges(field, tabs, edges, ez)


def face_count(width):
    point = lax.broadcasted_iota(jnp.int32, (1, width), 1)
    count = jnp.zeros((1, width), F32)
    for stride in (NP * NP, NP, 1):
        index = lax.rem(lax.div(point, stride), NP)
        count = count + jnp.where((index == 0) | (index == NP - 1), 1.0, 0.0)
    return count


def inside_kernel(field, stencil, part):
    rows = field.shape[1]
    width = field.shape[2]
    ez = rows // (EX * EY)
    half = width // 2
    side = NP * NP
    pair = 2 * side
    tiles = width // pair
    even = stencil.at[0 : 3 * half]
    odd = stencil.at[3 * half : 6 * half]
    start = 6 * half
    across = stencil.at[start : start + 4 * side]
    placed = stencil.at[start + 4 * side : start + 8 * side]
    taken = stencil.at[start + 8 * side : start + 8 * side + width]
    keep = 1.0 - FACE_RATE * face_count(width)
    lanes = lax.broadcasted_iota(jnp.int32, (1, pair), 1)
    first = lanes < side
    tile = [field[:, :, j * pair : (j + 1) * pair].reshape(3 * rows, pair) for j in range(tiles)]
    swap = [pltpu.roll(value, side, 1) for value in tile]

    high = [value.astype(BF16).astype(F32) for value in tile]
    high_swap = [value.astype(BF16).astype(F32) for value in swap]

    faces = dot(jnp.concatenate(high, axis=1).astype(BF16), taken[:, : 4 * side])
    in_y = faces[:, :pair].reshape(3 * EX, EY, ez, pair)
    wall = jnp.zeros((3 * EX, 1, ez, pair), F32)
    beside_y = jnp.where(
        first,
        jnp.concatenate([wall, in_y[:, :-1]], axis=1),
        jnp.concatenate([in_y[:, 1:], wall], axis=1),
    ).reshape(3 * rows, pair)
    in_z = faces[:, pair:].reshape(3 * EX * EY, ez, pair)
    beside_z = jnp.where(
        first, pltpu.roll(in_z, 1, 1), pltpu.roll(in_z, ez - 1, 1)
    ).reshape(3 * rows, pair)
    beside = jnp.concatenate([beside_y, beside_z], axis=1).astype(BF16)

    def three(value):
        top, rest = split_two(value)
        return jnp.concatenate([top, rest, top], axis=1)

    mirror = jnp.concatenate([swap[tiles - 1 - j] for j in range(tiles // 2)], axis=1)
    near = jnp.concatenate(tile[: tiles // 2], axis=1)
    from_even = dot(three(near + mirror), even[...])
    from_odd = dot(three(near - mirror), odd[...])

    for j in range(tiles):
        cols = slice(j * pair, (j + 1) * pair)
        low = tile[j] - high[j]
        low_swap = swap[j] - high_swap[j]
        one = jnp.concatenate([jnp.where(first, high[j], low_swap), high[j]], axis=1).astype(BF16)
        two = jnp.concatenate([jnp.where(first, high_swap[j], low), high_swap[j]], axis=1).astype(BF16)
        got_one = dot(one, across[:, : 4 * side])
        got_two = dot(two, across[:, 4 * side :])
        slope_y = jnp.where(first, got_one[:, :pair], got_two[:, :pair])
        slope_z = got_one[:, pair:] + got_two[:, pair:]
        curve = jnp.where(first, got_two[:, :pair], got_one[:, :pair])
        if j < tiles // 2:
            at = slice(j * pair, (j + 1) * pair)
            up = slice(half + j * pair, half + (j + 1) * pair)
            slope_x = from_odd[:, at] + from_even[:, at]
            curve = pltpu.roll(curve, side, 1) + (from_even[:, up] + from_odd[:, up])
        else:
            k = tiles - 1 - j
            at = slice(k * pair, (k + 1) * pair)
            up = slice(half + k * pair, half + (k + 1) * pair)
            slope_x = pltpu.roll(from_odd[:, at] - from_even[:, at], side, 1)
            curve = pltpu.roll(curve + (from_even[:, up] - from_odd[:, up]), side, 1)
        value = tile[j] * keep[:, cols] + curve
        if j % 2 == 0:
            outer = dot(beside, placed[:, j * pair : (j + 2) * pair])
        value = value + FACE_RATE * outer[:, j % 2 * pair : (j % 2 + 1) * pair]
        value = value.reshape(3, rows, pair)
        for d, slope in enumerate((slope_x, slope_y, slope_z)):
            value = value + slope.reshape(3, rows, pair) * tile[j].reshape(3, rows, pair)[d][None]
        layer = EY * ez
        if j == 0:
            beyond = swap[tiles - 1].reshape(3, rows, pair)[:, :layer]
            beyond = jnp.where(first, FACE_RATE * beyond, 0.0)
            value = jnp.concatenate([value[:, :layer], value[:, layer:] + beyond], axis=1)
        if j == tiles - 1:
            beyond = swap[0].reshape(3, rows, pair)[:, layer:]
            beyond = jnp.where(first, 0.0, FACE_RATE * beyond)
            value = jnp.concatenate([value[:, :layer] + beyond, value[:, layer:]], axis=1)
        part[:, :, cols] = value


def join_kernel(part, pair_x, cross_x, pair_y, cross_y, tabs, field, *edges):
    ez = part.shape[1] // (EX * EY)
    add_edges(part, pair_x, cross_x, pair_y, cross_y, tabs, field, ez)
    write_edges(field, tabs, edges, ez)


def encode_kernel(
    part, pair_x, cross_x, pair_y, cross_y, tabs, w_encode,
    field, snapshot, z1, h1,
):
    ez = part.shape[1] // (EX * EY)
    add_edges(part, pair_x, cross_x, pair_y, cross_y, tabs, field, ez)
    snap = jnp.concatenate([field[0].astype(BF16), field[2].astype(BF16)], axis=1)
    snapshot[...] = snap
    hidden = dot(snap, w_encode[...])
    z1[...] = hidden
    h1[...] = (hidden * jax.nn.sigmoid(hidden)).astype(BF16)


def same_kernel(value, out):
    out[...] = value[...]


def restore_kernel(field, back, after_this, out, done):
    for c in range(3):
        out[c] = moved(back[...], field[c])
    done[...] = jnp.zeros_like(done)


def silu_grad(value):
    sigma = jax.nn.sigmoid(value)
    return sigma * (1.0 + value * (1.0 - sigma))


def with_layers(own, pair, cross, ez, groups):
    channels = own.shape[-1]
    place = lax.axis_index("grp")
    grid = own[...].astype(F32).reshape(EX, EY, ez, channels)
    even = is_even("grp")
    pair = pair[...].reshape(EX, EY, ez, channels).astype(F32)
    cross = cross[...].reshape(EX, EY, ez, channels).astype(F32)
    before = jnp.where(even, cross[:, EY - 1 :], pair[:, EY - 1 :])
    after = jnp.where(even, pair[:, :1], cross[:, :1])
    before = jnp.where(place > 0, before, 0.0)
    after = jnp.where(place < groups - 1, after, 0.0)
    return jnp.concatenate([before, grid, after], axis=1)


def along_span(grid, ez, groups):
    shape = grid.shape
    rows = int(np.prod(shape[:-1]))
    crop = ez // groups
    flat = grid.reshape(rows, shape[-1])
    place = lax.rem(lax.broadcasted_iota(jnp.int32, (rows, 1), 0), crop)
    before = jnp.where(place == 0, 0.0, pltpu.roll(flat, 1, 0))
    after = jnp.where(place == crop - 1, 0.0, pltpu.roll(flat, rows - 1, 0))
    return before.reshape(shape), after.reshape(shape)


def tap_sum(taken, w_conv, dy):
    channels = w_conv.shape[1]
    first = 3 * dy
    rows = taken.shape[1]

    def times(value, start):
        return dot(value, w_conv[start + first : start + first + 3].reshape(-1, channels))

    both = times(taken.reshape(EX * rows, taken.shape[2]), 9)
    return both + jnp.concatenate([times(taken[1], 18), times(taken[0], 0)], axis=0)


def centre_kernel(groups, h1, w_conv, field, wall, z2, target):
    found = 0.0
    for c, start in ((0, 0), (2, 2 * NP * NP)):
        high, low = split_two(field[c])
        three = jnp.concatenate([high, low, high], axis=1)
        found = found + dot(three, wall[:, start : start + 2 * NP * NP])
    target[...] = found.astype(BF16)
    rows, channels = h1.shape
    ez = rows // (EX * EY)
    grid = h1[...].astype(F32).reshape(EX, EY, ez, channels)
    before, after = along_span(grid, ez, groups)
    taken = jnp.concatenate([before, grid, after], axis=-1).astype(BF16)
    z2[...] = tap_sum(taken.reshape(EX, rows // EX, 3 * channels), w_conv, 1)


def forward_kernel(groups, total, z2, h1, pair, cross, w_conv, w_head, target, dz2, h2, resid, padded):
    rows, channels = h1.shape
    ez = rows // (EX * EY)
    grid = with_layers(h1, pair, cross, ez, groups)
    before, after = along_span(grid, ez, groups)
    padded[...] = jnp.concatenate([before, grid, after], axis=-1).astype(BF16)
    hidden = z2[...]
    for dy in (0, 2):
        taken = padded[:, dy : dy + EY].reshape(EX, rows // EX, 3 * channels)
        hidden = hidden + tap_sum(taken, w_conv, dy)
    act = (hidden * jax.nn.sigmoid(hidden)).astype(BF16)
    output = dot(act, w_head[...])
    miss = (LOSS_WEIGHT * (output - target[...].astype(F32)) / total).astype(BF16)
    h2[...] = act
    resid[...] = miss
    dz2[...] = (dot_nt(miss, w_head[...]) * silu_grad(hidden)).astype(BF16)


def tap_sum_back(shifted, w_conv, dy):
    total = 0.0
    for dz, taken in enumerate(shifted):
        tap = 3 * dy + dz
        both = dot_nt(taken.reshape(-1, taken.shape[2]), w_conv[9 + tap])
        ahead_x = dot_nt(taken[0], w_conv[18 + tap])
        behind_x = dot_nt(taken[1], w_conv[tap])
        total = total + both + jnp.concatenate([behind_x, ahead_x], axis=0)
    return total


def centre_back_kernel(groups, dz2, w_conv, h2, resid, dh1, head):
    rows, channels = dz2.shape
    ez = rows // (EX * EY)
    grid = dz2[...].astype(F32).reshape(EX, EY, ez, channels)
    before, after = along_span(grid, ez, groups)
    shifted = [
        part.astype(BF16).reshape(EX, rows // EX, channels) for part in (after, grid, before)
    ]
    dh1[...] = tap_sum_back(shifted, w_conv, 1)
    head[...] = dot(h2[...].astype(F32).T.astype(BF16), resid[...])


def back_kernel(groups, dh1, head, dz2, pair, cross, w_conv, z1, snapshot, kept, sent, out):
    rows, channels = dz2.shape
    ez = rows // (EX * EY)
    grid = with_layers(dz2, pair, cross, ez, groups)
    before, after = along_span(grid, ez, groups)
    shifted = [part.astype(BF16) for part in (after, grid, before)]
    features = snapshot.shape[1]
    out[:, features:] = head[...]
    total = dh1[...]
    for dy in (0, 2):
        taken = [
            part[:, 2 - dy : 2 - dy + EY].reshape(EX, rows // EX, channels) for part in shifted
        ]
        total = total + tap_sum_back(taken, w_conv, dy)
    dz1 = total * silu_grad(z1[...])
    out[:, :features] = dot(dz1.T.astype(BF16), snapshot[...])
    quarter = channels // groups
    place = lax.axis_index("grp")
    for k in range(groups):
        piece = sent if k % 2 else kept
        at = pl.multiple_of(jnp.bitwise_xor(place, k) * quarter, quarter)
        piece[k // 2] = out[pl.ds(at, quarter)].astype(piece.dtype)


def core_kernel(kept, got, out_kept, out_sent):
    out_kept[...] = kept[0] + got[0].astype(F32)
    out_sent[...] = (kept[1] + got[1].astype(F32)).astype(BF16)


def taps_kernel(
    groups, sims, h_own, h_one, h_two, h_three, d_own, d_one, d_two, d_three, after_this, *refs
):
    out, h_all, r_all = refs[-3:]
    rows, channels = h_own.shape
    ez = rows // (EX * EY)
    quarter = channels // groups
    crop = ez // groups
    place = lax.axis_index("grp")
    layer = EY * ez
    taken = 3 * quarter
    slot = lax.broadcasted_iota(jnp.int32, (taken, channels), 0)
    channel = lax.broadcasted_iota(jnp.int32, (taken, channels), 1)
    chosen = jnp.where(channel == place * quarter + lax.rem(slot, quarter), 1.0, 0.0).astype(BF16)
    pairs = ((h_own, d_own), (h_one, d_one), (h_two, d_two), (h_three, d_three))
    for k, (h, d) in enumerate(pairs):
        at = jnp.bitwise_xor(place, k)
        mine = dot_nt(chosen, d[...])
        for x in range(EX):
            h_all[x, at] = h[x * layer : (x + 1) * layer]
            r_all[x, at] = mine[:, x * layer : (x + 1) * layer]
    deep = groups * layer
    turned = jnp.concatenate([r_all[x, g] for x in range(EX) for g in range(groups)], axis=1)
    spot = lax.broadcasted_iota(jnp.int32, (1, EX * deep), 1)
    after = pltpu.roll(turned[:quarter], EX * deep - 1, 1)
    after = jnp.where(lax.rem(spot, crop) == crop - 1, 0.0, after)
    before = pltpu.roll(turned[2 * quarter :], 1, 1)
    before = jnp.where(lax.rem(spot, crop) == 0, 0.0, before)
    turned = jnp.concatenate([after, turned[quarter : 2 * quarter], before], axis=0)
    spot = lax.rem(spot, deep)
    up = jnp.where(spot >= deep - ez, 0.0, pltpu.roll(turned, EX * deep - ez, 1))
    down = jnp.where(spot < ez, 0.0, pltpu.roll(turned, ez, 1))
    whole = h_all[...].reshape(EX * deep, channels)
    for dy, side in enumerate((up, turned, down)):
        side = side.astype(BF16)
        for dx in range(3):
            if dx == 0:
                got = dot(side[:, deep:], whole[:deep])
            elif dx == 1:
                got = dot(side, whole)
            else:
                got = dot(side[:, :deep], whole[deep:])
            start = (9 * dx + 3 * dy) * quarter
            out[start : start + taken] = got
    me = lax.rem(lax.axis_index("sim"), sims)
    piece_rows = 27 * quarter // sims
    for k, piece in enumerate(refs[:-3]):
        at = pl.multiple_of(jnp.bitwise_xor(me, k) * piece_rows, 8)
        piece[...] = out[pl.ds(at, piece_rows)].astype(piece.dtype)


def dense_kernel(kept, got, *refs):
    out_kept, out_sent = refs[-3:-1]
    for source, target in zip(refs[:1], refs[-1:]):
        target[...] = source[...]
    total = kept[...] + got[...].astype(F32)
    grid = total.reshape(2, 2, kept.shape[0] // 4, kept.shape[1])
    odd = lax.rem(lax.div(lax.axis_index("sim"), 2), 2) == 1
    out_kept[...] = jnp.where(odd, grid[:, 1], grid[:, 0])
    out_sent[...] = jnp.where(odd, grid[:, 0], grid[:, 1]).astype(BF16)


def half_kernel(scale, kept, got, out_kept, out_sent):
    total = kept[...] + got[...].astype(F32)
    upper = lax.rem(lax.div(lax.axis_index("sim"), scale), 2) == 1
    out_kept[...] = jnp.where(upper, total[1], total[0])
    out_sent[...] = jnp.where(upper, total[0], total[1]).astype(BF16)


def packed(taps, dense):
    channels = taps.shape[1]
    parts = [taps]
    for start in range(0, dense.shape[1], channels):
        piece = dense[:, start : start + channels]
        short_by = channels - piece.shape[1]
        if short_by:
            piece = jnp.concatenate([piece, jnp.zeros((piece.shape[0], short_by), F32)], axis=1)
        parts.append(piece)
    return jnp.concatenate(parts, axis=0)


def sum_kernel(parts, kept, *refs):
    total = kept[...]
    for other in refs[: parts - 1]:
        total = total + other[...].astype(F32)
    refs[-1][...] = total.astype(BF16)


def share_kernel(taps, one, two, three, dense, dense_in, after_this, out):
    total = taps[...]
    for other in (one, two, three):
        total = total + other[...].astype(F32)
    out[...] = packed(total, dense[...] + dense_in[...].astype(F32)).astype(BF16)


def place_kernel(masks, count, *refs):
    shares = refs[: len(masks)]
    outs = refs[-7:-4]
    held = refs[-4:-1]
    sems = refs[-1]
    channels = shares[0].shape[1]
    tap_rows, own_rows = [out.shape[0] // count for out in outs[:2]]
    features = outs[1].shape[1]
    me = lax.axis_index("sim")
    copies = []
    for i, (mask, share) in enumerate(zip(masks, shares)):
        source = jnp.bitwise_xor(me, mask)
        value = share[...].astype(F32)
        held[0][i] = value[:tap_rows]
        start = tap_rows
        for first in range(0, features, channels):
            held[1][i, :, first : first + channels] = value[start : start + own_rows]
            start += own_rows
        held[2][i] = value[start : start + own_rows, : outs[2].shape[1]]
        for j, out in enumerate(outs):
            size = tap_rows if j == 0 else own_rows
            rows = pl.ds(pl.multiple_of(source * size, 8), size)
            copy = pltpu.make_async_copy(held[j].at[i], out.at[rows], sems.at[i, j])
            copy.start()
            copies.append(copy)
    for copy in copies:
        copy.wait()


def placed_shares(shares, shapes, count):
    outs = ()
    groups = [(first, first + 1) for first in range(0, count - 4, 2)]
    for masks in groups + [(count - 4, count - 3, count - 2), (count - 1,)]:
        tap_rows, own_rows = [shape.shape[0] // count for shape in shapes[:2]]
        sizes = (tap_rows, own_rows, own_rows)
        held = [
            pltpu.VMEM((len(masks), size, shape.shape[1]), F32)
            for size, shape in zip(sizes, shapes)
        ]
        anywhere = pl.BlockSpec(memory_space=pl.ANY)
        outs = pl.pallas_call(
            functools.partial(place_kernel, masks, count),
            out_shape=shapes,
            in_specs=[pl.BlockSpec(memory_space=pltpu.VMEM)] * len(masks) + [anywhere] * len(outs),
            out_specs=(anywhere,) * 3,
            scratch_shapes=held + [pltpu.SemaphoreType.DMA((len(masks), 3))],
            input_output_aliases={len(masks) + i: i for i in range(len(outs))},
            compiler_params=pltpu.CompilerParams(vmem_limit_bytes=VMEM_LIMIT),
            cost_estimate=pl.CostEstimate(flops=1000, bytes_accessed=1000, transcendentals=0),
        )(*[shares[mask] for mask in masks], *outs)
    return outs


def call(kernel, outs, scratch=(), in_hbm=(), inputs=0, flops=1000):
    specs = {}
    if in_hbm:
        specs["in_specs"] = [
            pl.BlockSpec(memory_space=pl.ANY if i in in_hbm else pltpu.VMEM) for i in range(inputs)
        ]
    return pl.pallas_call(
        kernel,
        out_shape=outs,
        scratch_shapes=list(scratch),
        compiler_params=pltpu.CompilerParams(vmem_limit_bytes=VMEM_LIMIT),
        cost_estimate=pl.CostEstimate(flops=flops, bytes_accessed=1000, transcendentals=0),
        **specs,
    )


def shaped(shape, kind):
    return jax.ShapeDtypeStruct(shape, kind)


def swapped(value, axis, mask):
    count = lax.axis_size(axis)
    return lax.ppermute(value, axis, [(i, i ^ mask) for i in range(count)])


def crossed(value, axis, periodic):
    count = lax.axis_size(axis)
    route = [(i, i + 1 if i % 2 else i - 1) for i in range(count)]
    if periodic:
        route = [(i, j % count) for i, j in route]
    return lax.ppermute(value, axis, [(i, j) for i, j in route if 0 <= j < count])


def exchanged(edges):
    pair_x, cross_x, pair_y, cross_y = edges
    cross_x = crossed(cross_x, "sim", True)
    pair_x = swapped(pair_x, "sim", 1)
    cross_y = crossed(cross_y, "grp", False)
    pair_y = swapped(pair_y, "grp", 1)
    return pair_x, cross_x, pair_y, cross_y


def gathered(share, sims):
    got = {0: share}
    for k in range(2, sims, 2):
        got[k] = swapped(share, "sim", k)
    for k in range(0, sims, 2):
        got[k + 1] = swapped(got[k], "sim", 1)
    return [got[k] for k in range(sims)]


def body(velocity, slot_of, w_encode, w_conv, w_head):
    stencil, wall = (jnp.asarray(table) for table in element_tables())
    block = velocity[0, 0]
    slots = slot_of[0]
    rows, width = block.shape[1:]
    ez = rows // (EX * EY)
    channels = w_encode.shape[1]
    features = w_encode.shape[0]
    outputs = w_head.shape[1]
    sims = lax.axis_size("sim")
    groups = lax.axis_size("grp")
    total = rows * sims * groups
    quarter = channels // groups

    whole = shaped((3, rows, width), F32)
    x_edge = shaped((3, EY * ez // 2, 2 * NP * NP), BF16)
    y_edge = shaped((3, ez, 2 * NP * NP), BF16)
    edge_shapes = (x_edge, x_edge, y_edge, y_edge)

    order, back, tabs = call(
        order_kernel,
        (
            shaped((rows, rows), BF16),
            shaped((rows, rows), BF16),
            shaped((4, width, 2 * NP * NP), BF16),
        ),
        flops=4 * 10**9,
    )(slots)
    field, *edges = call(prepare_kernel, (whole,) + edge_shapes, flops=4 * 10**9)(block, order, tabs)
    halos = exchanged(edges)
    part = call(inside_kernel, whole)(field, stencil)
    field, *edges = call(join_kernel, (whole,) + edge_shapes)(part, *halos, tabs)
    halos = exchanged(edges)
    part = call(inside_kernel, whole)(field, stencil)
    field, snapshot, z1, h1 = call(
        encode_kernel,
        (
            whole,
            shaped((rows, features), BF16),
            shaped((rows, channels), F32),
            shaped((rows, channels), BF16),
        ),
    )(part, *halos, tabs, w_encode)

    h_three = swapped(h1, "grp", 3)
    h_one = swapped(h1, "grp", 1)
    h_two = swapped(h_three, "grp", 1)
    rows_bf = shaped((rows, channels), BF16)
    square = shaped((rows, channels), F32)
    z2, target = call(
        functools.partial(centre_kernel, groups),
        (square, shaped((rows, outputs), BF16)),
        flops=2 * 10**9,
    )(h1, w_conv, field, wall)
    dz2, h2, resid = call(
        functools.partial(forward_kernel, groups, total),
        (rows_bf, rows_bf, shaped((rows, outputs), BF16)),
        (pltpu.VMEM((EX, EY + 2, ez, 3 * channels), BF16),),
    )(z2, h1, h_one, call(same_kernel, rows_bf, flops=2 * 10**9)(h_three), w_conv, w_head, target)

    d_three = swapped(dz2, "grp", 3)
    d_one = swapped(dz2, "grp", 1)
    d_two = swapped(d_three, "grp", 1)
    wide = features + outputs
    pair = (groups // 2, quarter, wide)
    dh1, head = call(
        functools.partial(centre_back_kernel, groups),
        (square, shaped((channels, outputs), F32)),
        flops=2 * 10**9,
    )(dz2, w_conv, h2, resid)
    e_kept, e_sent = call(
        functools.partial(back_kernel, groups),
        (shaped(pair, F32), shaped(pair, BF16)),
        (pltpu.VMEM((channels, wide), F32),),
    )(dh1, head, dz2, d_one, call(same_kernel, rows_bf, flops=2 * 10**9)(d_three), w_conv, z1, snapshot)
    e_got = swapped(e_sent, "grp", 1)
    e_kept, e_sent = call(core_kernel, (shaped(pair[1:], F32), shaped(pair[1:], BF16)))(e_kept, e_got)
    e_got = swapped(e_sent, "grp", 2)
    tap_rows = 27 * quarter // sims
    own_rows = quarter // sims
    direct = sims == 8
    if direct:
        pieces = [shaped((tap_rows, channels), BF16 if k % 2 else F32) for k in range(sims)]
    else:
        pieces = [shaped((27 * quarter, channels), BF16)]
    taps = call(
        functools.partial(taps_kernel, groups, sims if direct else 1),
        tuple(pieces),
        (
            pltpu.VMEM((27 * quarter, channels), F32),
            pltpu.VMEM((EX, groups, EY * ez, channels), BF16),
            pltpu.VMEM((EX, groups, 3 * quarter, EY * ez), F32),
        ),
        in_hbm=(8,),
        inputs=9,
    )(h1, h_one, h_two, h_three, dz2, d_one, d_two, d_three, e_kept)
    restore = call(restore_kernel, (whole, shaped((8, 128), F32)), in_hbm=(2,), inputs=3)
    if direct:
        tap_piece = shaped((tap_rows, channels), BF16)
        part = (2, 2 * own_rows, wide)
        e_kept, e_sent, *later = call(
            dense_kernel, (shaped(part, F32), shaped(part, BF16)) + (tap_piece,)
        )(e_kept, e_got, taps[1])
        e_got = swapped(e_sent, "sim", 2)
        taps_in = {k: swapped(taps[k + 1], "sim", 1) for k in (6, 4, 2)}
        taps_in.update((k, swapped(piece, "sim", 1)) for k, piece in zip((0,), later))
        add_two = call(functools.partial(sum_kernel, 2), tap_piece)
        add_three = call(functools.partial(sum_kernel, 3), tap_piece)
        six = swapped(add_two(taps[6], taps_in[6], e_sent), "sim", 2)
        part = shaped((2 * own_rows, wide), F32), shaped((2 * own_rows, wide), BF16)
        e_kept, e_sent = call(functools.partial(half_kernel, 4), part)(e_kept, e_got)
        e_got = swapped(e_sent, "sim", 4)
        two = add_two(taps[2], taps_in[2], e_sent)
        four = swapped(add_three(taps[4], taps_in[4], six, two), "sim", 4)
        two = swapped(two, "sim", 2)
        part = shaped((own_rows, wide), F32), shaped((own_rows, wide), BF16)
        e_kept, e_sent = call(functools.partial(half_kernel, 1), part, flops=4 * 10**9)(
            e_kept.reshape(2, own_rows, wide), e_got.reshape(2, own_rows, wide)
        )
        velocity_next, done = restore(field, back, e_sent)
        e_got = swapped(e_sent, "sim", 1)
        blocks = -(-wide // channels)
        share = call(share_kernel, shaped((tap_rows + blocks * own_rows, channels), BF16))(
            taps[0], taps_in[0], two, four, e_kept, e_got, done
        )
        shares = gathered(share, sims)
        shapes = (
            shaped((27 * quarter, channels), F32),
            shaped((quarter, features), F32),
            shaped((quarter, outputs), F32),
        )
        taps, encode, head = placed_shares(shares, shapes, sims)
    else:
        taps = taps[0].reshape(sims, tap_rows, channels)
        taps = lax.all_to_all(taps, "sim", 0, 0, tiled=True)
        taps = jnp.sum(taps.astype(F32), axis=0).astype(BF16)
        taps = lax.all_gather(taps, "sim").astype(F32)
        velocity_next, done = restore(field, back, e_kept)
        dense = e_kept + e_got.astype(F32)
        dense = dense.astype(BF16).reshape(sims, own_rows, wide)
        dense = lax.all_to_all(dense, "sim", 0, 0, tiled=True)
        dense = jnp.sum(dense.astype(F32), axis=0).astype(BF16)
        dense = lax.all_gather(dense, "sim").reshape(quarter, wide).astype(F32)
        encode = dense[:, :features]
        head = dense[:, features:]
    taps = taps.reshape(27, quarter, channels)
    return velocity_next[None, None], encode.T, taps.transpose(0, 2, 1), head


def solution(mesh):
    placed = (P("sim", "grp", None, None, None), P("sim", "grp", None), P(), P(), P())
    return jax.shard_map(
        body,
        mesh=mesh,
        in_specs=placed,
        out_specs=(
            P("sim", "grp", None, None, None),
            P(None, "grp"),
            P(None, None, "grp"),
            P("grp", None),
        ),
        check_vma=False,
    )
```
